32 devices in a mesh: seq: 16 (over z, x, core), fsdp: 2 (over y).
Axes of the slice: x: 2, y: 2, z: 4, core: 2. Of those that a mesh axis runs over, the one named last changes fastest.
Arguments:
- tokens: bfloat16 [112, 56, 384], P('seq', 'fsdp'), may hold values from -6 to 6
- norm_gains: bfloat16 [2, 2, 384], P(None, None, 'fsdp'), may hold values from 0.25 to 1.75
- w_qkv: bfloat16 [2, 384, 1152], P(None, 'fsdp'), may hold values from -0.3125 to 0.3125
- w_proj: bfloat16 [2, 384, 384], P(None, 'fsdp'), may hold values from -0.875 to 0.875
- w_up: bfloat16 [2, 384, 1536], P(None, 'fsdp'), may hold values from -0.3125 to 0.3125
- w_down: bfloat16 [2, 1536, 384], P(None, 'fsdp'), may hold values from -0.15625 to 0.15625
- tables: bfloat16 [2, 12, 169], P(None, 'fsdp'), may hold values from -4 to 4
- region_ids: int32 [112, 56], P('seq', 'fsdp'), may hold values from 0 to 3, as said below
- rel_index: int32 [49, 49], replicated, may hold values from 0 to 168, as said below
- cotangent: bfloat16 [112, 56, 384], P('seq', 'fsdp'), may hold values from -6 to 6
Outputs:
- mixed: bfloat16 [112, 56, 384], P('seq', 'fsdp')
- tokens_grad: bfloat16 [112, 56, 384], P('seq', 'fsdp')
- gains_grad: float32 [2, 2, 384], P(None, None, 'fsdp')
- qkv_grad: float32 [2, 384, 1152], P(None, 'fsdp')
- proj_grad: float32 [2, 384, 384], P(None, 'fsdp')
- up_grad: float32 [2, 384, 1536], P(None, 'fsdp')
- down_grad: float32 [2, 1536, 384], P(None, 'fsdp')
- tables_grad: float32 [2, 12, 169], P(None, 'fsdp')
The draws below stay inside these ranges and needn't reach their ends.
Inputs may be any that keep to these rules, and one draw needn't show every extreme that they name: `region_ids`: labels of the tokens of the grid rolled by -3; inside a window, tokens attend only to tokens of the same label. `rel_index`: entry (i, j) depends only on the offset between positions i and j of a window (row-major) and differs for different offsets.
All inputs are finite; a program needn't handle non-finite values.
Results may differ from the reference program's by a relative error of at most 0.02.
Values may be sent and summed in bfloat16 or wider, within the bound.
No kernel may reach another device: no remote copies, remote signals or barrier semaphores. Data moves between devices by JAX's collectives and lax.ppermute only.
A program may use at most 128 MiB of HBM per device.

```python
import jax
import jax.numpy as jnp
from jax import lax

C = 384
HEADS = 12
HD = 32
FF = 1536
WIN = 7
SHIFT = 3
TABLE = 169
WCOLS = 8
HEIGHT = 112
WIDTH = 56
N_SEQ = 16


def draw_region_ids(key, part):
    key = jax.random.fold_in(key, 11)
    key_rows, key_cols = jax.random.split(key)
    row_split = jax.random.randint(key_rows, (HEIGHT // WIN, WIDTH // WIN), 1, WIN)
    col_split = jax.random.randint(key_cols, (HEIGHT // WIN, WIDTH // WIN), 1, WIN)
    row_split = jnp.repeat(jnp.repeat(row_split, WIN, axis=0), WIN, axis=1)
    col_split = jnp.repeat(jnp.repeat(col_split, WIN, axis=0), WIN, axis=1)
    inner_row = (jnp.arange(HEIGHT, dtype=jnp.int32) % WIN)[:, None]
    inner_col = (jnp.arange(WIDTH, dtype=jnp.int32) % WIN)[None, :]
    below = (inner_row >= row_split).astype(jnp.int32)
    right = (inner_col >= col_split).astype(jnp.int32)
    return (below + 2 * right).astype(jnp.int32)


def draw_rel_index(key, part):
    key = jax.random.fold_in(key, 23)
    order = jax.random.permutation(key, TABLE).astype(jnp.int32)
    places = jnp.arange(WIN * WIN, dtype=jnp.int32)
    row_pos = places // WIN
    col_pos = places % WIN
    offset = (row_pos[:, None] - row_pos[None, :] + WIN - 1) * (2 * WIN - 1) + (col_pos[:, None] - col_pos[None, :] + WIN - 1)
    return order[offset].astype(jnp.int32)


def levels(key, dims, cuts, smallest, high):
    factor_of, own = 1.0, jax.random.fold_in(key, 6)
    for dim, shards_of in cuts:
        steps = jnp.exp(jax.random.uniform(jax.random.fold_in(own, dim), (shards_of,), jnp.float32, smallest / len(cuts), high / len(cuts)))
        factor_of = factor_of * jnp.repeat(steps, dims[dim] // shards_of).reshape([-1 if axis == dim else 1 for axis in range(len(dims))])
    return factor_of


def bell_draw(own_key, dims, scale, most, cuts=(), kind=jnp.bfloat16):
    drawn = scale * jax.random.normal(own_key, dims, jnp.float32)
    if cuts:
        drawn = drawn * levels(own_key, dims, cuts, -0.22, 0.18)
    return jnp.clip(drawn, -most, most).astype(kind)


def setup_inputs(seed: int = 0) -> dict:
    seeds = jax.random.split(jax.random.key(seed), 11)
    return {
        "tokens": bell_draw(seeds[0], (HEIGHT, WIDTH, C), 1.0, 6.0, ((0, 16), (1, 2))),
        "norm_gains": jnp.clip(1.0 + 0.15 * jax.random.normal(seeds[1], (2, 2, C), jnp.float32), 0.25, 1.75).astype(jnp.bfloat16),
        "w_qkv": bell_draw(seeds[2], (2, C, 3 * C), C ** -0.5, 0.3125, ((1, 2),)),
        "w_proj": bell_draw(seeds[3], (2, C, C), (C // 8) ** -0.5, 0.875, ((1, 2),)),
        "w_up": bell_draw(seeds[4], (2, C, FF), C ** -0.5, 0.3125, ((1, 2),)),
        "w_down": bell_draw(seeds[5], (2, FF, C), FF ** -0.5, 0.15625, ((1, 2),)),
        "tables": bell_draw(seeds[6], (2, HEADS, TABLE), 1.0, 4.0, ((1, 2),)),
        "region_ids": draw_region_ids(jax.random.fold_in(seeds[10], 71), 0),
        "rel_index": draw_rel_index(jax.random.fold_in(seeds[10], 71), 0),
        "cotangent": bell_draw(seeds[9], (HEIGHT, WIDTH, C), 1.0, 6.0, ((0, 16), (1, 2))),
    }


EPSILON = 1e-05
MASKED_SCORE = -1000000000.0

@jax.custom_vjp
def low(v):
    return lax.optimization_barrier(v.astype(jnp.bfloat16)).astype(jnp.float32)

@jax.custom_vjp
def low_back(v):
    return v

def low_keep(v):
    return (low(v), None)

def low_pass(kept, grad):
    return (grad,)

def back_keep(v):
    return (v, None)

def back_low(kept, grad):
    return (low(grad),)
low.defvjp(low_keep, low_pass)
low_back.defvjp(back_keep, back_low)

def layer_norm(values, gain):
    centred = values - lax.optimization_barrier(jnp.mean(values, -1, keepdims=True))
    return centred * lax.rsqrt(lax.optimization_barrier(jnp.mean(centred * centred, -1, keepdims=True)) + EPSILON) * gain

def product(left, right):
    return jnp.dot(left, right, precision=lax.Precision.HIGHEST)

def windows(grid):
    feat = grid.shape[-1]
    split = grid.reshape(N_SEQ, WIN, WCOLS, WIN, feat)
    return split.transpose(0, 2, 1, 3, 4).reshape(N_SEQ, WCOLS, WIN * WIN, feat)

def unwindow(blocks):
    feat = blocks.shape[-1]
    split = blocks.reshape(N_SEQ, WCOLS, WIN, WIN, feat)
    return split.transpose(0, 2, 1, 3, 4).reshape(N_SEQ * WIN, WCOLS * WIN, feat)

def attend(query, keys, values, labels, bias, masked):
    raw = low_back(jnp.einsum('wihd,wjhd->whij', query, keys, precision=lax.Precision.HIGHEST))
    scores = raw + bias[None]
    if masked:
        same = labels[:, :, None] == labels[:, None, :]
        scores = jnp.where(same[:, None], scores, MASKED_SCORE)
    peak = lax.optimization_barrier(jnp.max(scores, -1, keepdims=True))
    weighted = jnp.exp(scores - peak)
    probs = low(weighted / lax.optimization_barrier(jnp.sum(weighted, -1, keepdims=True)))
    return jnp.einsum('whij,wjhd->wihd', probs, values, precision=lax.Precision.HIGHEST)

def block(grid, gains, qkv_w, proj_w, up_w, down_w, table, rel_index, region_ids, masked):
    hidden_q = low(layer_norm(grid, gains[0]))
    qkv = low_back(product(hidden_q, qkv_w))
    query = low(qkv[..., :C] * HD ** (-0.5))
    keys = low(qkv[..., C:2 * C])
    values = low(qkv[..., 2 * C:])
    heads_shape = (N_SEQ, WCOLS, WIN * WIN, HEADS, HD)
    query_w = windows(query).reshape(heads_shape)
    keys_w = windows(keys).reshape(heads_shape)
    values_w = windows(values).reshape(heads_shape)
    labels_w = windows(region_ids[:, :, None])[..., 0]
    bias = table[:, rel_index]

    def one_row(items):
        return attend(items[0], items[1], items[2], items[3], bias, masked)
    attended = lax.map(jax.checkpoint(one_row), (query_w, keys_w, values_w, labels_w))
    mixed = unwindow(attended.reshape(N_SEQ, WCOLS, WIN * WIN, C))
    mixed = low(low_back(mixed))
    middle = grid + low_back(product(mixed, proj_w))
    hidden_b = low(layer_norm(middle, gains[1]))
    inner = low_back(product(hidden_b, up_w))
    activated = low(jax.nn.gelu(inner))
    return middle + low_back(product(activated, down_w))

def forward(grid, gains, qkv_w, proj_w, up_w, down_w, table_w, rel_index, region_ids):
    output_one = block(grid, gains[0], qkv_w[0], proj_w[0], up_w[0], down_w[0], table_w[0], rel_index, region_ids, False)
    output_one = low_back(low(output_one))
    rolled = jnp.roll(output_one, (-SHIFT, -SHIFT), (0, 1))
    output_two = block(rolled, gains[1], qkv_w[1], proj_w[1], up_w[1], down_w[1], table_w[1], rel_index, region_ids, True)
    return jnp.roll(output_two, (SHIFT, SHIFT), (0, 1))

def reference(tokens, norm_gains, w_qkv, w_proj, w_up, w_down, tables, region_ids, rel_index, cotangent):

    def wrapped(grid, gains, qkv_w, proj_w, up_w, down_w, table_w):
        return forward(grid, gains, qkv_w, proj_w, up_w, down_w, table_w, rel_index, region_ids)
    floats = tuple((item.astype(jnp.float32) for item in (tokens, norm_gains, w_qkv, w_proj, w_up, w_down, tables)))
    output, pull = jax.vjp(wrapped, *floats)
    grads = pull(cotangent.astype(jnp.float32))
    return (output.astype(jnp.bfloat16), grads[0].astype(jnp.bfloat16), grads[1], grads[2], grads[3], grads[4], grads[5], grads[6])
```

```python
import functools

import jax
import jax.numpy as jnp
from jax import lax
from jax.experimental import pallas as pl
from jax.experimental.pallas import tpu as pltpu
from jax.sharding import PartitionSpec as P

WIN = 7
SHIFT = 3
TABLE = 169
SIDE = 8
SLOT = SIDE * SIDE
HEAD = 32
PAIR = 2 * SLOT
EPSILON = 1e-05
MASKED_SCORE = -1000000000.0
F32 = jnp.float32
BF16 = jnp.bfloat16
VMEM_LIMIT = 40 * 1024 * 1024


def exchange(array, ds, dy):
    n, m = lax.axis_size("seq"), lax.axis_size("fsdp")
    pairs = [(s * m + y, (s ^ ds) * m + (y ^ dy)) for s in range(n) for y in range(m)]
    return lax.ppermute(array, ("seq", "fsdp"), pairs)


def take_from(array, ds, dy):
    n, m = lax.axis_size("seq"), lax.axis_size("fsdp")
    pairs = [((s + ds) % n * m + (y + dy) % m, s * m + y) for s in range(n) for y in range(m)]
    return lax.ppermute(array, ("seq", "fsdp"), pairs)


def halo(near_rows, near_cols, corner, step):
    return (
        take_from(near_rows, step, 0),
        take_from(near_cols, 0, step),
        take_from(corner, step, step),
    )


def other_half(weight, layer, place):
    rows = weight.shape[1] // 4
    start = (2 * place[0] + place[1]) * rows
    mine = lax.dynamic_slice(weight, (layer, start, 0), (1, rows, weight.shape[2]))[0]
    first = exchange(mine, 0, 1)
    second = exchange(first, 2, 0)
    third = exchange(first, 1, 0)
    fourth = exchange(second, 1, 0)
    return (first, second, third, fourth)


def add(*terms):
    total = terms[0].astype(F32)
    for term in terms[1:]:
        total = total + term.astype(F32)
    return total


def sum_higher(value):
    step = 16
    while step < lax.axis_size("seq"):
        value = add(value, exchange(value, step, 0)).astype(value.dtype)
        step *= 2
    return value


def reduce_pieces(keep, send):
    got = exchange(send, 1, 0)
    part = [[add(keep[dy, dx], got[dy, dx]).astype(BF16) for dx in range(2)] for dy in range(2)]
    mine = add(
        part[0][0],
        exchange(part[0][1], 2, 0),
        exchange(part[1][0], 0, 1),
        exchange(part[1][1], 2, 1),
    ).astype(BF16)
    total = add(mine[:, 0], *[exchange(mine[:, dz], 4 * dz, 0) for dz in range(1, 4)]).astype(BF16)
    total = sum_higher(total)
    column = jnp.stack([total] + [exchange(total, 4 * dz, 0) for dz in range(1, 4)])
    plane = jnp.stack([column, exchange(column, 2, 0)])
    return jnp.stack([plane, exchange(plane, 1, 0)])


def sum_small(value):
    value = add(value, exchange(value, 1, 0))
    value = add(value, exchange(value, 2, 0), exchange(value, 0, 1), exchange(value, 2, 1))
    value = add(value, *[exchange(value, 4 * dz, 0) for dz in range(1, 4)])
    return sum_higher(value)


def flip(index, bits):
    return jnp.bitwise_xor(index, bits)


def fetch(place, layer, own, parts, full, sems):
    half = full.shape[0] // 2
    rows = half // 4
    core, x, y = place[0], place[1], place[3]
    copies = [
        pltpu.make_async_copy(
            own.at[layer], full.at[pl.ds(pl.multiple_of(y * half, 16), half)], sems.at[0]
        )
    ]
    for index, part in enumerate(parts):
        spot = 2 * flip(core, index // 2) + flip(x, index % 2)
        start = pl.multiple_of((1 - y) * half + spot * rows, 16)
        copies.append(
            pltpu.make_async_copy(part, full.at[pl.ds(start, rows)], sems.at[1 + index])
        )
    for copy in copies:
        copy.start()
    return copies


def wait_all(copies):
    for copy in copies:
        copy.wait()


def row_segments(mode, refs, row, width):
    if mode == "plain":
        return [(0, refs[0][row], 0, width)]
    own, rows, cols, corner = refs
    rest = width - SHIFT
    if mode == "in":
        if row < WIN - SHIFT:
            return [
                (0, own[row + SHIFT], SHIFT, rest),
                (rest, cols[row + SHIFT], 0, SHIFT),
            ]
        at = row - (WIN - SHIFT)
        return [(0, rows[at], SHIFT, rest), (rest, corner[at], 0, SHIFT)]
    if row >= SHIFT:
        return [(0, cols[row - SHIFT], 0, SHIFT), (SHIFT, own[row - SHIFT], 0, rest)]
    return [(0, corner[row], 0, SHIFT), (SHIFT, rows[row], 0, rest)]


def fill_windows(mode, refs, out):
    width = refs[0].shape[1]
    out[...] = jnp.zeros_like(out)
    for row in range(WIN):
        for first, source, start, count in row_segments(mode, refs, row, width):
            source = source.astype(F32)
            for window in range(width // WIN):
                low = max(first, window * WIN)
                high = min(first + count, window * WIN + WIN)
                if low < high:
                    spot = window * SLOT + row * SIDE + low - window * WIN
                    begin = start + low - first
                    out[spot : spot + high - low, :] = source[begin : begin + high - low, :]


def fill_grid(source, buffer, width):
    for row in range(WIN):
        for window in range(width // WIN):
            spot = window * SLOT + row * SIDE
            buffer[row, window * WIN : window * WIN + WIN, :] = source[spot : spot + WIN, :]


def normalize(values):
    centred = values - jnp.mean(values, -1, keepdims=True)
    factor = lax.rsqrt(jnp.mean(centred * centred, -1, keepdims=True) + EPSILON)
    return centred * factor, factor


def normalize_back(grad_norm, normed, factor):
    spread = jnp.mean(grad_norm * normed, -1, keepdims=True)
    return factor * (grad_norm - jnp.mean(grad_norm, -1, keepdims=True) - normed * spread)


def mm(left, right):
    return lax.dot_general(left, right, (((1,), (0,)), ((), ())), preferred_element_type=F32)


def mm_nt(left, right):
    return lax.dot_general(left, right, (((1,), (1,)), ((), ())), preferred_element_type=F32)


def only_head(group, which):
    rows = lax.broadcasted_iota(jnp.int32, group.shape, 0)
    inside = (rows >= which * HEAD) & (rows < (which + 1) * HEAD)
    return jnp.where(inside, group, jnp.zeros_like(group))


def diagonal(block):
    lanes = lax.broadcasted_iota(jnp.int32, (SLOT, PAIR), 1)
    return jnp.where(lanes < SLOT, block[:SLOT], block[SLOT:])


def spread_diagonal(packed):
    lanes = lax.broadcasted_iota(jnp.int32, (SLOT, PAIR), 1)
    low = jnp.where(lanes < SLOT, packed, 0.0)
    high = jnp.where(lanes < SLOT, 0.0, packed)
    return jnp.concatenate([low, high], axis=0).astype(BF16)


def store_piece(place, keep, send, core, y, x, kind, z, value):
    at = (flip(place[3], y), flip(place[1], x), kind, flip(place[2], z))
    value = value.astype(BF16)

    @pl.when(place[0] == core)
    def _():
        keep[at] = value

    @pl.when(place[0] != core)
    def _():
        send[at] = value


def store_columns(place, keep, send, chunk, kind, value):
    rows = value.shape[0] // 8
    for y in range(2):
        for z in range(4):
            at = (y * 4 + z) * rows
            store_piece(
                place, keep, send, chunk // 2, y, chunk % 2, kind, z, value[at : at + rows]
            )


def store_rows(place, keep, send, chunk, kind, value):
    rows = value.shape[0] // 8
    for x in range(2):
        for z in range(4):
            at = (x * 4 + z) * rows
            store_piece(
                place, keep, send, chunk % 2, chunk // 2, x, kind, z, value[at : at + rows]
            )


def attend_forward_kernel(layer, mode, n_grid, *refs):
    place, refs = refs[0], refs[1:]
    grid, refs = refs[:n_grid], refs[n_grid:]
    gains, bias, same, qkv_own, *refs = refs
    qkv_parts, refs = refs[:4], refs[4:]
    proj_own, *refs = refs
    proj_parts, refs = refs[:4], refs[4:]
    x_out, m_out, query_t, keys_t, keys, values, mixed_t, probs = refs[:8]
    qkv_w, proj_w, sems, flat, values_t = refs[8:]
    width_c = flat.shape[1]
    heads = width_c // HEAD
    qkv_copies = fetch(place, layer, qkv_own, qkv_parts, qkv_w, sems.at[0])
    proj_copies = fetch(place, layer, proj_own, proj_parts, proj_w, sems.at[1])
    fill_windows(mode, grid, flat)
    x_out[...] = flat[...].astype(BF16)
    normed, _ = normalize(flat[...])
    hidden = (normed * gains[layer, 0:1, :]).astype(BF16)
    wait_all(qkv_copies)
    query = (mm(hidden, qkv_w[:, :width_c]) * HEAD ** (-0.5)).astype(BF16)
    query_t[...] = query.T
    keys[...] = mm(hidden, qkv_w[:, width_c : 2 * width_c]).astype(BF16)
    keys_t[...] = keys[...].T
    values[...] = mm(hidden, qkv_w[:, 2 * width_c :]).astype(BF16)
    values_t[...] = values[...].T
    for head in range(heads):
        group = slice(head // 4 * 128, head // 4 * 128 + 128)
        rows = slice(head * HEAD, head * HEAD + HEAD)
        for pair in range(flat.shape[0] // PAIR):
            span = slice(pair * PAIR, pair * PAIR + PAIR)
            raw = mm(keys[span, group], only_head(query_t[group, span], head % 4))
            scores = jnp.where(
                same[:, span] > 0.5, diagonal(raw) + bias[head], MASKED_SCORE
            )
            weighted = jnp.exp(scores - jnp.max(scores, 0, keepdims=True))
            attention = weighted / jnp.sum(weighted, 0, keepdims=True)
            probs[head, :, span] = attention
            mixed_t[rows, span] = mm(values_t[rows, span], spread_diagonal(attention)).astype(BF16)
    wait_all(proj_copies)
    m_out[...] = flat[...] + mm(mixed_t[...].T, proj_w[...])


def attend_backward_kernel(layer, shifted, *refs):
    place, grad_m, x_in, gains, query_t, keys_t, keys, values, mixed_t, probs, qkv_own, *refs = refs
    qkv_parts, refs = refs[:4], refs[4:]
    proj_own, *refs = refs
    proj_parts, refs = refs[:4], refs[4:]
    n_out = 8 if shifted else 5
    keep, send, gain_grad, bias_grad, grid_out, *edges = refs[:n_out]
    qkv_w, proj_w, sems, grad_t, out_t, flat, buffer = refs[n_out:]
    width_c = flat.shape[1]
    heads = width_c // HEAD
    proj_copies = fetch(place, layer, proj_own, proj_parts, proj_w, sems.at[1])
    qkv_copies = fetch(place, layer, qkv_own, qkv_parts, qkv_w, sems.at[0])
    normed, factor = normalize(x_in[...].astype(F32))
    gain = gains[layer, 0:1, :]
    hidden_t = (normed * gain).astype(BF16).T
    attended = grad_m[...].astype(BF16)
    store_columns(place, keep, send, 3, 0, mm(mixed_t[...], attended))
    wait_all(proj_copies)
    out_t[...] = mm_nt(proj_w[...], attended).astype(BF16)
    for head in range(heads):
        group = slice(head // 4 * 128, head // 4 * 128 + 128)
        rows = slice(head * HEAD, head * HEAD + HEAD)
        total = jnp.zeros((SLOT, PAIR), F32)
        for pair in range(flat.shape[0] // PAIR):
            span = slice(pair * PAIR, pair * PAIR + PAIR)
            attention = probs[head, :, span]
            grad_p = diagonal(mm(values[span, group], only_head(out_t[group, span], head % 4)))
            grad_s = attention * (grad_p - jnp.sum(grad_p * attention, 0, keepdims=True))
            total = total + grad_s
            spread_p = spread_diagonal(attention)
            spread_s = spread_diagonal(grad_s)
            grad_t[rows, span] = (
                mm(keys_t[rows, span], spread_s) * HEAD ** (-0.5)
            ).astype(BF16)
            grad_t[width_c + head * HEAD : width_c + head * HEAD + HEAD, span] = mm_nt(
                query_t[rows, span], spread_s
            ).astype(BF16)
            grad_t[2 * width_c + head * HEAD : 2 * width_c + head * HEAD + HEAD, span] = mm_nt(
                out_t[rows, span], spread_p
            ).astype(BF16)
        bias_grad[head] = total
    for chunk in range(3):
        part = grad_t[chunk * width_c : (chunk + 1) * width_c, :]
        store_columns(place, keep, send, chunk, 0, mm_nt(hidden_t, part))
    wait_all(qkv_copies)
    grad_hidden = mm(qkv_w[...], grad_t[...]).T
    gain_grad[...] = jnp.sum(grad_hidden * normed, 0, keepdims=True)
    flat[...] = grad_m[...] + normalize_back(grad_hidden * gain, normed, factor)
    width = grid_out.shape[1]
    fill_grid(flat, buffer, width)
    grid_out[...] = buffer[:, :width, :].astype(BF16)
    if shifted:
        bottom, right, corner = edges
        bottom[...] = buffer[WIN - SHIFT :, :width, :].astype(BF16)
        right[...] = buffer[:, width - SHIFT : width, :].astype(BF16)
        corner[...] = buffer[WIN - SHIFT :, width - SHIFT : width, :].astype(BF16)


GELU_A = 0.7978845608028654
GELU_B = 0.044715


def gelu_parts(inner):
    square = inner * inner
    tanh = jnp.tanh(GELU_A * (inner * (1.0 + GELU_B * square)))
    return square, tanh


def mlp_forward_kernel(layer, *refs):
    place, middle, gains, up_own, *refs = refs
    up_parts, refs = refs[:4], refs[4:]
    down_own, *refs = refs
    down_parts, refs = refs[:4], refs[4:]
    grid_out, top, left, corner, up_w, down_w, sems, flat, buffer = refs
    width_c = flat.shape[1]
    up_copies = fetch(place, layer, up_own, up_parts, up_w, sems.at[0])
    down_copies = fetch(place, layer, down_own, down_parts, down_w, sems.at[1])
    normed, _ = normalize(middle[...])
    hidden = (normed * gains[layer, 1:2, :]).astype(BF16)
    output = middle[...]
    wait_all(up_copies)
    wait_all(down_copies)
    for chunk in range(up_w.shape[1] // width_c):
        cols = slice(chunk * width_c, (chunk + 1) * width_c)
        inner = mm(hidden, up_w[:, cols])
        _, tanh = gelu_parts(inner)
        output = output + mm((0.5 * inner * (1.0 + tanh)).astype(BF16), down_w[cols, :])
    flat[...] = output
    width = grid_out.shape[1]
    fill_grid(flat, buffer, width)
    grid_out[...] = buffer[:, :width, :].astype(BF16)
    top[...] = buffer[:SHIFT, :width, :].astype(BF16)
    left[...] = buffer[:, :SHIFT, :].astype(BF16)
    corner[...] = buffer[:SHIFT, :SHIFT, :].astype(BF16)


def mlp_backward_kernel(layer, mode, forward, *refs):
    place, middle, *refs = refs
    grid, refs = refs[:4], refs[4:]
    gains, up_own, *refs = refs
    up_parts, refs = refs[:4], refs[4:]
    down_own, *refs = refs
    down_parts, refs = refs[:4], refs[4:]
    n_out = 5 if forward else 4
    keep, send, gain_grad, grad_m, *out = refs[:n_out]
    up_w, down_w, sems, flat, buffer = refs[n_out:]
    width_c = flat.shape[1]
    up_copies = fetch(place, layer, up_own, up_parts, up_w, sems.at[0])
    down_copies = fetch(place, layer, down_own, down_parts, down_w, sems.at[1])
    normed, factor = normalize(middle[...])
    gain = gains[layer, 1:2, :]
    hidden = (normed * gain).astype(BF16)
    hidden_t = hidden.T
    fill_windows(mode, grid, flat)
    grad_low = flat[...].astype(BF16)
    output = middle[...]
    grad_hidden = jnp.zeros(flat.shape, F32)
    wait_all(up_copies)
    wait_all(down_copies)
    for chunk in range(up_w.shape[1] // width_c):
        cols = slice(chunk * width_c, (chunk + 1) * width_c)
        inner = mm(hidden, up_w[:, cols])
        square, tanh = gelu_parts(inner)
        activated = (0.5 * inner * (1.0 + tanh)).astype(BF16)
        slope = 0.5 * (1.0 + tanh) + (0.5 * GELU_A) * inner * (1.0 - tanh * tanh) * (
            1.0 + 3.0 * GELU_B * square
        )
        if forward:
            output = output + mm(activated, down_w[cols, :])
        store_rows(place, keep, send, chunk, 1, mm(activated.T, grad_low))
        grad_inner = (mm_nt(grad_low, down_w[cols, :]) * slope).astype(BF16)
        store_columns(place, keep, send, chunk, 0, mm(hidden_t, grad_inner))
        grad_hidden = grad_hidden + mm_nt(grad_inner, up_w[:, cols])
    gain_grad[...] = jnp.sum(grad_hidden * normed, 0, keepdims=True)
    grad_m[...] = flat[...] + normalize_back(grad_hidden * gain, normed, factor)
    if forward:
        flat[...] = output
        width = out[0].shape[1]
        fill_grid(flat, buffer, width)
        out[0][...] = buffer[:, :width, :].astype(BF16)


def collect_kernel(place, attend_one, mlp_one, attend_two, mlp_two, qkv, proj, up, down):
    rows, cols = attend_one.shape[-2:]
    for layer, attend, mlp in ((0, attend_one, mlp_one), (1, attend_two, mlp_two)):
        for core in range(2):
            for x in range(2):
                chunk = 2 * core + x
                for z in range(4):
                    at = (flip(place[0], core), flip(place[1], x), flip(place[2], z))
                    band = slice(z * rows, (z + 1) * rows)
                    span = slice(chunk * cols, (chunk + 1) * cols)
                    piece = attend[at + (0,)].astype(F32)
                    if chunk < 3:
                        qkv[layer, band, span] = piece
                    else:
                        proj[layer, band, :] = piece
                    up[layer, band, span] = mlp[at + (0,)].astype(F32)
                    first = (chunk * 4 + z) * rows
                    down[layer, first : first + rows, :] = mlp[at + (1,)].astype(F32)


VMEM = pl.BlockSpec(memory_space=pltpu.VMEM)
SMEM = pl.BlockSpec(memory_space=pltpu.SMEM)
ANY = pl.BlockSpec(memory_space=pl.ANY)


def call(kernel, name, ins, outs, scratch, flops):
    moved = sum(a.size * a.dtype.itemsize for _, a in ins) + sum(
        a.size * a.dtype.itemsize for a in outs
    )
    return pl.pallas_call(
        kernel,
        name=name,
        out_shape=outs,
        in_specs=[space for space, _ in ins],
        out_specs=[VMEM] * len(outs),
        scratch_shapes=scratch,
        cost_estimate=pl.CostEstimate(flops=flops, bytes_accessed=moved, transcendentals=0),
        compiler_params=pltpu.CompilerParams(vmem_limit_bytes=VMEM_LIMIT),
    )(*[array for _, array in ins])


def shape_of(*dims, dtype=BF16):
    return jax.ShapeDtypeStruct(dims, dtype)


def weight_ins(weight, parts):
    return [(ANY, weight)] + [(ANY, part) for part in parts]


def weight_scratch(first, second):
    return [
        pltpu.VMEM((2 * first.shape[1], first.shape[2]), BF16),
        pltpu.VMEM((2 * second.shape[1], second.shape[2]), BF16),
        pltpu.SemaphoreType.DMA((2, 5)),
    ]


def attend_forward(layer, mode, place, grid, gains, bias, same, qkv, proj):
    width, width_c = grid[0].shape[1:]
    tokens = width // WIN * SLOT
    heads = width_c // HEAD
    ins = [(SMEM, place)] + [(VMEM, g) for g in grid] + [(VMEM, gains), (VMEM, bias), (VMEM, same)]
    ins += weight_ins(*qkv) + weight_ins(*proj)
    outs = [
        shape_of(tokens, width_c),
        shape_of(tokens, width_c, dtype=F32),
        shape_of(width_c, tokens),
        shape_of(width_c, tokens),
        shape_of(tokens, width_c),
        shape_of(tokens, width_c),
        shape_of(width_c, tokens),
        shape_of(heads, SLOT, tokens, dtype=F32),
    ]
    scratch = weight_scratch(qkv[0], proj[0]) + [
        pltpu.VMEM((tokens, width_c), F32),
        pltpu.VMEM((width_c, tokens), BF16),
    ]
    kernel = functools.partial(attend_forward_kernel, layer, mode, len(grid))
    return call(kernel, "attend_forward", ins, outs, scratch, 2 * tokens * width_c * 5 * width_c)


def attend_backward(layer, shifted, place, grad_m, kept, gains, qkv, proj, width):
    tokens, width_c = grad_m.shape
    heads = width_c // HEAD
    x_in, _, *rest = kept
    ins = [(SMEM, place), (VMEM, grad_m), (VMEM, x_in), (VMEM, gains)] + [(VMEM, a) for a in rest]
    ins += weight_ins(*qkv) + weight_ins(*proj)
    pieces = shape_of(2, 2, 1, 4, width_c // 8, width_c)
    outs = [
        pieces,
        pieces,
        shape_of(1, width_c, dtype=F32),
        shape_of(heads, SLOT, PAIR, dtype=F32),
        shape_of(WIN, width, width_c),
    ]
    if shifted:
        outs += [
            shape_of(SHIFT, width, width_c),
            shape_of(WIN, SHIFT, width_c),
            shape_of(SHIFT, SHIFT, width_c),
        ]
    scratch = weight_scratch(qkv[0], proj[0]) + [
        pltpu.VMEM((3 * width_c, tokens), BF16),
        pltpu.VMEM((width_c, tokens), BF16),
        pltpu.VMEM((tokens, width_c), F32),
        pltpu.VMEM((WIN, -(-width // 8) * 8, width_c), F32),
    ]
    kernel = functools.partial(attend_backward_kernel, layer, shifted)
    return call(kernel, "attend_backward", ins, outs, scratch, 2 * tokens * width_c * 12 * width_c)


def mlp_forward(layer, place, middle, gains, up, down, width):
    tokens, width_c = middle.shape
    ins = [(SMEM, place), (VMEM, middle), (VMEM, gains)] + weight_ins(*up) + weight_ins(*down)
    outs = [
        shape_of(WIN, width, width_c),
        shape_of(SHIFT, width, width_c),
        shape_of(WIN, SHIFT, width_c),
        shape_of(SHIFT, SHIFT, width_c),
    ]
    scratch = weight_scratch(up[0], down[0]) + [
        pltpu.VMEM((tokens, width_c), F32),
        pltpu.VMEM((WIN, -(-width // 8) * 8, width_c), F32),
    ]
    kernel = functools.partial(mlp_forward_kernel, layer)
    return call(kernel, "mlp_forward", ins, outs, scratch, 2 * tokens * width_c * 8 * width_c)


def mlp_backward(layer, mode, forward, place, middle, grid, gains, up, down):
    tokens, width_c = middle.shape
    width = grid[0].shape[1]
    ins = [(SMEM, place), (VMEM, middle)] + [(VMEM, g) for g in grid] + [(VMEM, gains)]
    ins += weight_ins(*up) + weight_ins(*down)
    pieces = shape_of(2, 2, 2, 4, width_c // 8, width_c)
    outs = [
        pieces,
        pieces,
        shape_of(1, width_c, dtype=F32),
        shape_of(tokens, width_c, dtype=F32),
    ]
    if forward:
        outs.append(shape_of(WIN, width, width_c))
    scratch = weight_scratch(up[0], down[0]) + [
        pltpu.VMEM((tokens, width_c), F32),
        pltpu.VMEM((WIN, -(-width // 8) * 8, width_c), F32),
    ]
    kernel = functools.partial(mlp_backward_kernel, layer, mode, forward)
    return call(kernel, "mlp_backward", ins, outs, scratch, 2 * tokens * width_c * 20 * width_c)


def both_halves(own, axis, y):
    other = exchange(own, 0, 1)
    low = jnp.where(y == 0, own, other)
    high = jnp.where(y == 0, other, own)
    return jnp.concatenate([low, high], axis=axis)


def same_label(labels):
    same = labels[:, :, None] == labels[:, None, :]
    return same.astype(F32).transpose(1, 0, 2).reshape(SLOT, -1)


def per_device(
    tokens, norm_gains, w_qkv, w_proj, w_up, w_down, tables, region_ids, rel_index, cotangent
):
    seq, y = lax.axis_index("seq"), lax.axis_index("fsdp")
    place = jnp.stack([seq & 1, (seq >> 1) & 1, (seq >> 2) & 3, y]).astype(jnp.int32)
    width = tokens.shape[1]
    weights = [
        {
            name: (weight, other_half(weight, layer, place))
            for name, weight in (("qkv", w_qkv), ("proj", w_proj), ("up", w_up), ("down", w_down))
        }
        for layer in range(2)
    ]
    gains = both_halves(norm_gains, 2, y).astype(F32)
    table = both_halves(tables, 1, y)
    index = rel_index.reshape(WIN, WIN, WIN, WIN)
    index = jnp.pad(index, [(0, 1)] * 4, constant_values=-1).reshape(SLOT, SLOT).T
    index = jnp.concatenate([index, index], axis=1)
    onehot = (index[:, :, None] == jnp.arange(TABLE, dtype=jnp.int32)).astype(BF16)
    bias = jnp.einsum("lht,jit->lhji", table, onehot, preferred_element_type=F32)
    labels = region_ids.reshape(WIN, width // WIN, WIN).transpose(1, 0, 2)
    edge = [(0, 0), (0, 1), (0, 1)]
    same_two = same_label(jnp.pad(labels, edge, constant_values=-1).reshape(-1, SLOT))
    same_one = same_label(
        jnp.pad(jnp.zeros_like(labels), edge, constant_values=-1).reshape(-1, SLOT)
    )

    one, two = weights
    kept_one = attend_forward(
        0, "plain", place, (tokens,), gains, bias[0], same_one, one["qkv"], one["proj"]
    )
    middle, *edges = mlp_forward(0, place, kept_one[1], gains, one["up"], one["down"], width)
    rolled = (middle, *halo(*edges, 1))
    top = (
        cotangent,
        *halo(cotangent[:SHIFT], cotangent[:, :SHIFT], cotangent[:SHIFT, :SHIFT], 1),
    )
    kept_two = attend_forward(
        1, "in", place, rolled, gains, bias[1], same_two, two["qkv"], two["proj"]
    )
    keep_m2, send_m2, gain_b2, grad_m2, out_two = mlp_backward(
        1, "in", True, place, kept_two[1], top, gains, two["up"], two["down"]
    )
    keep_a2, send_a2, gain_a2, bias_grad2, grad_in2, *edges = attend_backward(
        1, True, place, grad_m2, kept_two, gains, two["qkv"], two["proj"], width
    )
    back = (grad_in2, *halo(*edges, -1))
    keep_m1, send_m1, gain_b1, grad_m1 = mlp_backward(
        0, "out", False, place, kept_one[1], back, gains, one["up"], one["down"]
    )
    keep_a1, send_a1, gain_a1, bias_grad1, tokens_grad = attend_backward(
        0, False, place, grad_m1, kept_one, gains, one["qkv"], one["proj"], width
    )

    rest = width - SHIFT
    above, beside, corner = halo(
        out_two[WIN - SHIFT :, :rest], out_two[: WIN - SHIFT, rest:], out_two[WIN - SHIFT :, rest:], -1
    )
    mixed = jnp.concatenate(
        [
            jnp.concatenate([corner, above], axis=1),
            jnp.concatenate([beside, out_two[: WIN - SHIFT, :rest]], axis=1),
        ],
        axis=0,
    )

    all_m2 = reduce_pieces(keep_m2, send_m2)
    all_a2 = reduce_pieces(keep_a2, send_a2)
    all_m1 = reduce_pieces(keep_m1, send_m1)
    all_a1 = reduce_pieces(keep_a1, send_a1)
    bias_grads = jnp.stack([bias_grad1, bias_grad2])
    table_grads = jnp.einsum(
        "lhji,jit->lht", bias_grads.astype(BF16), onehot, preferred_element_type=F32
    )
    width_c = tokens.shape[2]
    heads = table.shape[1]
    small = jnp.concatenate(
        [
            gain_a1,
            gain_b1,
            gain_a2,
            gain_b2,
            jnp.pad(table_grads.reshape(2 * heads, TABLE), [(0, 0), (0, width_c - TABLE)]),
        ],
        axis=0,
    )
    small = sum_small(small)
    gains_grad = lax.dynamic_slice_in_dim(
        small[:4].reshape(2, 2, width_c), y * (width_c // 2), width_c // 2, axis=2
    )
    tables_grad = lax.dynamic_slice_in_dim(
        small[4:, :TABLE].reshape(2, heads, TABLE), y * (heads // 2), heads // 2, axis=1
    )
    grads = [shape_of(*w.shape, dtype=F32) for w in (w_qkv, w_proj, w_up, w_down)]
    ins = [(SMEM, place)] + [(VMEM, a) for a in (all_a1, all_m1, all_a2, all_m2)]
    qkv_grad, proj_grad, up_grad, down_grad = call(collect_kernel, "collect", ins, grads, [], 1000)
    return (mixed, tokens_grad, gains_grad, qkv_grad, proj_grad, up_grad, down_grad, tables_grad)


def solution(mesh):
    return jax.shard_map(
        per_device,
        mesh=mesh,
        in_specs=(
            P("seq", "fsdp", None),
            P(None, None, "fsdp"),
            P(None, "fsdp", None),
            P(None, "fsdp", None),
            P(None, "fsdp", None),
            P(None, "fsdp", None),
            P(None, "fsdp", None),
            P("seq", "fsdp"),
            P(),
            P("seq", "fsdp", None),
        ),
        out_specs=(
            P("seq", "fsdp", None),
            P("seq", "fsdp", None),
            P(None, None, "fsdp"),
            P(None, "fsdp", None),
            P(None, "fsdp", None),
            P(None, "fsdp", None),
            P(None, "fsdp", None),
            P(None, "fsdp", None),
        ),
        check_vma=False,
    )
```

```python
import functools
import types

import jax
import jax.numpy as jnp
from jax import lax
from jax.experimental import pallas as pl
from jax.experimental.pallas import tpu as pltpu
from jax.sharding import PartitionSpec as P

WIN = 7
SHIFT = 3
TABLE = 169
SIDE = 8
SLOT = SIDE * SIDE
HEAD = 32
PAIR = 2 * SLOT
EPSILON = 1e-05
MASKED_SCORE = -1000000000.0
F32 = jnp.float32
BF16 = jnp.bfloat16
VMEM_LIMIT = 24 * 1024 * 1024
PACK_VMEM_LIMIT = 60 * 1024 * 1024
BYTES_PER_US = 3500000


def exchange(array, ds, dy):
    n, m = lax.axis_size("seq"), lax.axis_size("fsdp")
    pairs = [(s * m + y, (s ^ ds) * m + (y ^ dy)) for s in range(n) for y in range(m)]
    return lax.ppermute(array, ("seq", "fsdp"), pairs)


def take_from(array, ds, dy):
    n, m = lax.axis_size("seq"), lax.axis_size("fsdp")
    pairs = [((s + ds) % n * m + (y + dy) % m, s * m + y) for s in range(n) for y in range(m)]
    return lax.ppermute(array, ("seq", "fsdp"), pairs)


def halo(near_rows, near_cols, corner, step):
    return (
        take_from(near_rows, step, 0),
        take_from(near_cols, 0, step),
        take_from(corner, step, step),
    )


def share_halves(piece, after=()):
    first = exchange(piece, 0, 1)
    if after:
        first = tie(first, after)
    return (first, exchange(first, 1, 0))


def add(*terms):
    total = terms[0].astype(F32)
    for term in terms[1:]:
        total = total + term.astype(F32)
    return total


def sum_higher(value):
    step = 16
    while step < lax.axis_size("seq"):
        value = add(value, exchange(value, step, 0)).astype(value.dtype)
        step *= 2
    return value


def start_cube(keep, got, small):
    kinds, _, rows, cols = keep.shape[2:]
    count = small[0].shape[0]
    out = shape_of(kinds * 2 * rows + count, cols)
    ins = {"keep": (VMEM, keep), "got": (VMEM, got)} | numbered("small", VMEM, small)
    r = call(add_core_kernel, "add_core", ins, {"out" + str(i): out for i in range(8)}, {})
    outs = listed(r, "out")
    return [outs[0]] + [
        exchange(outs[i], (i >> 1 & 1) * 2 + (i & 1) * 4, i >> 2) for i in (7, 6, 5, 4, 3, 2, 1)
    ]


def start_side(keeps, gots, after=()):
    kinds = sum(keep.shape[2] for keep in keeps)
    out = shape_of(2, kinds, *keeps[0].shape[3:])
    ins = numbered("keep", VMEM, keeps) | numbered("got", VMEM, gots)
    r = call(add_side_kernel, "add_side", ins, {"own": out, "other": out}, {}, after)
    return r.own, exchange(r.other, 0, 1)


def start_face(parts, after=()):
    _, kinds, _, rows, cols = parts[0].shape
    out = shape_of(kinds * 2 * rows, cols)
    ins = numbered("part", VMEM, parts)
    outs = {"out" + str(i): out for i in range(4)}
    r = call(add_face_kernel, "add_face", ins, outs, {}, after)
    return r.out0, exchange(r.out3, 6, 0), exchange(r.out2, 2, 0), exchange(r.out1, 4, 0)


def finish_sum(parts, rows, after=()):
    kinds = parts[0].shape[0] // (2 * rows)
    out = shape_of(parts[0].shape[0] - kinds * rows, parts[0].shape[1])
    kernel = functools.partial(halve_kernel, kinds, rows)
    ins = numbered("part", VMEM, parts)
    r = call(kernel, "halve", ins, {"own": out, "other": out}, {}, after)
    return sum_higher(add(r.own, exchange(r.other, 8, 0)).astype(BF16))


def gather(total, rows, after=()):
    ins = {"own": (VMEM, total), "other": (VMEM, exchange(total, 8, 0))}
    out = shape_of(2, rows, total.shape[1])
    pair = call(stack_kernel, "stack", ins, {"out": out}, {}, after).out
    here = [pair, exchange(pair, 4, 0), exchange(pair, 2, 0), exchange(pair, 6, 0)]
    return here + [exchange(part, 1, 0) for part in here]


def flip(index, bits):
    return jnp.bitwise_xor(index, bits)


def pack_kernel(layer, r):
    core = r.place[0]
    width_c = r.proj.shape[2]
    rows = r.qkv.shape[1] // 2
    if layer == 0:
        attend, mlp = r.attend, r.mlp
    else:
        attend, mlp = r.both.at[:rows], r.both.at[rows:]
    start = pl.multiple_of(core * rows, 16)
    pairs = [
        (r.qkv.at[layer, pl.ds(start, rows), :], attend.at[:, : 3 * width_c]),
        (r.proj.at[layer, pl.ds(start, rows), :], attend.at[:, 3 * width_c :]),
        (r.up.at[layer, pl.ds(start, rows), :], mlp.at[:rows]),
    ]
    for index in range(4):
        first = pl.multiple_of((core * 4 + index) * rows, 16)
        cols = slice(index * width_c, (index + 1) * width_c)
        pairs.append((r.down.at[layer, pl.ds(first, rows), :], mlp.at[rows:, cols]))
    copies = start_copies(pairs, r.sems)
    wait_all(copies)


def pack_small_kernel(r):
    r.small[...] = jnp.zeros_like(r.small)
    for index in range(2):
        r.small[2 * index : 2 * index + 2, : r.gains.shape[2]] = r.gains[index].astype(F32)
        first = 4 + index * r.tables.shape[1]
        r.small[first : first + r.tables.shape[1], :TABLE] = r.tables[index].astype(F32)


def table_sums_kernel(r):
    heads = r.grad0.shape[0]
    total = jnp.zeros((2 * heads, TABLE), F32)
    for key in range(SLOT):
        pair = jnp.concatenate([r.grad0[:, key, :], r.grad1[:, key, :]], axis=0)
        total = total + mm(pair.astype(BF16), r.onehot[key])
    r.wide[...] = jnp.zeros_like(r.wide)
    half = r.out.shape[1] // 2
    r.wide[:heads, :TABLE] = total[:heads]
    r.wide[:heads, half : half + TABLE] = total[heads:]
    r.out[...] = r.wide[...].astype(BF16)


def params_kernel(r):
    half = r.gains.shape[2] // 2
    heads = r.table.shape[1] // 2
    flipped = r.place[3] == 1
    first = jnp.where(flipped, r.other[...], r.own[...])
    second = jnp.where(flipped, r.own[...], r.other[...])
    for index in range(2):
        for part, value in ((0, first), (1, second)):
            r.gains[index, :, part * half : (part + 1) * half] = value[
                2 * index : 2 * index + 2, :half
            ]
            rows = value[4 + index * heads : 4 + (index + 1) * heads, :TABLE]
            r.table[index, part * heads : (part + 1) * heads, :] = rows


def start_copies(pairs, sems):
    copies = [
        pltpu.make_async_copy(source, target, sems.at[index])
        for index, (source, target) in enumerate(pairs)
    ]
    for copy in copies:
        copy.start()
    return copies


def fetch(place, layer, own, parts, pick, full, sems):
    half = full.shape[0] // 2
    rows = half // len(parts)
    y = place[3]
    pairs = [(own.at[layer], full.at[pl.ds(pl.multiple_of(y * half, 16), half)])]
    for spot, part in zip((place[0], flip(place[0], 1)), parts):
        pieces = pick(part)
        count = rows // len(pieces)
        for index, piece in enumerate(pieces):
            start = pl.multiple_of((1 - y) * half + spot * rows + index * count, 16)
            pairs.append((piece, full.at[pl.ds(start, count)]))
    return start_copies(pairs, sems)


def fetch_attend(place, layer, own, parts, qkv_w, proj_w, sems):
    rows = own[0].shape[1] // 2
    wide = qkv_w.shape[1]

    def qkv(part):
        return [part.at[:rows, :wide]]

    def proj(part):
        return [part.at[:rows, wide:]]

    return (
        fetch(place, layer, own[0], parts, qkv, qkv_w, sems.at[0]),
        fetch(place, layer, own[1], parts, proj, proj_w, sems.at[1]),
    )


def fetch_mlp(place, layer, own, parts, up_w, down_w, sems):
    rows = own[0].shape[1] // 2
    first = parts[0].shape[0] - 2 * rows
    width_c = down_w.shape[1]

    def up(part):
        return [part.at[first : first + rows]]

    def down(part):
        return [part.at[first + rows :, i * width_c : (i + 1) * width_c] for i in range(4)]

    return (
        fetch(place, layer, own[0], parts, up, up_w, sems.at[0]),
        fetch(place, layer, own[1], parts, down, down_w, sems.at[1]),
    )


def add_refs(refs):
    total = refs[0][...].astype(F32)
    for ref in refs[1:]:
        total = total + ref[...].astype(F32)
    return total


def add_core_kernel(r):
    kinds, _, rows, _ = r.keep.shape[2:]
    small = (r.small0[...].astype(F32) + r.small1[...].astype(F32)).astype(BF16)
    for index, out in enumerate(listed(r, "out")):
        y, x, z = index >> 2, index >> 1 & 1, index & 1
        for kind in range(kinds):
            for high in range(2):
                at = (y, x, kind, 2 * high + z)
                first = (kind * 2 + high) * rows
                value = r.keep[at].astype(F32) + r.got[at].astype(F32)
                out[first : first + rows, :] = value.astype(BF16)
        out[kinds * 2 * rows :, :] = small


def add_side_kernel(r):
    for y, out in enumerate((r.own, r.other)):
        first = 0
        for keep, got in zip(listed(r, "keep"), listed(r, "got")):
            for x in range(2):
                value = keep[y, x].astype(F32) + got[y, x].astype(F32)
                out[x, first : first + keep.shape[2]] = value.astype(BF16)
            first += keep.shape[2]


def add_face_kernel(r):
    _, kinds, _, rows, _ = r.part0.shape
    for index, out in enumerate(listed(r, "out")):
        x, z = index >> 1, index & 1
        for kind in range(kinds):
            for high in range(2):
                at = (x, kind, 2 * high + z)
                first = (kind * 2 + high) * rows
                value = r.part0[at].astype(F32) + r.part1[at].astype(F32)
                out[first : first + rows, :] = value.astype(BF16)


def halve_kernel(kinds, rows, r):
    parts = listed(r, "part")
    for high, out in enumerate((r.own, r.other)):
        for kind in range(kinds):
            first = (kind * 2 + high) * rows
            value = add_refs([part.at[first : first + rows, :] for part in parts])
            out[kind * rows : (kind + 1) * rows, :] = value.astype(BF16)
        if out.shape[0] > kinds * rows:
            value = add_refs([part.at[kinds * 2 * rows :, :] for part in parts])
            out[kinds * rows :, :] = value.astype(BF16)


def stack_kernel(r):
    rows = r.out.shape[1]
    r.out[0] = r.own[:rows, :]
    r.out[1] = r.other[:rows, :]


def wait_all(copies):
    for copy in copies:
        copy.wait()


def row_segments(mode, refs, row, width):
    if mode == "plain":
        return [(0, refs[0][row], 0, width)]
    own, rows, cols, corner = refs
    rest = width - SHIFT
    if mode == "in":
        if row < WIN - SHIFT:
            return [
                (0, own[row + SHIFT], SHIFT, rest),
                (rest, cols[row + SHIFT], 0, SHIFT),
            ]
        at = row - (WIN - SHIFT)
        return [(0, rows[at], SHIFT, rest), (rest, corner[at], 0, SHIFT)]
    if row >= SHIFT:
        return [(0, cols[row - SHIFT], 0, SHIFT), (SHIFT, own[row - SHIFT], 0, rest)]
    return [(0, corner[row], 0, SHIFT), (SHIFT, rows[row], 0, rest)]


def fill_windows(mode, refs, out):
    width = refs[0].shape[1]
    out[...] = jnp.zeros_like(out)
    for row in range(WIN):
        for first, source, start, count in row_segments(mode, refs, row, width):
            source = source.astype(F32)
            for window in range(width // WIN):
                low = max(first, window * WIN)
                high = min(first + count, window * WIN + WIN)
                if low < high:
                    spot = window * SLOT + row * SIDE + low - window * WIN
                    begin = start + low - first
                    out[spot : spot + high - low, :] = source[begin : begin + high - low, :]


def fill_grid(source, buffer, width):
    for row in range(WIN):
        for window in range(width // WIN):
            spot = window * SLOT + row * SIDE
            buffer[row, window * WIN : window * WIN + WIN, :] = source[spot : spot + WIN, :]


def normalize(values):
    centred = values - jnp.mean(values, -1, keepdims=True)
    factor = lax.rsqrt(jnp.mean(centred * centred, -1, keepdims=True) + EPSILON)
    return centred * factor, factor


def normalize_back(grad_norm, normed, factor):
    spread = jnp.mean(grad_norm * normed, -1, keepdims=True)
    return factor * (grad_norm - jnp.mean(grad_norm, -1, keepdims=True) - normed * spread)


def mm(left, right):
    return lax.dot_general(left, right, (((1,), (0,)), ((), ())), preferred_element_type=F32)


def mm_nt(left, right):
    return lax.dot_general(left, right, (((1,), (1,)), ((), ())), preferred_element_type=F32)


def only_head(group, which):
    rows = lax.broadcasted_iota(jnp.int32, group.shape, 0)
    inside = (rows >= which * HEAD) & (rows < (which + 1) * HEAD)
    return jnp.where(inside, group, jnp.zeros_like(group))


def diagonal(block):
    lanes = lax.broadcasted_iota(jnp.int32, (SLOT, PAIR), 1)
    return jnp.where(lanes < SLOT, block[:SLOT], block[SLOT:])


def spread_diagonal(packed):
    lanes = lax.broadcasted_iota(jnp.int32, (SLOT, PAIR), 1)
    low = jnp.where(lanes < SLOT, packed, 0.0)
    high = jnp.where(lanes < SLOT, 0.0, packed)
    return jnp.concatenate([low, high], axis=0).astype(BF16)


def store_columns(r, out, x, kind, value):
    rows = value.shape[0] // 8
    value = value.astype(BF16)
    for y in range(2):
        for z in range(4):
            first = (y * 4 + z) * rows
            at = (flip(r.place[3], y), flip(r.place[1], x), kind, flip(r.place[2], z))
            out[at] = value[first : first + rows]


def store_rows(r, out, y, kind, value):
    rows = value.shape[0] // 8
    value = value.astype(BF16)
    for x in range(2):
        for z in range(4):
            first = (x * 4 + z) * rows
            at = (flip(r.place[3], y), flip(r.place[1], x), kind, flip(r.place[2], z))
            out[at] = value[first : first + rows]


def grid_refs(r, which):
    if not hasattr(r, "rows_in"):
        return [r.own]
    return [r.own if which == 0 else r.own_two] + [
        edge.at[which] for edge in (r.rows_in, r.cols_in, r.corner_in)
    ]


def attend_forward_kernel(layer, mode, r):
    width_c = r.flat.shape[1]
    heads = width_c // HEAD
    copies = fetch_attend(
        r.place, layer, (r.qkv, r.proj), listed(r, "a_part"), r.qkv_w, r.proj_w, r.a_sems
    )
    fill_windows(mode, grid_refs(r, 0), r.flat)
    r.x[...] = r.flat[...].astype(BF16)
    normed, _ = normalize(r.flat[...])
    hidden = (normed * r.gains[layer, 0:1, :]).astype(BF16)
    wait_all(copies[0])
    query = (mm(hidden, r.qkv_w[:, :width_c]) * HEAD ** (-0.5)).astype(BF16)
    r.query_t[...] = query.T
    r.keys[...] = mm(hidden, r.qkv_w[:, width_c : 2 * width_c]).astype(BF16)
    r.keys_t[...] = r.keys[...].T
    r.values[...] = mm(hidden, r.qkv_w[:, 2 * width_c :]).astype(BF16)
    r.values_t[...] = r.values[...].T
    if mode == "plain":
        place = lax.broadcasted_iota(jnp.int32, (SLOT, PAIR), 0)
        meet = (place < WIN * SIDE) & (jnp.bitwise_and(place, SIDE - 1) < WIN)
    for head in range(heads):
        group = slice(head // 4 * 128, head // 4 * 128 + 128)
        rows = slice(head * HEAD, head * HEAD + HEAD)
        for pair in range(r.flat.shape[0] // PAIR):
            span = slice(pair * PAIR, pair * PAIR + PAIR)
            raw = mm(r.keys[span, group], only_head(r.query_t[group, span], head % 4))
            if mode != "plain":
                meet = r.same[:, span] > 0.5
            scores = jnp.where(meet, diagonal(raw) + r.bias[layer, head], MASKED_SCORE)
            weighted = jnp.exp(scores - jnp.max(scores, 0, keepdims=True))
            attention = weighted / jnp.sum(weighted, 0, keepdims=True)
            r.probs[head, :, span] = attention
            r.mixed_t[rows, span] = mm(r.values_t[rows, span], spread_diagonal(attention)).astype(
                BF16
            )
    wait_all(copies[1])
    r.middle[...] = r.flat[...] + mm(r.mixed_t[...].T, r.proj_w[...])


def attend_backward_kernel(layer, parts, kind, r):
    width_c = r.x.shape[1]
    heads = width_c // HEAD
    if "s" in parts or "i" in parts:
        copies = fetch_attend(
            r.place, layer, (r.qkv, r.proj), listed(r, "a_part"), r.qkv_w, r.proj_w, r.a_sems
        )
    normed, factor = normalize(r.x[...].astype(F32))
    gain = r.gains[layer, 0:1, :]
    attended = r.grad_m[...].astype(BF16)
    if "s" in parts:
        wait_all(copies[1])
        r.out_t[...] = mm_nt(r.proj_w[...], attended).astype(BF16)
        for head in range(heads):
            group = slice(head // 4 * 128, head // 4 * 128 + 128)
            rows = slice(head * HEAD, head * HEAD + HEAD)
            row_k = slice(width_c + head * HEAD, width_c + head * HEAD + HEAD)
            row_v = slice(2 * width_c + head * HEAD, 2 * width_c + head * HEAD + HEAD)
            total = jnp.zeros((SLOT, PAIR), F32)
            for pair in range(r.x.shape[0] // PAIR):
                span = slice(pair * PAIR, pair * PAIR + PAIR)
                attention = r.probs[head, :, span]
                grad_p = diagonal(
                    mm(r.values[span, group], only_head(r.out_t[group, span], head % 4))
                )
                grad_s = attention * (grad_p - jnp.sum(grad_p * attention, 0, keepdims=True))
                total = total + grad_s
                spread_p = spread_diagonal(attention)
                spread_s = spread_diagonal(grad_s)
                grad_q = mm(r.keys_t[rows, span], spread_s) * HEAD ** (-0.5)
                r.grad_t[rows, span] = grad_q.astype(BF16)
                r.grad_t[row_k, span] = mm_nt(r.query_t[rows, span], spread_s).astype(BF16)
                r.grad_t[row_v, span] = mm_nt(r.out_t[rows, span], spread_p).astype(BF16)
            r.bias_grad[head] = total
    if "w" in parts:
        r.left[0] = (normed * gain).astype(BF16).T
        r.left[1] = r.mixed_t[...]
        r.right[: 3 * width_c, :] = r.grad_t[...]
        r.right[3 * width_c :, :] = attended.T
        for apart, out in ((1, r.send), (0, r.keep)):
            for x in range(2):
                chunk = 2 * flip(r.place[0], apart) + x
                left = r.left[(chunk == 3).astype(jnp.int32)]
                right = r.right[pl.ds(pl.multiple_of(chunk * width_c, 128), width_c), :]
                store_columns(r, out, x, kind, mm_nt(left, right))
    if "s" in parts or "i" in parts:
        if "s" not in parts:
            wait_all(copies[1])
        wait_all(copies[0])
    if "i" in parts:
        grad_hidden = mm(r.qkv_w[...], r.grad_t[...]).T
        r.flat[...] = r.grad_m[...] + normalize_back(grad_hidden * gain, normed, factor)
        width = r.grid.shape[1]
        fill_grid(r.flat, r.buffer, width)
        r.grid[...] = r.buffer[:, :width, :].astype(BF16)
        if hasattr(r, "rows"):
            r.rows[0] = r.buffer[WIN - SHIFT :, :width, :].astype(BF16)
            r.cols[0] = r.buffer[:, width - SHIFT : width, :].astype(BF16)
            r.corner[0] = r.buffer[WIN - SHIFT :, width - SHIFT : width, :].astype(BF16)


GELU_A = 0.7978845608028654
GELU_B = 0.044715


def gelu_parts(inner):
    square = inner * inner
    tanh = jnp.tanh(GELU_A * (inner * (1.0 + GELU_B * square)))
    return square, tanh


def mlp_forward_kernel(layer, r):
    width_c = r.flat.shape[1]
    copies = fetch_mlp(
        r.place, layer, (r.up, r.down), listed(r, "m_part"), r.up_w, r.down_w, r.m_sems
    )
    normed, _ = normalize(r.middle[...])
    hidden = (normed * r.gains[layer, 1:2, :]).astype(BF16)
    output = r.middle[...]
    wait_all(copies[0])
    wait_all(copies[1])
    for chunk in range(r.up_w.shape[1] // width_c):
        cols = slice(chunk * width_c, (chunk + 1) * width_c)
        inner = mm(hidden, r.up_w[:, cols])
        _, tanh = gelu_parts(inner)
        output = output + mm((0.5 * inner * (1.0 + tanh)).astype(BF16), r.down_w[cols, :])
    r.flat[...] = output
    width = r.grid.shape[1]
    fill_grid(r.flat, r.buffer, width)
    r.grid[...] = r.buffer[:, :width, :].astype(BF16)
    r.rows[0] = r.buffer[:SHIFT, :width, :].astype(BF16)
    r.cols[0] = r.buffer[:, :SHIFT, :].astype(BF16)
    r.corner[0] = r.buffer[:SHIFT, :SHIFT, :].astype(BF16)
    r.rows[1] = r.top[:SHIFT]
    r.cols[1] = r.top[:, :SHIFT, :]
    r.corner[1] = r.top[:SHIFT, :SHIFT, :]


def mlp_backward_kernel(layer, mode, which, r):
    width_c = r.flat.shape[1]
    copies = fetch_mlp(
        r.place, layer, (r.up, r.down), listed(r, "m_part"), r.up_w, r.down_w, r.m_sems
    )
    normed, factor = normalize(r.middle[...])
    gain = r.gains[layer, 1:2, :]
    hidden = (normed * gain).astype(BF16)
    hidden_t = hidden.T
    fill_windows(mode, grid_refs(r, which), r.flat)
    grad_low = r.flat[...].astype(BF16)
    forward = hasattr(r, "out")
    output = r.middle[...]
    grad_hidden = jnp.zeros(r.flat.shape, F32)
    wait_all(copies[0])
    wait_all(copies[1])
    outs = (r.keep, r.send)
    for up_apart, down_apart in ((1, 1), (1, 0), (0, 1), (0, 0)):
        high, low = flip(r.place[0], up_apart), flip(r.place[0], down_apart)
        cols = pl.ds(pl.multiple_of((2 * high + low) * width_c, 128), width_c)
        inner = mm(hidden, r.up_w[:, cols])
        square, tanh = gelu_parts(inner)
        activated = (0.5 * inner * (1.0 + tanh)).astype(BF16)
        slope = 0.5 * (1.0 + tanh) + (0.5 * GELU_A) * inner * (1.0 - tanh * tanh) * (
            1.0 + 3.0 * GELU_B * square
        )
        if forward:
            output = output + mm(activated, r.down_w[cols, :])
        store_rows(r, outs[down_apart], high, 1, mm(activated.T, grad_low))
        grad_inner = (mm_nt(grad_low, r.down_w[cols, :]) * slope).astype(BF16)
        store_columns(r, outs[up_apart], low, 0, mm(hidden_t, grad_inner))
        grad_hidden = grad_hidden + mm_nt(grad_inner, r.up_w[:, cols])
    r.grad_m[...] = r.flat[...] + normalize_back(grad_hidden * gain, normed, factor)
    if forward:
        r.flat[...] = output
        width = r.out.shape[1]
        fill_grid(r.flat, r.buffer, width)
        r.out[...] = r.buffer[:, :width, :].astype(BF16)
        r.rows[1] = r.buffer[WIN - SHIFT :, :width, :].astype(BF16)
        r.cols[1] = r.buffer[:, width - SHIFT : width, :].astype(BF16)
        r.corner[1] = r.buffer[WIN - SHIFT :, width - SHIFT : width, :].astype(BF16)


def roll_out_kernel(r):
    refs = grid_refs(r, 1)
    width = r.mixed.shape[1]
    for row in range(WIN):
        for first, source, start, count in row_segments("out", refs, row, width):
            r.buffer[row, first : first + count, :] = source.astype(F32)[start : start + count, :]
    r.mixed[...] = r.buffer[:, :width, :].astype(BF16)


def collect_kernel(layer, r):
    rows, cols = r.table.shape[-2:]
    half = r.qkv.shape[1]
    for index, ref in enumerate(listed(r, "all")):
        for high in range(2):
            for kind in range(3):
                piece = ref[high, kind * rows : (kind + 1) * rows, :]
                r.table[index >> 2, index >> 1 & 1, 2 * high + (index & 1), kind] = piece
    for core in range(2):
        for x in range(2):
            chunk = 2 * core + x
            for z in range(4):
                at = (flip(r.place[0], core), flip(r.place[1], x), flip(r.place[2], z))
                band = slice(z * rows, (z + 1) * rows)
                span = slice(chunk * cols, (chunk + 1) * cols)
                r.up[0, band, span] = r.table[at + (0,)].astype(F32)
                first = (chunk * 4 + z) * rows
                r.down[0, first : first + rows, :] = r.table[at + (1,)].astype(F32)
                piece = r.table[at + (2,)].astype(F32)
                if chunk < 3:
                    r.qkv[0, band, span] = piece
                else:
                    r.proj[0, band, :] = piece
    r.wide[...] = jnp.zeros_like(r.wide)
    for which, weight, grad in ((0, r.w_qkv, r.qkv), (1, r.w_up, r.up)):
        total = jnp.zeros((half, 128), F32)
        for first in range(0, grad.shape[2], 128):
            span = slice(first, first + 128)
            total = total + weight[layer, :, span].astype(F32) * grad[0, :, span]
        r.wide[:half, :] = total
        line = jnp.sum(r.wide[...].T, 0, keepdims=True)[:, :half]
        r.gains_grad[0, which : which + 1, :] = line / r.gains[layer, which : which + 1, :].astype(
            F32
        )


VMEM = pl.BlockSpec(memory_space=pltpu.VMEM)
ANY = pl.BlockSpec(memory_space=pl.ANY)
HBM = pl.BlockSpec(memory_space=pltpu.HBM)


def listed(r, name):
    found = []
    while name + str(len(found)) in vars(r):
        found.append(getattr(r, name + str(len(found))))
    return found


def numbered(name, space, arrays):
    return {name + str(index): (space, array) for index, array in enumerate(arrays)}


def place_here():
    seq = lax.axis_index("seq")
    return (
        jnp.bitwise_and(seq, 1),
        jnp.bitwise_and(lax.shift_right_logical(seq, 1), 1),
        jnp.bitwise_and(lax.shift_right_logical(seq, 2), 3),
        lax.axis_index("fsdp"),
    )


def shape_of(*dims, dtype=BF16):
    return jax.ShapeDtypeStruct(dims, dtype)


def call(kernel, name, ins, outs, scratch, after=(), us=1, vmem=VMEM_LIMIT):
    names = list(ins) + [None] * len(after) + list(outs) + list(scratch)

    def body(*refs):
        named = {n: ref for n, ref in zip(names, refs) if n}
        kernel(types.SimpleNamespace(place=place_here(), **named))

    results = pl.pallas_call(
        body,
        name=name,
        out_shape=list(outs.values()),
        in_specs=[space for space, _ in ins.values()] + [ANY] * len(after),
        out_specs=[VMEM] * len(outs),
        scratch_shapes=list(scratch.values()),
        cost_estimate=pl.CostEstimate(
            flops=1000, bytes_accessed=us * BYTES_PER_US, transcendentals=0
        ),
        compiler_params=pltpu.CompilerParams(vmem_limit_bytes=vmem),
    )(*[array for _, array in ins.values()], *after)
    return types.SimpleNamespace(**dict(zip(outs, results)))


def weight_scratch(first, second, names):
    return {
        names[0]: pltpu.VMEM((2 * first.shape[1], first.shape[2]), BF16),
        names[1]: pltpu.VMEM((2 * second.shape[1], second.shape[2]), BF16),
        names[2]: pltpu.SemaphoreType.DMA((2, 9)),
    }


def attend_weights(weights, parts):
    ins = {"qkv": (HBM, weights[0]), "proj": (HBM, weights[1])} | numbered("a_part", HBM, parts)
    return ins, weight_scratch(weights[0], weights[1], ("qkv_w", "proj_w", "a_sems"))


def mlp_weights(weights, parts):
    ins = {"up": (HBM, weights[2]), "down": (HBM, weights[3])} | numbered("m_part", HBM, parts)
    return ins, weight_scratch(weights[2], weights[3], ("up_w", "down_w", "m_sems"))


def tie(array, after):
    return pl.pallas_call(
        lambda *refs: None,
        name="tie",
        out_shape=jax.ShapeDtypeStruct(array.shape, array.dtype),
        in_specs=[ANY] * (1 + len(after)),
        out_specs=ANY,
        input_output_aliases={0: 0},
        compiler_params=pltpu.CompilerParams(vmem_limit_bytes=1024 * 1024),
    )(array, *after)


def grid_buffer(width, width_c):
    return pltpu.VMEM((WIN, -(-width // 8) * 8, width_c), F32)


def pack(layer, weights, after=()):
    rows = weights[0].shape[1] // 2
    wide = 4 * weights[1].shape[2]
    ins = {
        name: (HBM, w) for name, w in zip(("qkv", "proj", "up", "down"), weights)
    }
    outs = {"both": shape_of(3 * rows, wide)}
    if layer == 0:
        outs = {"attend": shape_of(rows, wide), "mlp": shape_of(2 * rows, wide)}
    scratch = {"sems": pltpu.SemaphoreType.DMA((7,))}
    kernel = functools.partial(pack_kernel, layer)
    limit = PACK_VMEM_LIMIT if layer == 0 else VMEM_LIMIT
    return call(kernel, "pack", ins, outs, scratch, after, vmem=limit)


def pack_small(gains, tables, after=()):
    ins = {"gains": (VMEM, gains), "tables": (VMEM, tables)}
    outs = {"small": shape_of(4 + 2 * tables.shape[1], 2 * gains.shape[2], dtype=F32)}
    return call(pack_small_kernel, "pack_small", ins, outs, {}, after).small


def table_sums(grads, onehot, width_c, after=()):
    heads = grads[0].shape[0]
    rows = heads + -heads % 16
    ins = numbered("grad", VMEM, grads) | {"onehot": (VMEM, onehot)}
    scratch = {"wide": pltpu.VMEM((rows, width_c), F32)}
    outs = {"out": shape_of(rows, width_c)}
    return call(table_sums_kernel, "table_sums", ins, outs, scratch, after).out


def params(own, other, heads):
    width_c = own.shape[1]
    ins = {"own": (VMEM, own), "other": (VMEM, other)}
    outs = {"gains": shape_of(2, 2, width_c, dtype=F32), "table": shape_of(2, heads, TABLE, dtype=F32)}
    return call(params_kernel, "params", ins, outs, {})


def grid_ins(grid, edges=()):
    ins = {"own": (VMEM, grid)}
    if edges:
        ins |= {n: (VMEM, e) for n, e in zip(("rows_in", "cols_in", "corner_in"), edges)}
    return ins


def edge_outs(width, width_c):
    return {
        "rows": shape_of(2, SHIFT, width, width_c),
        "cols": shape_of(2, WIN, SHIFT, width_c),
        "corner": shape_of(2, SHIFT, SHIFT, width_c),
    }


def attend_forward(layer, mode, grid, edges, gains, bias, same, weights, parts, after=()):
    width, width_c = grid.shape[1:]
    tokens = width // WIN * SLOT
    heads = width_c // HEAD
    more, scratch = attend_weights(weights, parts)
    ins = {"gains": (VMEM, gains), "bias": (VMEM, bias)}
    ins |= grid_ins(grid, edges) | more
    if mode != "plain":
        ins |= {"same": (VMEM, same)}
    outs = {
        "x": shape_of(tokens, width_c),
        "middle": shape_of(tokens, width_c, dtype=F32),
        "query_t": shape_of(width_c, tokens),
        "keys_t": shape_of(width_c, tokens),
        "keys": shape_of(tokens, width_c),
        "values": shape_of(tokens, width_c),
        "mixed_t": shape_of(width_c, tokens),
        "probs": shape_of(heads, SLOT, tokens, dtype=F32),
    }
    scratch |= {
        "flat": pltpu.VMEM((tokens, width_c), F32),
        "values_t": pltpu.VMEM((width_c, tokens), BF16),
    }
    kernel = functools.partial(attend_forward_kernel, layer, mode)
    return call(kernel, "attend_forward", ins, outs, scratch, after, 4)


def mlp_forward(layer, middle, gains, weights, parts, top, after=()):
    tokens, width_c = middle.shape
    width = top.shape[1]
    more, scratch = mlp_weights(weights, parts)
    ins = {"middle": (VMEM, middle), "gains": (VMEM, gains)} | more
    ins |= {"top": (VMEM, top)}
    outs = {"grid": shape_of(WIN, width, width_c)} | edge_outs(width, width_c)
    scratch |= {
        "flat": pltpu.VMEM((tokens, width_c), F32),
        "buffer": grid_buffer(width, width_c),
    }
    return call(functools.partial(mlp_forward_kernel, layer), "mlp_forward", ins, outs, scratch, after, 4)


def backward(layer, kept, grid, edges, gains, weights, a_parts, m_parts, after=()):
    tokens, width_c = kept.middle.shape
    width = grid.shape[1]
    heads = width_c // HEAD
    second = layer == 1
    attend_ins, attend_scratch = attend_weights(weights, a_parts)
    mlp_ins, mlp_scratch = mlp_weights(weights, m_parts)
    ins = {"gains": (VMEM, gains)} | grid_ins(grid, edges)
    if second:
        ins["own_two"] = ins.pop("own")
    names = ("middle", "x", "query_t", "keys_t", "values", "probs")
    ins |= {name: (VMEM, getattr(kept, name)) for name in names} | attend_ins | mlp_ins
    pieces = shape_of(2, 2, 2 if second else 3, 4, width_c // 8, width_c)
    outs = {
        "keep": pieces,
        "send": pieces,
        "grad_m": shape_of(tokens, width_c, dtype=F32),
        "grad_t": shape_of(3 * width_c, tokens),
        "bias_grad": shape_of(heads, SLOT, PAIR, dtype=F32),
    }
    scratch = attend_scratch | mlp_scratch
    scratch |= {
        "out_t": pltpu.VMEM((width_c, tokens), BF16),
        "flat": pltpu.VMEM((tokens, width_c), F32),
    }
    if second:
        outs |= {"out": shape_of(WIN, width, width_c), "grid": shape_of(WIN, width, width_c)}
        outs |= edge_outs(width, width_c)
        scratch |= {"buffer": grid_buffer(width, width_c)}
    else:
        ins |= {"mixed_t": (VMEM, kept.mixed_t)}
        scratch |= sides(width_c, tokens)

    def kernel(r):
        mlp_backward_kernel(layer, "in" if second else "out", layer, r)
        attend_backward_kernel(layer, "si" if second else "sw", 2, r)

    return call(kernel, "backward", ins, outs, scratch, after, 15)


def sides(width_c, tokens):
    return {
        "left": pltpu.VMEM((2, width_c, tokens), BF16),
        "right": pltpu.VMEM((4 * width_c, tokens), BF16),
    }


def attend_weight_grads(layer, kept, back, gains, after=()):
    tokens, width_c = back.grad_m.shape
    ins = {"gains": (VMEM, gains), "grad_m": (VMEM, back.grad_m)}
    ins |= {"x": (VMEM, kept.x), "mixed_t": (VMEM, kept.mixed_t), "grad_t": (VMEM, back.grad_t)}
    pieces = shape_of(2, 2, 1, 4, width_c // 8, width_c)
    kernel = functools.partial(attend_backward_kernel, layer, "w", 0)
    outs = {"keep": pieces, "send": pieces}
    return call(kernel, "attend_weight_grads", ins, outs, sides(width_c, tokens), after, 2)


def input_grad(layer, kept, back, gains, weights, a_parts, own_two, edges, after=()):
    tokens, width_c = back.grad_m.shape
    width = own_two.shape[1]
    more, scratch = attend_weights(weights, a_parts)
    ins = {"gains": (VMEM, gains), "grad_m": (VMEM, back.grad_m)}
    ins |= {"x": (VMEM, kept.x), "grad_t": (VMEM, back.grad_t)} | more
    ins |= grid_ins(own_two, edges)
    ins["own_two"] = ins.pop("own")
    outs = {"grid": shape_of(WIN, width, width_c), "mixed": shape_of(WIN, width, width_c)}
    scratch |= {
        "flat": pltpu.VMEM((tokens, width_c), F32),
        "buffer": grid_buffer(width, width_c),
    }

    def kernel(r):
        attend_backward_kernel(layer, "i", 0, r)
        roll_out_kernel(r)

    return call(kernel, "input_grad", ins, outs, scratch, after, 3)


def collect(layer, pieces, weights, gains, into=()):
    names = ("qkv", "proj", "up", "down", "gains_grad")
    grads = [shape_of(*w.shape, dtype=F32) for w in (*weights, gains)]
    arrays = [*pieces, weights[0], weights[2], gains]
    ins = [*["all" + str(i) for i in range(len(pieces))], "w_qkv", "w_up", "gains"]
    scratch = {
        "table": pltpu.VMEM((2, 2, 4, 3, pieces[0].shape[1] // 3, pieces[0].shape[2]), BF16),
        "wide": pltpu.VMEM((256, 128), F32),
    }
    order = ins + [None] * len(into) + list(names) + list(scratch)

    def body(*refs):
        named = {n: r for n, r in zip(order, refs) if n}
        collect_kernel(layer, types.SimpleNamespace(place=place_here(), **named))

    return pl.pallas_call(
        body,
        name="collect",
        grid=(1,),
        out_shape=grads,
        in_specs=[VMEM] * len(arrays) + [ANY] * len(into),
        out_specs=[pl.BlockSpec((1, *g.shape[1:]), lambda i: (layer, 0, 0)) for g in grads],
        scratch_shapes=list(scratch.values()),
        input_output_aliases={len(arrays) + i: i for i in range(len(into))},
        compiler_params=pltpu.CompilerParams(vmem_limit_bytes=VMEM_LIMIT),
    )(*arrays, *into)


def same_label(labels):
    same = labels[:, :, None] == labels[:, None, :]
    return same.astype(F32).transpose(1, 0, 2).reshape(SLOT, -1)


def per_device(
    tokens, norm_gains, w_qkv, w_proj, w_up, w_down, tables, region_ids, rel_index, cotangent
):
    y = lax.axis_index("fsdp")
    width, width_c = tokens.shape[1:]
    weights = (w_qkv, w_proj, w_up, w_down)

    heads = 2 * tables.shape[1]

    piece = pack(0, weights)
    small = pack_small(norm_gains, tables, after=(piece.attend,))
    settings = params(small, exchange(small, 0, 1), heads)
    gains = settings.gains
    attend_one = share_halves(piece.attend)
    mlp_piece = tie(piece.mlp, (small,))
    index = rel_index.reshape(WIN, WIN, WIN, WIN)
    index = jnp.pad(index, [(0, 1)] * 4, constant_values=-1).reshape(SLOT, SLOT).T
    index = jnp.concatenate([index, index], axis=1)
    onehot = (index[:, :, None] == jnp.arange(TABLE, dtype=jnp.int32)).astype(BF16)
    bias = jnp.einsum(
        "lht,jit->lhji", settings.table.astype(BF16), onehot, preferred_element_type=F32
    )
    labels = region_ids.reshape(WIN, width // WIN, WIN).transpose(1, 0, 2)
    labels = jnp.pad(labels, [(0, 0), (0, 1), (0, 1)], constant_values=-1)
    same = same_label(labels.reshape(-1, SLOT))
    piece = pack(1, weights, after=(gains, bias, same))
    one = attend_forward(
        0, "plain", tokens, (), gains, bias, None, weights, attend_one, after=(piece.both,)
    )
    mlp_one = share_halves(mlp_piece, after=(one.middle,))
    done = mlp_forward(0, one.middle, gains, weights, mlp_one, cotangent)
    edges = halo(done.rows, done.cols, done.corner, 1)
    parts_two = share_halves(piece.both, after=edges)
    two = attend_forward(
        1, "in", done.grid, edges, gains, bias, same, weights, parts_two
    )
    back2 = backward(1, two, cotangent, edges, gains, weights, parts_two, parts_two)
    got_m2 = exchange(back2.send, 1, 0)
    edges = halo(back2.rows, back2.cols, back2.corner, -1)
    att2 = attend_weight_grads(1, two, back2, gains)
    side_two = start_side(
        (back2.keep, att2.keep), (got_m2, exchange(att2.send, 1, 0)), after=edges
    )
    back1 = backward(
        0, one, back2.grid, edges, gains, weights, attend_one, mlp_one, after=(side_two[0],)
    )
    face_two = start_face(side_two, after=(back1.grad_m,))
    rows = width_c // 8
    small = table_sums((back1.bias_grad, back2.bias_grad), onehot, width_c, after=face_two[:1])
    cube_one = start_cube(
        back1.keep, exchange(tie(back1.send, face_two[:1]), 1, 0), (small, exchange(small, 1, 0))
    )
    last = input_grad(
        0, one, back1, gains, weights, attend_one, back2.out, edges, after=cube_one[:1]
    )
    total_two = finish_sum(face_two, rows, after=(last.mixed,))
    total_one = finish_sum(cube_one, rows, after=(total_two,))
    all_two = gather(total_two, 3 * rows)
    all_one = gather(total_one, 3 * rows, after=all_two[:1])
    sums = collect(1, all_two, weights, norm_gains)
    sums = collect(0, all_one, weights, norm_gains, into=sums)
    small = total_one[3 * rows : 3 * rows + heads].astype(F32).reshape(heads, 2, width_c // 2)
    small = small[:, :, :TABLE].transpose(1, 0, 2)
    tables_grad = lax.dynamic_slice_in_dim(small, y * (heads // 2), heads // 2, axis=1)
    return (last.mixed, last.grid, sums[4], *sums[:4], tables_grad)


def solution(mesh):
    return jax.shard_map(
        per_device,
        mesh=mesh,
        in_specs=(
            P("seq", "fsdp", None),
            P(None, None, "fsdp"),
            P(None, "fsdp", None),
            P(None, "fsdp", None),
            P(None, "fsdp", None),
            P(None, "fsdp", None),
            P(None, "fsdp", None),
            P("seq", "fsdp"),
            P(),
            P("seq", "fsdp", None),
        ),
        out_specs=(
            P("seq", "fsdp", None),
            P("seq", "fsdp", None),
            P(None, None, "fsdp"),
            P(None, "fsdp", None),
            P(None, "fsdp", None),
            P(None, "fsdp", None),
            P(None, "fsdp", None),
            P(None, "fsdp", None),
        ),
        check_vma=False,
    )
```

```python
import functools
import types

import jax
import jax.numpy as jnp
from jax import lax
from jax.experimental import pallas as pl
from jax.experimental.pallas import tpu as pltpu
from jax.sharding import PartitionSpec as P

WIN = 7
SHIFT = 3
TABLE = 169
SIDE = 8
SLOT = SIDE * SIDE
HEAD = 32
PAIR = 2 * SLOT
EPSILON = 1e-05
MASKED_SCORE = -1000000000.0
F32 = jnp.float32
BF16 = jnp.bfloat16
VMEM_LIMIT = 24 * 1024 * 1024
PACK_VMEM_LIMIT = 60 * 1024 * 1024
BYTES_PER_US = 3500000


def exchange(array, ds, dy):
    n, m = lax.axis_size("seq"), lax.axis_size("fsdp")
    pairs = [(s * m + y, (s ^ ds) * m + (y ^ dy)) for s in range(n) for y in range(m)]
    return lax.ppermute(array, ("seq", "fsdp"), pairs)


def take_from(array, ds, dy):
    n, m = lax.axis_size("seq"), lax.axis_size("fsdp")
    pairs = [((s + ds) % n * m + (y + dy) % m, s * m + y) for s in range(n) for y in range(m)]
    return lax.ppermute(array, ("seq", "fsdp"), pairs)


def halo(near_rows, near_cols, corner, step):
    return (
        take_from(near_rows, step, 0),
        take_from(near_cols, 0, step),
        take_from(corner, step, step),
    )


def share_halves(piece, after=()):
    first = exchange(piece, 0, 1)
    if after:
        first = tie(first, after)
    return (first, exchange(first, 1, 0))


def add(*terms):
    total = terms[0].astype(F32)
    for term in terms[1:]:
        total = total + term.astype(F32)
    return total


def sum_higher(value):
    step = 16
    while step < lax.axis_size("seq"):
        value = add(value, exchange(value, step, 0)).astype(value.dtype)
        step *= 2
    return value


def start_side(keeps, gots, after=(), small=()):
    kinds = sum(keep.shape[2] for keep in keeps)
    out = shape_of(2, kinds, *keeps[0].shape[3:])
    ins = numbered("keep", VMEM, keeps) | numbered("got", VMEM, gots) | numbered("small", VMEM, small)
    outs = {"own": out, "other": out} | small_out(small)
    r = call(add_side_kernel, "add_side", ins, outs, {}, after)
    parts = (r.own, exchange(r.other, 0, 1))
    return (parts, (r.total, exchange(r.total, 0, 1))) if small else parts


def small_out(small):
    return {"total": shape_of(*small[0].shape)} if small else {}


def start_face(parts, after=(), small=()):
    _, kinds, _, rows, cols = parts[0].shape
    extra = small[0].shape[0] if small else 0
    out = shape_of(kinds * 2 * rows + extra, cols)
    ins = numbered("part", VMEM, parts) | numbered("small", VMEM, small)
    outs = {"out" + str(i): out for i in range(4)}
    r = call(add_face_kernel, "add_face", ins, outs, {}, after)
    return r.out0, exchange(r.out3, 6, 0), exchange(r.out2, 2, 0), exchange(r.out1, 4, 0)


def finish_sum(parts, rows, after=()):
    kinds = parts[0].shape[0] // (2 * rows)
    out = shape_of(parts[0].shape[0] - kinds * rows, parts[0].shape[1])
    kernel = functools.partial(halve_kernel, kinds, rows)
    ins = numbered("part", VMEM, parts)
    r = call(kernel, "halve", ins, {"own": out, "other": out}, {}, after)
    got = exchange(r.other, 8, 0)
    ins = {"part0": (VMEM, r.own), "part1": (VMEM, got)}
    total = call(add_all_kernel, "add_all", ins, {"out": out}, {}).out
    return sum_higher(total), got


def gather_pair(total, rows, after=()):
    ins = {"own": (VMEM, total), "other": (VMEM, exchange(total, 8, 0))}
    out = shape_of(2, rows, total.shape[1])
    return call(stack_kernel, "stack", ins, {"out": out}, {}, after).out


def gather(pair, after=()):
    here = [pair, exchange(pair, 4, 0), exchange(pair, 2, 0), exchange(pair, 6, 0)]
    if after:
        here = [tie(part, after) for part in here]
    return here + [exchange(part, 1, 0) for part in here]


def flip(index, bits):
    return jnp.bitwise_xor(index, bits)


def pack_kernel(layer, r):
    core = r.place[0]
    width_c = r.proj.shape[2]
    rows = r.qkv.shape[1] // 2
    if layer == 0:
        attend, mlp = r.attend.at[:rows], r.mlp
    else:
        attend, mlp = r.both.at[:rows], r.both.at[rows:]
    start = pl.multiple_of(core * rows, 16)
    pairs = [
        (r.qkv.at[layer, pl.ds(start, rows), :], attend.at[:, : 3 * width_c]),
        (r.proj.at[layer, pl.ds(start, rows), :], attend.at[:, 3 * width_c :]),
        (r.up.at[layer, pl.ds(start, rows), :], mlp.at[:rows]),
    ]
    for index in range(4):
        first = pl.multiple_of((core * 4 + index) * rows, 16)
        cols = slice(index * width_c, (index + 1) * width_c)
        pairs.append((r.down.at[layer, pl.ds(first, rows), :], mlp.at[rows:, cols]))
    copies = start_copies(pairs, r.sems)
    if layer == 0:
        wait_all(start_copies([(r.tables, r.tables_v), (r.gains, r.gains_v)], r.small_sems))
        r.small[...] = jnp.zeros_like(r.small)
        heads = r.tables.shape[1]
        half = r.gains.shape[2]
        for index in range(2):
            r.small[index * heads : (index + 1) * heads, :TABLE] = r.tables_v[index].astype(F32)
            r.small[2 * index : 2 * index + 2, 256 : 256 + half] = r.gains_v[index].astype(F32)
        r.attend[rows:] = r.small[...].astype(BF16)
    wait_all(copies)


def chosen(index, key):
    line = jnp.broadcast_to(index[key : key + 1, :], (TABLE, index.shape[1]))
    entries = lax.broadcasted_iota(jnp.int32, line.shape, 0)
    return jnp.where(line == entries, 1.0, 0.0).astype(BF16)


def table_sums_kernel(r):
    heads = r.grad0.shape[0]
    total = jnp.zeros((2 * heads, TABLE), F32)
    for key in range(SLOT):
        pair = jnp.concatenate([r.grad0[:, key, :], r.grad1[:, key, :]], axis=0)
        total = total + mm_nt(pair.astype(BF16), chosen(r.index, key))
    r.wide[...] = jnp.zeros_like(r.wide)
    half = r.out.shape[1] // 2
    r.wide[:heads, :TABLE] = total[:heads]
    r.wide[:heads, half : half + TABLE] = total[heads:]
    r.out[...] = r.wide[...].astype(BF16)


def slots(rows, count):
    row = jnp.bitwise_and(lax.broadcasted_iota(jnp.int32, (rows, count), 0), SLOT - 1)
    token = lax.broadcasted_iota(jnp.int32, (rows, count), 1)
    at = token
    for side in range(1, WIN):
        at = at + jnp.where(token >= side * WIN, 1, 0)
    return jnp.where(row == at, 1.0, 0.0).astype(BF16)


def is_token(shape, axis):
    place = jnp.bitwise_and(lax.broadcasted_iota(jnp.int32, shape, axis), SLOT - 1)
    return (place < WIN * SIDE) & (jnp.bitwise_and(place, SIDE - 1) < WIN)


def spread_index(rel):
    count = rel.shape[0]
    keys = mm_nt(slots(SLOT, count), rel.astype(F32).astype(BF16))
    pairs = mm_nt(keys.astype(BF16), slots(PAIR, count))
    real = is_token(pairs.shape, 0) & is_token(pairs.shape, 1)
    return jnp.where(real, (pairs + 0.5).astype(jnp.int32), -1)


def same_label(r):
    r.labels[...] = jnp.full_like(r.labels, -1.0)
    for window in range(r.region.shape[1] // WIN):
        r.labels[:WIN, :WIN] = r.region[:, window * WIN : window * WIN + WIN].astype(F32)
        block = r.labels[:, :SIDE].astype(BF16)
        lane = lax.broadcasted_iota(jnp.int32, (SIDE, SLOT), 1)
        row = lax.broadcasted_iota(jnp.int32, (SIDE, SLOT), 0)
        repeat = jnp.where(jnp.bitwise_and(lane, SIDE - 1) == row, 1.0, 0.0).astype(BF16)
        own = (lane >= row * SIDE) & (lane < row * SIDE + SIDE)
        line = jnp.sum(jnp.where(own, mm(block, repeat), 0.0), 0, keepdims=True)
        wide = jnp.broadcast_to(line, (SLOT, SLOT))
        diagonal_only = lax.broadcasted_iota(jnp.int32, wide.shape, 0) == (
            lax.broadcasted_iota(jnp.int32, wide.shape, 1)
        )
        column = jnp.sum(jnp.where(diagonal_only, wide, 0.0), 1, keepdims=True)
        r.same[:, window * SLOT : window * SLOT + SLOT] = jnp.where(wide == column, 1.0, 0.0)


def params_kernel(r):
    half = r.gains.shape[2] // 2
    heads = r.bias.shape[1] // 2
    rows = r.own.shape[0] - r.extra.shape[0]
    flipped = r.place[3] == 1
    r.extra[...] = jnp.where(flipped, r.other[rows:].astype(F32), r.own[rows:].astype(F32))
    for part in range(2):
        for index in range(2):
            r.gains[index, :, part * half : (part + 1) * half] = r.extra[
                2 * index : 2 * index + 2, 256 : 256 + half
            ]
            start = (2 * index + part) * heads
            r.table[start : start + heads, :] = r.extra[index * heads : (index + 1) * heads, :TABLE]
        if part == 0:
            r.extra[...] = jnp.where(
                flipped, r.own[rows:].astype(F32), r.other[rows:].astype(F32)
            )
    r.index[...] = spread_index(r.rel[...])
    table = r.table[...].astype(BF16)
    for key in range(SLOT):
        line = mm(table, chosen(r.index, key))
        r.bias[0, :, key, :] = line[: 2 * heads]
        r.bias[1, :, key, :] = line[2 * heads :]


def start_copies(pairs, sems):
    copies = [
        pltpu.make_async_copy(source, target, sems.at[index])
        for index, (source, target) in enumerate(pairs)
    ]
    for copy in copies:
        copy.start()
    return copies


def fetch(place, layer, own, parts, pick, full, sems):
    half = full.shape[0] // 2
    rows = half // len(parts)
    y = place[3]
    pairs = [(own.at[layer], full.at[pl.ds(pl.multiple_of(y * half, 16), half)])]
    for spot, part in zip((place[0], flip(place[0], 1)), parts):
        pieces = pick(part)
        count = rows // len(pieces)
        for index, piece in enumerate(pieces):
            start = pl.multiple_of((1 - y) * half + spot * rows + index * count, 16)
            pairs.append((piece, full.at[pl.ds(start, count)]))
    return start_copies(pairs, sems)


def fetch_attend(place, layer, own, parts, qkv_w, proj_w, sems):
    rows = own[0].shape[1] // 2
    wide = qkv_w.shape[1]

    def qkv(part):
        return [part.at[:rows, :wide]]

    def proj(part):
        return [part.at[:rows, wide:]]

    return (
        fetch(place, layer, own[0], parts, qkv, qkv_w, sems.at[0]),
        fetch(place, layer, own[1], parts, proj, proj_w, sems.at[1]),
    )


def fetch_mlp(place, layer, own, parts, up_w, down_w, sems):
    rows = own[0].shape[1] // 2
    first = parts[0].shape[0] - 2 * rows
    width_c = up_w.shape[0]

    def up(part):
        return [part.at[first : first + rows]]

    def down(part):
        return [part.at[first + rows :, i * width_c : (i + 1) * width_c] for i in range(4)]

    copies = [fetch(place, layer, own[0], parts, up, up_w, sems.at[0])]
    if down_w is not None:
        copies.append(fetch(place, layer, own[1], parts, down, down_w, sems.at[1]))
    return copies


def add_refs(refs):
    total = refs[0][...].astype(F32)
    for ref in refs[1:]:
        total = total + ref[...].astype(F32)
    return total


def add_small(r):
    return add_refs(listed(r, "small")).astype(BF16)


def kinds_of(refs):
    return [(ref, kind) for ref in refs for kind in range(ref.shape[2])]


def add_side_kernel(r):
    pairs = zip(kinds_of(listed(r, "keep")), kinds_of(listed(r, "got")))
    for index, ((keep, first), (got, second)) in enumerate(pairs):
        for y, out in enumerate((r.own, r.other)):
            for x in range(2):
                value = keep[y, x, first].astype(F32) + got[y, x, second].astype(F32)
                out[x, index] = value.astype(BF16)
    if hasattr(r, "total"):
        r.total[...] = add_small(r)


def add_face_kernel(r):
    _, kinds, _, rows, _ = r.part0.shape
    for index, out in enumerate(listed(r, "out")):
        x, z = index >> 1, index & 1
        for kind in range(kinds):
            for high in range(2):
                at = (x, kind, 2 * high + z)
                first = (kind * 2 + high) * rows
                value = r.part0[at].astype(F32) + r.part1[at].astype(F32)
                out[first : first + rows, :] = value.astype(BF16)
        if hasattr(r, "small0"):
            out[kinds * 2 * rows :, :] = add_small(r)


def halve_kernel(kinds, rows, r):
    parts = listed(r, "part")
    for high, out in enumerate((r.own, r.other)):
        for kind in range(kinds):
            first = (kind * 2 + high) * rows
            value = add_refs([part.at[first : first + rows, :] for part in parts])
            out[kind * rows : (kind + 1) * rows, :] = value.astype(BF16)
        if out.shape[0] > kinds * rows:
            value = add_refs([part.at[kinds * 2 * rows :, :] for part in parts])
            out[kinds * rows :, :] = value.astype(BF16)


def add_all_kernel(r):
    r.out[...] = add_refs(listed(r, "part")).astype(BF16)


def stack_kernel(r):
    rows = r.out.shape[1]
    r.out[0] = r.own[:rows, :]
    r.out[1] = r.other[:rows, :]


def wait_all(copies):
    for copy in copies:
        copy.wait()


def row_segments(mode, refs, row, width):
    if mode == "plain":
        return [(0, refs[0][row], 0, width)]
    own, rows, cols, corner = refs
    rest = width - SHIFT
    if mode == "in":
        if row < WIN - SHIFT:
            return [
                (0, own[row + SHIFT], SHIFT, rest),
                (rest, cols[row + SHIFT], 0, SHIFT),
            ]
        at = row - (WIN - SHIFT)
        return [(0, rows[at], SHIFT, rest), (rest, corner[at], 0, SHIFT)]
    if row >= SHIFT:
        return [(0, cols[row - SHIFT], 0, SHIFT), (SHIFT, own[row - SHIFT], 0, rest)]
    return [(0, corner[row], 0, SHIFT), (SHIFT, rows[row], 0, rest)]


def fill_windows(mode, refs, out):
    width = refs[0].shape[1]
    out[...] = jnp.zeros_like(out)
    for row in range(WIN):
        for first, source, start, count in row_segments(mode, refs, row, width):
            source = source.astype(F32)
            for window in range(width // WIN):
                low = max(first, window * WIN)
                high = min(first + count, window * WIN + WIN)
                if low < high:
                    spot = window * SLOT + row * SIDE + low - window * WIN
                    begin = start + low - first
                    out[spot : spot + high - low, :] = source[begin : begin + high - low, :]


def fill_grid(source, buffer, width):
    for row in range(WIN):
        for window in range(width // WIN):
            spot = window * SLOT + row * SIDE
            buffer[row, window * WIN : window * WIN + WIN, :] = source[spot : spot + WIN, :]


def normalize(values):
    centred = values - jnp.mean(values, -1, keepdims=True)
    factor = lax.rsqrt(jnp.mean(centred * centred, -1, keepdims=True) + EPSILON)
    return centred * factor, factor


def normalize_back(grad_norm, normed, factor):
    spread = jnp.mean(grad_norm * normed, -1, keepdims=True)
    return factor * (grad_norm - jnp.mean(grad_norm, -1, keepdims=True) - normed * spread)


def mm(left, right):
    return lax.dot_general(left, right, (((1,), (0,)), ((), ())), preferred_element_type=F32)


def mm_nt(left, right):
    return lax.dot_general(left, right, (((1,), (1,)), ((), ())), preferred_element_type=F32)


def only_head(group, which):
    rows = lax.broadcasted_iota(jnp.int32, group.shape, 0)
    inside = (rows >= which * HEAD) & (rows < (which + 1) * HEAD)
    return jnp.where(inside, group, jnp.zeros_like(group))


def diagonal(block):
    lanes = lax.broadcasted_iota(jnp.int32, (SLOT, PAIR), 1)
    return jnp.where(lanes < SLOT, block[:SLOT], block[SLOT:])


def spread_diagonal(packed):
    lanes = lax.broadcasted_iota(jnp.int32, (SLOT, PAIR), 1)
    low = jnp.where(lanes < SLOT, packed, 0.0)
    high = jnp.where(lanes < SLOT, 0.0, packed)
    return jnp.concatenate([low, high], axis=0).astype(BF16)


def target(r, apart, kind):
    if not apart:
        return r.keep, kind
    if hasattr(r, "send"):
        return r.send, kind
    return listed(r, "send")[kind], 0


def store_columns(r, apart, x, kind, value):
    rows = value.shape[0] // 8
    out, kind = target(r, apart, kind)
    value = value.astype(BF16)
    for y in range(2):
        for z in range(4):
            first = (y * 4 + z) * rows
            at = (flip(r.place[3], y), flip(r.place[1], x), kind, flip(r.place[2], z))
            out[at] = value[first : first + rows]


def store_rows(r, apart, y, kind, value):
    rows = value.shape[0] // 8
    out, kind = target(r, apart, kind)
    value = value.astype(BF16)
    for x in range(2):
        for z in range(4):
            first = (x * 4 + z) * rows
            at = (flip(r.place[3], y), flip(r.place[1], x), kind, flip(r.place[2], z))
            out[at] = value[first : first + rows]


def grid_refs(r, which):
    if not hasattr(r, "rows_in"):
        return [r.own]
    return [r.own if which == 0 else r.own_two] + [
        edge.at[which] for edge in (r.rows_in, r.cols_in, r.corner_in)
    ]


def attend_forward_kernel(layer, mode, r):
    width_c = r.flat.shape[1]
    heads = width_c // HEAD
    copies = fetch_attend(
        r.place, layer, (r.qkv, r.proj), listed(r, "a_part"), r.qkv_w, r.proj_w, r.a_sems
    )
    fill_windows(mode, grid_refs(r, 0), r.flat)
    r.x[...] = r.flat[...].astype(BF16)
    normed, _ = normalize(r.flat[...])
    hidden = (normed * r.gains[layer, 0:1, :]).astype(BF16)
    wait_all(copies[0])
    query = (mm(hidden, r.qkv_w[:, :width_c]) * HEAD ** (-0.5)).astype(BF16)
    r.query_t[...] = query.T
    r.keys[...] = mm(hidden, r.qkv_w[:, width_c : 2 * width_c]).astype(BF16)
    r.keys_t[...] = r.keys[...].T
    r.values[...] = mm(hidden, r.qkv_w[:, 2 * width_c :]).astype(BF16)
    r.values_t[...] = r.values[...].T
    if mode == "plain":
        meet = is_token((SLOT, PAIR), 0)
    else:
        same_label(r)
    for head in range(heads):
        group = slice(head // 4 * 128, head // 4 * 128 + 128)
        rows = slice(head * HEAD, head * HEAD + HEAD)
        for pair in range(r.flat.shape[0] // PAIR):
            span = slice(pair * PAIR, pair * PAIR + PAIR)
            raw = mm(r.keys[span, group], only_head(r.query_t[group, span], head % 4))
            if mode != "plain":
                meet = r.same[:, span] > 0.5
            scores = jnp.where(meet, diagonal(raw) + r.bias[layer, head], MASKED_SCORE)
            weighted = jnp.exp(scores - jnp.max(scores, 0, keepdims=True))
            attention = weighted / jnp.sum(weighted, 0, keepdims=True)
            r.probs[head, :, span] = attention
            r.mixed_t[rows, span] = mm(r.values_t[rows, span], spread_diagonal(attention)).astype(
                BF16
            )
    wait_all(copies[1])
    r.middle[...] = r.flat[...] + mm(r.mixed_t[...].T, r.proj_w[...])


def attend_backward_kernel(layer, parts, kind, r):
    width_c = r.x.shape[1]
    heads = width_c // HEAD
    if "s" in parts or "i" in parts:
        copies = fetch_attend(
            r.place, layer, (r.qkv, r.proj), listed(r, "a_part"), r.qkv_w, r.proj_w, r.a_sems
        )
    normed, factor = normalize(r.x[...].astype(F32))
    gain = r.gains[layer, 0:1, :]
    attended = r.grad_m[...].astype(BF16)
    if "s" in parts:
        wait_all(copies[1])
        r.out_t[...] = mm_nt(r.proj_w[...], attended).astype(BF16)
        for head in range(heads):
            group = slice(head // 4 * 128, head // 4 * 128 + 128)
            rows = slice(head * HEAD, head * HEAD + HEAD)
            row_k = slice(width_c + head * HEAD, width_c + head * HEAD + HEAD)
            row_v = slice(2 * width_c + head * HEAD, 2 * width_c + head * HEAD + HEAD)
            total = jnp.zeros((SLOT, PAIR), F32)
            for pair in range(r.x.shape[0] // PAIR):
                span = slice(pair * PAIR, pair * PAIR + PAIR)
                attention = r.probs[head, :, span]
                grad_p = diagonal(
                    mm(r.values[span, group], only_head(r.out_t[group, span], head % 4))
                )
                grad_s = attention * (grad_p - jnp.sum(grad_p * attention, 0, keepdims=True))
                total = total + grad_s
                spread_p = spread_diagonal(attention)
                spread_s = spread_diagonal(grad_s)
                grad_q = mm(r.keys_t[rows, span], spread_s) * HEAD ** (-0.5)
                r.grad_t[rows, span] = grad_q.astype(BF16)
                r.grad_t[row_k, span] = mm_nt(r.query_t[rows, span], spread_s).astype(BF16)
                r.grad_t[row_v, span] = mm_nt(r.out_t[rows, span], spread_p).astype(BF16)
            r.bias_grad[head] = total
    if "w" in parts:
        r.left[0] = (normed * gain).astype(BF16).T
        r.left[1] = r.mixed_t[...]
        r.right[: 3 * width_c, :] = r.grad_t[...]
        r.right[3 * width_c :, :] = attended.T
        for apart in (1, 0):
            for x in range(2):
                chunk = 2 * flip(r.place[0], apart) + x
                left = r.left[(chunk == 3).astype(jnp.int32)]
                right = r.right[pl.ds(pl.multiple_of(chunk * width_c, 128), width_c), :]
                store_columns(r, apart, x, kind, mm_nt(left, right))
    if "s" in parts or "i" in parts:
        if "s" not in parts:
            wait_all(copies[1])
        wait_all(copies[0])
    if "i" in parts:
        grad_hidden = mm(r.qkv_w[...], r.grad_t[...]).T
        r.flat[...] = r.grad_m[...] + normalize_back(grad_hidden * gain, normed, factor)
        width = r.grid.shape[1]
        fill_grid(r.flat, r.buffer, width)
        r.grid[...] = r.buffer[:, :width, :].astype(BF16)
        if hasattr(r, "rows"):
            r.rows[0] = r.buffer[WIN - SHIFT :, :width, :].astype(BF16)
            r.cols[0] = r.buffer[:, width - SHIFT : width, :].astype(BF16)
            r.corner[0] = r.buffer[WIN - SHIFT :, width - SHIFT : width, :].astype(BF16)


GELU_A = 0.7978845608028654
GELU_B = 0.044715


def gelu_parts(inner):
    square = inner * inner
    tanh = jnp.tanh(GELU_A * (inner * (1.0 + GELU_B * square)))
    return square, tanh


def mlp_forward_kernel(layer, r):
    width_c = r.flat.shape[1]
    copies = fetch_mlp(
        r.place, layer, (r.up, r.down), listed(r, "m_part"), r.up_w, r.down_w, r.m_sems
    )
    normed, _ = normalize(r.middle[...])
    hidden = (normed * r.gains[layer, 1:2, :]).astype(BF16)
    output = r.middle[...]
    wait_all(copies[0])
    wait_all(copies[1])
    for chunk in range(r.up_w.shape[1] // width_c):
        cols = slice(chunk * width_c, (chunk + 1) * width_c)
        inner = mm(hidden, r.up_w[:, cols])
        _, tanh = gelu_parts(inner)
        output = output + mm((0.5 * inner * (1.0 + tanh)).astype(BF16), r.down_w[cols, :])
    r.flat[...] = output
    width = r.grid.shape[1]
    fill_grid(r.flat, r.buffer, width)
    r.grid[...] = r.buffer[:, :width, :].astype(BF16)
    r.rows[0] = r.buffer[:SHIFT, :width, :].astype(BF16)
    r.cols[0] = r.buffer[:, :SHIFT, :].astype(BF16)
    r.corner[0] = r.buffer[:SHIFT, :SHIFT, :].astype(BF16)
    r.rows[1] = r.top[:SHIFT]
    r.cols[1] = r.top[:, :SHIFT, :]
    r.corner[1] = r.top[:SHIFT, :SHIFT, :]


def activate(hidden, up):
    inner = mm(hidden, up)
    square, tanh = gelu_parts(inner)
    slope = 0.5 * (1.0 + tanh) + (0.5 * GELU_A) * inner * (1.0 - tanh * tanh) * (
        1.0 + 3.0 * GELU_B * square
    )
    return (0.5 * inner * (1.0 + tanh)).astype(BF16), slope


def prepare_kernel(layer, r):
    copies = fetch_mlp(
        r.place, layer, (r.up, None), listed(r, "m_part"), r.up_w, None, r.m_sems
    )
    normed, _ = normalize(r.middle[...])
    hidden = (normed * r.gains[layer, 1:2, :]).astype(BF16)
    r.hidden_t[...] = hidden.T
    wait_all(copies[0])
    width_c = hidden.shape[1]
    for chunk in range(r.up_w.shape[1] // width_c):
        cols = slice(chunk * width_c, (chunk + 1) * width_c)
        activated, slope = activate(hidden, r.up_w[:, cols])
        r.activated_t[cols, :] = activated.T
        r.slope[:, cols] = slope.astype(BF16)


def mlp_backward_kernel(layer, mode, which, r):
    width_c = r.flat.shape[1]
    copies = fetch_mlp(
        r.place, layer, (r.up, r.down), listed(r, "m_part"), r.up_w, r.down_w, r.m_sems
    )
    normed, factor = normalize(r.middle[...])
    gain = r.gains[layer, 1:2, :]
    prepared = hasattr(r, "slope")
    hidden = (normed * gain).astype(BF16)
    hidden_t = r.hidden_t[...] if prepared else hidden.T
    fill_windows(mode, grid_refs(r, which), r.flat)
    grad_low = r.flat[...].astype(BF16)
    forward = hasattr(r, "out")
    output = r.middle[...]
    grad_hidden = jnp.zeros(r.flat.shape, F32)
    wait_all(copies[0])
    wait_all(copies[1])
    for up_apart, down_apart in ((1, 1), (1, 0), (0, 1), (0, 0)):
        high, low = flip(r.place[0], up_apart), flip(r.place[0], down_apart)
        cols = pl.ds(pl.multiple_of((2 * high + low) * width_c, 128), width_c)
        if prepared:
            activated_t, slope = r.activated_t[cols, :], r.slope[:, cols].astype(F32)
        else:
            activated, slope = activate(hidden, r.up_w[:, cols])
            activated_t = activated.T
        if forward:
            output = output + mm(activated, r.down_w[cols, :])
        store_rows(r, down_apart, high, 1, mm(activated_t, grad_low))
        grad_inner = (mm_nt(grad_low, r.down_w[cols, :]) * slope).astype(BF16)
        store_columns(r, up_apart, low, 0, mm(hidden_t, grad_inner))
        grad_hidden = grad_hidden + mm_nt(grad_inner, r.up_w[:, cols])
    r.grad_m[...] = r.flat[...] + normalize_back(grad_hidden * gain, normed, factor)
    if forward:
        r.flat[...] = output
        width = r.out.shape[1]
        fill_grid(r.flat, r.buffer, width)
        r.out[...] = r.buffer[:, :width, :].astype(BF16)
        r.rows[1] = r.buffer[WIN - SHIFT :, :width, :].astype(BF16)
        r.cols[1] = r.buffer[:, width - SHIFT : width, :].astype(BF16)
        r.corner[1] = r.buffer[WIN - SHIFT :, width - SHIFT : width, :].astype(BF16)


def roll_out_kernel(r):
    refs = grid_refs(r, 1)
    width = r.mixed.shape[1]
    for row in range(WIN):
        for first, source, start, count in row_segments("out", refs, row, width):
            r.buffer[row, first : first + count, :] = source.astype(F32)[start : start + count, :]
    r.mixed[...] = r.buffer[:, :width, :].astype(BF16)


def collect_kernel(r):
    rows, cols = r.one0.shape[1] // 3, r.one0.shape[2]
    half = r.attend_f.shape[1]
    loads = start_copies([(r.w_qkv, r.qkv_w), (r.w_up, r.up_w)], r.load_sems)
    stores = []

    def store(value, out):
        copy = pltpu.make_async_copy(value, out, r.out_sems.at[len(stores)])
        copy.start()
        stores.append(copy)

    for layer, name in ((0, "one"), (1, "two")):
        places = []
        for index, ref in enumerate(listed(r, name)):
            core, x, z = flip(r.place[0], index >> 2), flip(r.place[1], index >> 1 & 1), index & 1
            for high in range(2):
                places.append((ref, high, 2 * core + x, flip(r.place[2], 2 * high + z)))
        for ref, high, chunk, z in places:
            first = pl.multiple_of((chunk * 4 + z) * rows, 16)
            r.down_f[layer, pl.ds(first, rows), :] = ref[high, rows : 2 * rows].astype(F32)
        store(r.down_f.at[layer], r.down.at[layer])
        for kind, full in ((0, r.up_f), (2, r.attend_f)):
            for ref, high, chunk, z in places:
                band = pl.ds(pl.multiple_of(z * rows, 16), rows)
                span = pl.ds(pl.multiple_of(chunk * cols, 128), cols)
                piece = ref[high, kind * rows : (kind + 1) * rows]
                full[layer, band, span] = piece.astype(F32)
        store(r.up_f.at[layer], r.up.at[layer])
        store(r.attend_f.at[layer, :, : 3 * cols], r.qkv.at[layer])
        store(r.attend_f.at[layer, :, 3 * cols :], r.proj.at[layer])
    heads = r.tables_grad.shape[1]
    small = r.total[3 * rows :].astype(F32)
    small = jnp.where(r.place[3] == 1, small[heads : 2 * heads], small[:heads])
    r.tables_grad[0] = small[:, :TABLE]
    r.tables_grad[1] = small[:, cols // 2 : cols // 2 + TABLE]
    wait_all(loads)
    r.wide[...] = jnp.zeros_like(r.wide)
    for layer in range(2):
        for which, weight, grad in ((0, r.qkv_w, r.attend_f), (1, r.up_w, r.up_f)):
            total = jnp.zeros((half, 128), F32)
            for first in range(0, weight.shape[2], 128):
                span = slice(first, first + 128)
                total = total + weight[layer, :, span].astype(F32) * grad[layer, :, span]
            r.wide[:half, :] = total
            line = jnp.sum(r.wide[...].T, 0, keepdims=True)[:, :half]
            gain = r.gains[layer, which : which + 1, :].astype(F32)
            r.gains_grad[layer, which : which + 1, :] = line / gain
    wait_all(stores)


VMEM = pl.BlockSpec(memory_space=pltpu.VMEM)
ANY = pl.BlockSpec(memory_space=pl.ANY)
HBM = pl.BlockSpec(memory_space=pltpu.HBM)


def listed(r, name):
    found = []
    while name + str(len(found)) in vars(r):
        found.append(getattr(r, name + str(len(found))))
    return found


def numbered(name, space, arrays):
    return {name + str(index): (space, array) for index, array in enumerate(arrays)}


def place_here():
    seq = lax.axis_index("seq")
    return (
        jnp.bitwise_and(seq, 1),
        jnp.bitwise_and(lax.shift_right_logical(seq, 1), 1),
        jnp.bitwise_and(lax.shift_right_logical(seq, 2), 3),
        lax.axis_index("fsdp"),
    )


def shape_of(*dims, dtype=BF16):
    return jax.ShapeDtypeStruct(dims, dtype)


def call(kernel, name, ins, outs, scratch, after=(), us=1, vmem=VMEM_LIMIT, spaces=None):
    names = list(ins) + [None] * len(after) + list(outs) + list(scratch)

    def body(*refs):
        named = {n: ref for n, ref in zip(names, refs) if n}
        kernel(types.SimpleNamespace(place=place_here(), **named))

    results = pl.pallas_call(
        body,
        name=name,
        out_shape=list(outs.values()),
        in_specs=[space for space, _ in ins.values()] + [ANY] * len(after),
        out_specs=spaces or [VMEM] * len(outs),
        scratch_shapes=list(scratch.values()),
        cost_estimate=pl.CostEstimate(
            flops=1000, bytes_accessed=us * BYTES_PER_US, transcendentals=0
        ),
        compiler_params=pltpu.CompilerParams(vmem_limit_bytes=vmem),
    )(*[array for _, array in ins.values()], *after)
    return types.SimpleNamespace(**dict(zip(outs, results)))


def weight_scratch(first, second, names):
    return {
        names[0]: pltpu.VMEM((2 * first.shape[1], first.shape[2]), BF16),
        names[1]: pltpu.VMEM((2 * second.shape[1], second.shape[2]), BF16),
        names[2]: pltpu.SemaphoreType.DMA((2, 9)),
    }


def attend_weights(weights, parts):
    ins = {"qkv": (HBM, weights[0]), "proj": (HBM, weights[1])} | numbered("a_part", HBM, parts)
    return ins, weight_scratch(weights[0], weights[1], ("qkv_w", "proj_w", "a_sems"))


def mlp_weights(weights, parts):
    ins = {"up": (HBM, weights[2]), "down": (HBM, weights[3])} | numbered("m_part", HBM, parts)
    return ins, weight_scratch(weights[2], weights[3], ("up_w", "down_w", "m_sems"))


def tie(array, after):
    return pl.pallas_call(
        lambda *refs: None,
        name="tie",
        out_shape=jax.ShapeDtypeStruct(array.shape, array.dtype),
        in_specs=[ANY] * (1 + len(after)),
        out_specs=ANY,
        input_output_aliases={0: 0},
        compiler_params=pltpu.CompilerParams(vmem_limit_bytes=1024 * 1024),
    )(array, *after)


def grid_buffer(width, width_c):
    return pltpu.VMEM((WIN, -(-width // 8) * 8, width_c), F32)


def extra_rows(heads):
    return heads + -heads % 16


def pack(layer, weights, gains=None, tables=None, after=()):
    rows = weights[0].shape[1] // 2
    wide = 4 * weights[1].shape[2]
    ins = {name: (HBM, w) for name, w in zip(("qkv", "proj", "up", "down"), weights)}
    outs = {"both": shape_of(3 * rows, wide)}
    scratch = {"sems": pltpu.SemaphoreType.DMA((7,))}
    if layer == 0:
        extra = extra_rows(2 * tables.shape[1])
        ins |= {"gains": (HBM, gains), "tables": (HBM, tables)}
        outs = {"attend": shape_of(rows + extra, wide), "mlp": shape_of(2 * rows, wide)}
        scratch |= {
            "small": pltpu.VMEM((extra, wide), F32),
            "gains_v": pltpu.VMEM(gains.shape, BF16),
            "tables_v": pltpu.VMEM(tables.shape, BF16),
            "small_sems": pltpu.SemaphoreType.DMA((2,)),
        }
    kernel = functools.partial(pack_kernel, layer)
    limit = PACK_VMEM_LIMIT if layer == 0 else VMEM_LIMIT
    return call(kernel, "pack", ins, outs, scratch, after, vmem=limit)


def table_sums(grads, index, width_c, after=()):
    heads = grads[0].shape[0]
    rows = heads + -heads % 16
    ins = numbered("grad", VMEM, grads) | {"index": (VMEM, index)}
    scratch = {"wide": pltpu.VMEM((rows, width_c), F32)}
    outs = {"out": shape_of(rows, width_c)}
    return call(table_sums_kernel, "table_sums", ins, outs, scratch, after).out


def params(own, other, rel, heads):
    width_c = own.shape[1] // 4
    ins = {"own": (VMEM, own), "other": (VMEM, other), "rel": (VMEM, rel)}
    outs = {
        "index": shape_of(SLOT, PAIR, dtype=jnp.int32),
        "gains": shape_of(2, 2, width_c, dtype=F32),
        "bias": shape_of(2, heads, SLOT, PAIR, dtype=F32),
    }
    scratch = {
        "table": pltpu.VMEM((2 * heads, TABLE), F32),
        "extra": pltpu.VMEM((extra_rows(heads), own.shape[1]), F32),
    }
    return call(params_kernel, "params", ins, outs, scratch)


def grid_ins(grid, edges=()):
    ins = {"own": (VMEM, grid)}
    if edges:
        ins |= {n: (VMEM, e) for n, e in zip(("rows_in", "cols_in", "corner_in"), edges)}
    return ins


def edge_outs(width, width_c):
    return {
        "rows": shape_of(2, SHIFT, width, width_c),
        "cols": shape_of(2, WIN, SHIFT, width_c),
        "corner": shape_of(2, SHIFT, SHIFT, width_c),
    }


def attend_forward(layer, mode, grid, edges, gains, bias, region, weights, parts, after=()):
    width, width_c = grid.shape[1:]
    tokens = width // WIN * SLOT
    heads = width_c // HEAD
    more, scratch = attend_weights(weights, parts)
    ins = {"gains": (VMEM, gains), "bias": (VMEM, bias)}
    ins |= grid_ins(grid, edges) | more
    if mode != "plain":
        ins |= {"region": (VMEM, region)}
        scratch |= {
            "labels": pltpu.VMEM((SIDE, 128), F32),
            "same": pltpu.VMEM((SLOT, tokens), F32),
        }
    outs = {
        "x": shape_of(tokens, width_c),
        "middle": shape_of(tokens, width_c, dtype=F32),
        "query_t": shape_of(width_c, tokens),
        "keys_t": shape_of(width_c, tokens),
        "keys": shape_of(tokens, width_c),
        "values": shape_of(tokens, width_c),
        "mixed_t": shape_of(width_c, tokens),
        "probs": shape_of(heads, SLOT, tokens, dtype=F32),
    }
    scratch |= {
        "flat": pltpu.VMEM((tokens, width_c), F32),
        "values_t": pltpu.VMEM((width_c, tokens), BF16),
    }
    kernel = functools.partial(attend_forward_kernel, layer, mode)
    return call(kernel, "attend_forward", ins, outs, scratch, after, 4)


def mlp_forward(layer, middle, gains, weights, parts, top, after=()):
    tokens, width_c = middle.shape
    width = top.shape[1]
    more, scratch = mlp_weights(weights, parts)
    ins = {"middle": (VMEM, middle), "gains": (VMEM, gains)} | more
    ins |= {"top": (VMEM, top)}
    outs = {"grid": shape_of(WIN, width, width_c)} | edge_outs(width, width_c)
    scratch |= {
        "flat": pltpu.VMEM((tokens, width_c), F32),
        "buffer": grid_buffer(width, width_c),
    }
    return call(functools.partial(mlp_forward_kernel, layer), "mlp_forward", ins, outs, scratch, after, 4)


def backward(layer, kept, grid, edges, gains, weights, a_parts, m_parts, ready=None, after=()):
    tokens, width_c = kept.middle.shape
    width = grid.shape[1]
    heads = width_c // HEAD
    second = layer == 1
    attend_ins, attend_scratch = attend_weights(weights, a_parts)
    mlp_ins, mlp_scratch = mlp_weights(weights, m_parts)
    ins = {"gains": (VMEM, gains)} | grid_ins(grid, edges)
    if second:
        ins["own_two"] = ins.pop("own")
    names = ("middle", "x", "query_t", "keys_t", "values", "probs")
    ins |= {name: (VMEM, getattr(kept, name)) for name in names} | attend_ins | mlp_ins
    pieces = [shape_of(2, 2, kinds, 4, width_c // 8, width_c) for kinds in (1, 2, 3)]
    if second:
        outs = {"keep": pieces[1], "send": pieces[1]}
    else:
        outs = {"keep": pieces[2]} | {"send" + str(i): pieces[0] for i in range(3)}
    outs |= {
        "grad_m": shape_of(tokens, width_c, dtype=F32),
        "grad_t": shape_of(3 * width_c, tokens),
        "bias_grad": shape_of(heads, SLOT, PAIR, dtype=F32),
    }
    scratch = attend_scratch | mlp_scratch
    scratch |= {
        "out_t": pltpu.VMEM((width_c, tokens), BF16),
        "flat": pltpu.VMEM((tokens, width_c), F32),
    }
    if second:
        outs |= {"out": shape_of(WIN, width, width_c), "grid": shape_of(WIN, width, width_c)}
        outs |= edge_outs(width, width_c)
        scratch |= {"buffer": grid_buffer(width, width_c)}
    else:
        ins |= {"mixed_t": (VMEM, kept.mixed_t)}
        ins |= {name: (VMEM, value) for name, value in vars(ready).items()}
        scratch |= sides(width_c, tokens)

    def kernel(r):
        mlp_backward_kernel(layer, "in" if second else "out", layer, r)
        attend_backward_kernel(layer, "si" if second else "sw", 2, r)

    return call(kernel, "backward", ins, outs, scratch, after, 15)


def prepare(layer, kept, gains, weights, parts, after=()):
    tokens, width_c = kept.middle.shape
    inner = weights[2].shape[2]
    ins = {"middle": (VMEM, kept.middle), "gains": (VMEM, gains), "up": (HBM, weights[2])}
    ins |= numbered("m_part", HBM, parts)
    outs = {
        "hidden_t": shape_of(width_c, tokens),
        "activated_t": shape_of(inner, tokens),
        "slope": shape_of(tokens, inner),
    }
    scratch = {
        "up_w": pltpu.VMEM((2 * weights[2].shape[1], inner), BF16),
        "m_sems": pltpu.SemaphoreType.DMA((2, 9)),
    }
    kernel = functools.partial(prepare_kernel, layer)
    return call(kernel, "prepare", ins, outs, scratch, after, 3)


def sides(width_c, tokens):
    return {
        "left": pltpu.VMEM((2, width_c, tokens), BF16),
        "right": pltpu.VMEM((4 * width_c, tokens), BF16),
    }


def attend_weight_grads(layer, kept, back, gains, after=()):
    tokens, width_c = back.grad_m.shape
    ins = {"gains": (VMEM, gains), "grad_m": (VMEM, back.grad_m)}
    ins |= {"x": (VMEM, kept.x), "mixed_t": (VMEM, kept.mixed_t), "grad_t": (VMEM, back.grad_t)}
    pieces = shape_of(2, 2, 1, 4, width_c // 8, width_c)
    kernel = functools.partial(attend_backward_kernel, layer, "w", 0)
    outs = {"keep": pieces, "send": pieces}
    return call(kernel, "attend_weight_grads", ins, outs, sides(width_c, tokens), after, 2)


def input_grad(layer, kept, back, gains, weights, a_parts, own_two, edges, after=()):
    tokens, width_c = back.grad_m.shape
    width = own_two.shape[1]
    more, scratch = attend_weights(weights, a_parts)
    ins = {"gains": (VMEM, gains), "grad_m": (VMEM, back.grad_m)}
    ins |= {"x": (VMEM, kept.x), "grad_t": (VMEM, back.grad_t)} | more
    ins |= grid_ins(own_two, edges)
    ins["own_two"] = ins.pop("own")
    outs = {"grid": shape_of(WIN, width, width_c), "mixed": shape_of(WIN, width, width_c)}
    scratch |= {
        "flat": pltpu.VMEM((tokens, width_c), F32),
        "buffer": grid_buffer(width, width_c),
    }

    def kernel(r):
        attend_backward_kernel(layer, "i", 0, r)
        roll_out_kernel(r)

    return call(kernel, "input_grad", ins, outs, scratch, after, 3)


def collect(one, two, total, weights, gains, tables):
    names = ("qkv", "proj", "up", "down", "gains_grad", "tables_grad")
    grads = [shape_of(*w.shape, dtype=F32) for w in (*weights, gains, tables)]
    ins = numbered("one", VMEM, one) | numbered("two", VMEM, two)
    ins |= {"w_qkv": (HBM, weights[0]), "w_up": (HBM, weights[2]), "gains": (VMEM, gains)}
    ins |= {"total": (VMEM, total)}
    scratch = {
        "attend_f": pltpu.VMEM(grads[2].shape, F32),
        "up_f": pltpu.VMEM(grads[2].shape, F32),
        "down_f": pltpu.VMEM(grads[3].shape, F32),
        "qkv_w": pltpu.VMEM(weights[0].shape, BF16),
        "up_w": pltpu.VMEM(weights[2].shape, BF16),
        "load_sems": pltpu.SemaphoreType.DMA((2,)),
        "out_sems": pltpu.SemaphoreType.DMA((8,)),
        "wide": pltpu.VMEM((256, 128), F32),
    }
    outs = dict(zip(names, grads))
    spaces = [HBM] * 4 + [VMEM] * 2
    return call(collect_kernel, "collect", ins, outs, scratch, spaces=spaces)


def per_device(
    tokens, norm_gains, w_qkv, w_proj, w_up, w_down, tables, region_ids, rel_index, cotangent
):
    width, width_c = tokens.shape[1:]
    weights = (w_qkv, w_proj, w_up, w_down)

    heads = 2 * tables.shape[1]

    piece = pack(0, weights, norm_gains, tables)
    attend_one = share_halves(piece.attend)
    settings = params(piece.attend, attend_one[0], rel_index, heads)
    gains, bias, index = settings.gains, settings.bias, settings.index
    mlp_piece = piece.mlp
    piece = pack(1, weights, after=(attend_one[0],))
    one = attend_forward(
        0, "plain", tokens, (), gains, bias, None, weights, attend_one, after=(piece.both,)
    )
    mlp_one = share_halves(mlp_piece, after=(one.middle,))
    done = mlp_forward(0, one.middle, gains, weights, mlp_one, cotangent)
    edges = halo(done.rows, done.cols, done.corner, 1)
    parts_two = share_halves(piece.both, after=edges)
    two = attend_forward(
        1, "in", done.grid, edges, gains, bias, region_ids, weights, parts_two
    )
    back2 = backward(1, two, cotangent, edges, gains, weights, parts_two, parts_two)
    got_m2 = exchange(back2.send, 1, 0)
    edges = halo(back2.rows, back2.cols, back2.corner, -1)
    att2 = attend_weight_grads(1, two, back2, gains)
    ready = prepare(0, one, gains, weights, mlp_one, after=(att2.send,))
    side_two = start_side(
        (back2.keep, att2.keep),
        (got_m2, exchange(att2.send, 1, 0)),
        after=(*edges, ready.slope),
    )
    back1 = backward(
        0,
        one,
        back2.grid,
        edges,
        gains,
        weights,
        attend_one,
        mlp_one,
        ready,
        after=(side_two[0],),
    )
    rows = width_c // 8
    gots = [exchange(send, 1, 0) for send in (back1.send0, back1.send1, back1.send2)]
    small = table_sums((back1.bias_grad, back2.bias_grad), index, width_c)
    side_one, small = start_side(
        (back1.keep,), gots, small=(small, exchange(small, 1, 0)), after=side_two[1:]
    )
    face_two = start_face(side_two, after=side_one[:1])
    last = input_grad(
        0, one, back1, gains, weights, attend_one, back2.out, edges, after=side_one[:1]
    )
    total_two, got_two = finish_sum(face_two, rows)
    face_one = start_face(side_one, small=small, after=(last.mixed, got_two))
    pair_two = gather_pair(total_two, 3 * rows)
    total_one, _ = finish_sum(face_one, rows, after=(pair_two,))
    pair_one = gather_pair(total_one, 3 * rows)
    sums = collect(gather(pair_one), gather(pair_two), total_one, weights, norm_gains, tables)
    return (
        last.mixed,
        last.grid,
        sums.gains_grad,
        sums.qkv,
        sums.proj,
        sums.up,
        sums.down,
        sums.tables_grad,
    )


def solution(mesh):
    return jax.shard_map(
        per_device,
        mesh=mesh,
        in_specs=(
            P("seq", "fsdp", None),
            P(None, None, "fsdp"),
            P(None, "fsdp", None),
            P(None, "fsdp", None),
            P(None, "fsdp", None),
            P(None, "fsdp", None),
            P(None, "fsdp", None),
            P("seq", "fsdp"),
            P(),
            P("seq", "fsdp", None),
        ),
        out_specs=(
            P("seq", "fsdp", None),
            P("seq", "fsdp", None),
            P(None, None, "fsdp"),
            P(None, "fsdp", None),
            P(None, "fsdp", None),
            P(None, "fsdp", None),
            P(None, "fsdp", None),
            P(None, "fsdp", None),
        ),
        check_vma=False,
    )
```

```python
import functools
import types

import jax
import jax.numpy as jnp
from jax import lax
from jax.experimental import pallas as pl
from jax.experimental.pallas import tpu as pltpu
from jax.sharding import PartitionSpec as P

WIN = 7
SHIFT = 3
TABLE = 169
SIDE = 8
SLOT = SIDE * SIDE
HEAD = 32
PAIR = 2 * SLOT
EPSILON = 1e-05
MASKED_SCORE = -1000000000.0
F32 = jnp.float32
BF16 = jnp.bfloat16
VMEM_LIMIT = 24 * 1024 * 1024
PACK_VMEM_LIMIT = 60 * 1024 * 1024
BYTES_PER_US = 3500000


def exchange(array, ds, dy):
    n, m = lax.axis_size("seq"), lax.axis_size("fsdp")
    pairs = [(s * m + y, (s ^ ds) * m + (y ^ dy)) for s in range(n) for y in range(m)]
    return lax.ppermute(array, ("seq", "fsdp"), pairs)


def take_from(array, ds, dy):
    n, m = lax.axis_size("seq"), lax.axis_size("fsdp")
    pairs = [((s + ds) % n * m + (y + dy) % m, s * m + y) for s in range(n) for y in range(m)]
    return lax.ppermute(array, ("seq", "fsdp"), pairs)


def halo(near_rows, near_cols, corner, step):
    return (
        take_from(near_rows, step, 0),
        take_from(near_cols, 0, step),
        take_from(corner, step, step),
    )


def share_halves(piece, after=()):
    first = exchange(piece, 0, 1)
    if after:
        first = tie(first, after)
    return (first, exchange(first, 1, 0))


def share(first, second, after):
    second = tie(second, after)
    return (first, second, exchange(first, 1, 0), exchange(second, 1, 0))


def add(*terms):
    total = terms[0].astype(F32)
    for term in terms[1:]:
        total = total + term.astype(F32)
    return total


def sum_higher(value):
    step = 16
    while step < lax.axis_size("seq"):
        value = add(value, exchange(value, step, 0)).astype(value.dtype)
        step *= 2
    return value


def start_side(keeps, gots, after=()):
    kinds = sum(keep.shape[2] for keep in keeps)
    out = shape_of(2, kinds, *keeps[0].shape[3:])
    ins = numbered("keep", VMEM, keeps) | numbered("got", VMEM, gots)
    r = call(add_side_kernel, "add_side", ins, dict(own=out, other=out), {}, after)
    return r.own, exchange(r.other, 0, 1)


def start_sides(keeps, gots, after=()):
    kinds = sum(keep.shape[2] for keep in keeps)
    out = shape_of(2, kinds, 2, *keeps[0].shape[4:])
    ins = numbered("keep", VMEM, keeps) | numbered("got", VMEM, gots)
    outs = dict(own0=out, own1=out, other0=out, other1=out)
    r = call(add_sides_kernel, "add_sides", ins, outs, {}, after)
    return r.own0, exchange(r.other0, 0, 1), r.own1, exchange(r.other1, 2, 0)


def add_pair(value, other):
    ins = numbered("part", VMEM, (value, other))
    return call(add_all_kernel, "add_all", ins, dict(out=shape_of(*value.shape)), {}).out


def start_face(parts, after=()):
    _, kinds, _, rows, cols = parts[0].shape
    out = shape_of(kinds * 2 * rows, cols)
    outs = {"out" + str(i): out for i in range(4)}
    r = call(add_face_kernel, "add_face", numbered("part", VMEM, parts), outs, {}, after)
    return r.out0, exchange(r.out3, 6, 0), exchange(r.out2, 2, 0), exchange(r.out1, 4, 0)


def start_faces(parts, after=(), small=()):
    _, kinds, _, rows, cols = parts[0].shape
    extra = small[0].shape[0] if small else 0
    first, second = shape_of(kinds * rows + extra, cols), shape_of(kinds * rows, cols)
    ins = numbered("part", VMEM, parts) | numbered("small", VMEM, small)
    outs = dict(out0=first, out1=second, side0=first, side1=second, corner0=first, corner1=second)
    outs |= dict(low=shape_of(2 * kinds * rows + extra, cols))
    r = call(add_faces_kernel, "add_faces", ins, outs, {}, after)
    corners = (exchange(r.corner0, 6, 0), exchange(r.corner1, 4, 1))
    low = exchange(r.low, 4, 0)
    return r.out0, r.out1, exchange(r.side0, 2, 0), exchange(r.side1, 0, 1), *corners, low


def finish_sum(terms, rows, kernel, after=()):
    out = shape_of(rows, terms[0].shape[1])
    r = call(kernel, "halve", numbered("term", VMEM, terms), dict(own=out, other=out), {}, after)
    got = exchange(r.other, 8, 0)
    return sum_higher(add_pair(r.own, got)), got


def gather_pair(total, rows, after=()):
    ins = dict(own=(VMEM, total), other=(VMEM, exchange(total, 8, 0)))
    out = shape_of(2, rows, total.shape[1])
    return call(stack_kernel, "stack", ins, dict(out=out), {}, after).out


def gather(pair, after=()):
    here = [pair, exchange(pair, 4, 0), exchange(pair, 2, 0), exchange(pair, 6, 0)]
    if after:
        here = [tie(part, after) for part in here]
    return here + [exchange(part, 1, 0) for part in here]


def flip(index, bits):
    return jnp.bitwise_xor(index, bits)


def mlp_pairs(layer, spot, up, down, out):
    count, width_c = out.shape[0] // 2, down.shape[2]
    start = pl.multiple_of(spot * count, 16)
    pairs = [(up.at[layer, pl.ds(start, count), :], out.at[:count])]
    for index in range(4):
        first = pl.multiple_of((spot * 4 + index) * count, 16)
        cols = slice(index * width_c, (index + 1) * width_c)
        pairs.append((down.at[layer, pl.ds(first, count), :], out.at[count:, cols]))
    return pairs


def attend_pairs(layer, spot, qkv, proj, out):
    rows, width_c = out.shape[0], proj.shape[2]
    start = pl.multiple_of(spot * rows, 16)
    return [
        (qkv.at[layer, pl.ds(start, rows), :], out.at[:, : 3 * width_c]),
        (proj.at[layer, pl.ds(start, rows), :], out.at[:, 3 * width_c :]),
    ]


def pack_mlp_kernel(r):
    rows = r.up.shape[1] // 2
    spot = 2 * r.place[0] + r.place[1]
    copies = start_copies(mlp_pairs(0, spot, r.up, r.down, r.out.at[:rows]), r.sems)
    wait_all(start_copies([(r.tables, r.tables_v), (r.gains, r.gains_v)], r.small_sems))
    r.small[...] = jnp.zeros_like(r.small)
    heads = r.tables.shape[1]
    half = r.gains.shape[2]
    for index in range(2):
        r.small[index * heads : (index + 1) * heads, :TABLE] = r.tables_v[index].astype(F32)
        r.small[2 * index : 2 * index + 2, 256 : 256 + half] = r.gains_v[index].astype(F32)
    r.out[rows:] = r.small[...].astype(BF16)
    wait_all(copies)


def pack_attend_kernel(r):
    wait_all(start_copies(attend_pairs(0, r.place[0], r.qkv, r.proj, r.out), r.sems))


def pack_both_kernel(r):
    rows = r.qkv.shape[1] // 2
    pairs = attend_pairs(1, r.place[0], r.qkv, r.proj, r.out.at[:rows])
    pairs += mlp_pairs(1, r.place[0], r.up, r.down, r.out.at[rows:])
    wait_all(start_copies(pairs, r.sems))


def chosen(index, key):
    line = jnp.broadcast_to(index[key : key + 1, :], (TABLE, index.shape[1]))
    entries = lax.broadcasted_iota(jnp.int32, line.shape, 0)
    return jnp.where(line == entries, 1.0, 0.0).astype(BF16)


def table_sums_kernel(r):
    heads = r.grad0.shape[0]
    total = jnp.zeros((2 * heads, TABLE), F32)
    for key in range(SLOT):
        pair = jnp.concatenate([r.grad0[:, key, :], r.grad1[:, key, :]], axis=0)
        total = total + mm_nt(pair.astype(BF16), chosen(r.index, key))
    r.wide[...] = jnp.zeros_like(r.wide)
    half = r.out.shape[1] // 2
    r.wide[:heads, :TABLE] = total[:heads]
    r.wide[:heads, half : half + TABLE] = total[heads:]
    r.out[...] = r.wide[...].astype(BF16)


def slots(rows, count):
    row = jnp.bitwise_and(lax.broadcasted_iota(jnp.int32, (rows, count), 0), SLOT - 1)
    token = lax.broadcasted_iota(jnp.int32, (rows, count), 1)
    at = token
    for side in range(1, WIN):
        at = at + jnp.where(token >= side * WIN, 1, 0)
    return jnp.where(row == at, 1.0, 0.0).astype(BF16)


def is_token(shape, axis):
    place = jnp.bitwise_and(lax.broadcasted_iota(jnp.int32, shape, axis), SLOT - 1)
    return (place < WIN * SIDE) & (jnp.bitwise_and(place, SIDE - 1) < WIN)


def spread_index(rel):
    count = rel.shape[0]
    keys = mm_nt(slots(SLOT, count), rel.astype(F32).astype(BF16))
    pairs = mm_nt(keys.astype(BF16), slots(PAIR, count))
    real = is_token(pairs.shape, 0) & is_token(pairs.shape, 1)
    return jnp.where(real, (pairs + 0.5).astype(jnp.int32), -1)


def same_label(r):
    r.labels[...] = jnp.full_like(r.labels, -1.0)
    for window in range(r.region.shape[1] // WIN):
        r.labels[:WIN, :WIN] = r.region[:, window * WIN : window * WIN + WIN].astype(F32)
        block = r.labels[:, :SIDE].astype(BF16)
        lane = lax.broadcasted_iota(jnp.int32, (SIDE, SLOT), 1)
        row = lax.broadcasted_iota(jnp.int32, (SIDE, SLOT), 0)
        repeat = jnp.where(jnp.bitwise_and(lane, SIDE - 1) == row, 1.0, 0.0).astype(BF16)
        own = (lane >= row * SIDE) & (lane < row * SIDE + SIDE)
        line = jnp.sum(jnp.where(own, mm(block, repeat), 0.0), 0, keepdims=True)
        wide = jnp.broadcast_to(line, (SLOT, SLOT))
        diagonal_only = lax.broadcasted_iota(jnp.int32, wide.shape, 0) == (
            lax.broadcasted_iota(jnp.int32, wide.shape, 1)
        )
        column = jnp.sum(jnp.where(diagonal_only, wide, 0.0), 1, keepdims=True)
        r.same[:, window * SLOT : window * SLOT + SLOT] = jnp.where(wide == column, 1.0, 0.0)


def params_kernel(r):
    half = r.gains.shape[2] // 2
    heads = r.bias.shape[1] // 2
    rows = r.own.shape[0] - r.extra.shape[0]
    flipped = r.place[3] == 1
    r.extra[...] = jnp.where(flipped, r.other[rows:].astype(F32), r.own[rows:].astype(F32))
    for part in range(2):
        for index in range(2):
            r.gains[index, :, part * half : (part + 1) * half] = r.extra[
                2 * index : 2 * index + 2, 256 : 256 + half
            ]
            start = (2 * index + part) * heads
            r.table[start : start + heads, :] = r.extra[index * heads : (index + 1) * heads, :TABLE]
        if part == 0:
            r.extra[...] = jnp.where(
                flipped, r.own[rows:].astype(F32), r.other[rows:].astype(F32)
            )
    r.index[...] = spread_index(r.rel[...])
    table = r.table[...].astype(BF16)
    for key in range(SLOT):
        line = mm(table, chosen(r.index, key))
        r.bias[0, :, key, :] = line[: 2 * heads]
        r.bias[1, :, key, :] = line[2 * heads :]


def start_copies(pairs, sems):
    copies = [
        pltpu.make_async_copy(source, target, sems.at[index])
        for index, (source, target) in enumerate(pairs)
    ]
    for copy in copies:
        copy.start()
    return copies


def fetch(place, layer, own, parts, pick, full, sems):
    half = full.shape[0] // 2
    rows = half // len(parts)
    y = place[3]
    pairs = [(own.at[layer], full.at[pl.ds(pl.multiple_of(y * half, 16), half)])]
    core, x = place[0], place[1]
    spots = [core, flip(core, 1)]
    if len(parts) == 4:
        spots = [2 * flip(core, index // 2) + flip(x, index % 2) for index in range(4)]
    for spot, part in zip(spots, parts):
        pieces = pick(part)
        count = rows // len(pieces)
        for index, piece in enumerate(pieces):
            start = pl.multiple_of((1 - y) * half + spot * rows + index * count, 16)
            pairs.append((piece, full.at[pl.ds(start, count)]))
    return start_copies(pairs, sems)


def fetch_attend(place, layer, own, parts, qkv_w, proj_w, sems):
    rows = own[0].shape[1] // 2
    wide = qkv_w.shape[1]

    def qkv(part):
        return [part.at[:rows, :wide]]

    def proj(part):
        return [part.at[:rows, wide:]]

    return [
        fetch(place, layer, own[0], parts, qkv, qkv_w, sems.at[0]),
        fetch(place, layer, own[1], parts, proj, proj_w, sems.at[1]),
    ]


def fetch_mlp(place, layer, own, parts, up_w, down_w, sems):
    rows = own[0].shape[1] // len(parts)
    first = parts[0].shape[0] - 2 * rows if len(parts) == 2 else 0
    width_c = up_w.shape[0]

    def up(part):
        return [part.at[first : first + rows]]

    def down(part):
        band = slice(first + rows, first + 2 * rows)
        return [part.at[band, i * width_c : (i + 1) * width_c] for i in range(4)]

    return [
        fetch(place, layer, own[0], parts, up, up_w, sems.at[0]),
        fetch(place, layer, own[1], parts, down, down_w, sems.at[1]),
    ]


def add_refs(refs):
    total = refs[0][...].astype(F32)
    for ref in refs[1:]:
        total = total + ref[...].astype(F32)
    return total


def add_small(r):
    return add_refs(listed(r, "small")).astype(BF16)


def kinds_of(refs):
    return [(ref, kind) for ref in refs for kind in range(ref.shape[2])]


def add_side_kernel(r):
    pairs = zip(kinds_of(listed(r, "keep")), kinds_of(listed(r, "got")))
    for index, ((keep, first), (got, second)) in enumerate(pairs):
        for y, out in enumerate((r.own, r.other)):
            for x in range(2):
                value = keep[y, x, first].astype(F32) + got[y, x, second].astype(F32)
                out[x, index] = value.astype(BF16)


def add_sides_kernel(r):
    pairs = zip(kinds_of(listed(r, "keep")), kinds_of(listed(r, "got")))
    for index, ((keep, first), (got, second)) in enumerate(pairs):
        for apart, outs in enumerate(((r.own0, r.own1), (r.other0, r.other1))):
            for along in range(2):
                for low in range(2):
                    for high, (y, x) in enumerate(((apart, along), (along, apart))):
                        z = 2 * high + low
                        value = keep[y, x, first, z].astype(F32) + got[y, x, second, z].astype(F32)
                        outs[high][along, index, low] = value.astype(BF16)


def add_face_kernel(r):
    _, kinds, _, rows, _ = r.part0.shape
    for index, out in enumerate(listed(r, "out")):
        x, z = index >> 1, index & 1
        for kind in range(kinds):
            for high in range(2):
                at = (x, kind, 2 * high + z)
                first = (kind * 2 + high) * rows
                value = r.part0[at].astype(F32) + r.part1[at].astype(F32)
                out[first : first + rows, :] = value.astype(BF16)


def add_faces_kernel(r):
    _, kinds, _, rows, _ = r.part0.shape
    size = kinds * rows
    for kind in range(kinds):
        band = slice(kind * rows, (kind + 1) * rows)
        later = slice(r.low.shape[0] - size + kind * rows, r.low.shape[0] - size + (kind + 1) * rows)
        for order, (own, got) in enumerate(((r.part0, r.part1), (r.part2, r.part3))):
            sums = [
                [add_refs((own.at[a, kind, z], got.at[a, kind, z])).astype(BF16) for z in range(2)]
                for a in range(2)
            ]
            outs = ((r.out0, r.side0, r.corner0), (r.out1, r.side1, r.corner1))[order]
            outs[0][band, :] = sums[0][0]
            outs[1][band, :] = sums[1][0]
            outs[2][band, :] = sums[1][1]
            r.low[later if order else band, :] = sums[0][1]
    if hasattr(r, "small0"):
        small = add_small(r)
        extra = slice(size, size + small.shape[0])
        for out in (r.out0, r.side0, r.corner0, r.low):
            out[extra, :] = small


def halve_kernel(r):
    terms = listed(r, "term")
    kinds = 3
    rows = r.own.shape[0] // kinds
    for high, out in enumerate((r.own, r.other)):
        for kind in range(kinds):
            first = (kind * 2 + high) * rows
            value = add_refs([term.at[first : first + rows, :] for term in terms])
            out[kind * rows : (kind + 1) * rows, :] = value.astype(BF16)


def halve_faces_kernel(r):
    own0, own1, side0, side1, corner0, corner1, low = listed(r, "term")
    size, first = own1.shape[0], own0.shape[0]
    r.own[...] = add_refs((own0, side0, corner0, low.at[:first])).astype(BF16)
    r.other[:size, :] = add_refs((own1, side1, corner1, low.at[first:])).astype(BF16)
    if first > size:
        r.other[size:, :] = r.own[size:, :]


def add_all_kernel(r):
    r.out[...] = add_refs(listed(r, "part")).astype(BF16)


def stack_kernel(r):
    rows = r.out.shape[1]
    r.out[0] = r.own[:rows, :]
    r.out[1] = r.other[:rows, :]


def wait_all(copies):
    for copy in copies:
        copy.wait()


def row_segments(mode, refs, row, width):
    if mode == "plain":
        return [(0, refs[0][row], 0, width)]
    own, rows, cols, corner = refs
    rest = width - SHIFT
    if mode == "in":
        if row < WIN - SHIFT:
            return [
                (0, own[row + SHIFT], SHIFT, rest),
                (rest, cols[row + SHIFT], 0, SHIFT),
            ]
        at = row - (WIN - SHIFT)
        return [(0, rows[at], SHIFT, rest), (rest, corner[at], 0, SHIFT)]
    if row >= SHIFT:
        return [(0, cols[row - SHIFT], 0, SHIFT), (SHIFT, own[row - SHIFT], 0, rest)]
    return [(0, corner[row], 0, SHIFT), (SHIFT, rows[row], 0, rest)]


def fill_windows(mode, refs, out):
    width = refs[0].shape[1]
    out[...] = jnp.zeros_like(out)
    for row in range(WIN):
        for first, source, start, count in row_segments(mode, refs, row, width):
            source = source.astype(F32)
            for window in range(width // WIN):
                low = max(first, window * WIN)
                high = min(first + count, window * WIN + WIN)
                if low < high:
                    spot = window * SLOT + row * SIDE + low - window * WIN
                    begin = start + low - first
                    out[spot : spot + high - low, :] = source[begin : begin + high - low, :]


def fill_grid(source, buffer, width):
    for row in range(WIN):
        for window in range(width // WIN):
            spot = window * SLOT + row * SIDE
            buffer[row, window * WIN : window * WIN + WIN, :] = source[spot : spot + WIN, :]


def normalize(values):
    centred = values - jnp.mean(values, -1, keepdims=True)
    factor = lax.rsqrt(jnp.mean(centred * centred, -1, keepdims=True) + EPSILON)
    return centred * factor, factor


def normalize_back(grad_norm, normed, factor):
    spread = jnp.mean(grad_norm * normed, -1, keepdims=True)
    return factor * (grad_norm - jnp.mean(grad_norm, -1, keepdims=True) - normed * spread)


def mm(left, right):
    return lax.dot_general(left, right, (((1,), (0,)), ((), ())), preferred_element_type=F32)


def mm_nt(left, right):
    return lax.dot_general(left, right, (((1,), (1,)), ((), ())), preferred_element_type=F32)


def only_head(group, which):
    rows = lax.broadcasted_iota(jnp.int32, group.shape, 0)
    inside = (rows >= which * HEAD) & (rows < (which + 1) * HEAD)
    return jnp.where(inside, group, jnp.zeros_like(group))


def by_head(group, axis):
    place = lax.broadcasted_iota(jnp.int32, group.shape, axis)
    copies = []
    for head in range(4):
        inside = (place >= head * HEAD) & (place < (head + 1) * HEAD)
        copies.append(jnp.where(inside, group, jnp.zeros_like(group)))
    return jnp.concatenate(copies, axis=1 - axis)


def diagonal(block):
    lanes = lax.broadcasted_iota(jnp.int32, (SLOT, PAIR), 1)
    return jnp.where(lanes < SLOT, block[:SLOT], block[SLOT:])


def spread_diagonal(packed):
    lanes = lax.broadcasted_iota(jnp.int32, (SLOT, PAIR), 1)
    low = jnp.where(lanes < SLOT, packed, 0.0)
    high = jnp.where(lanes < SLOT, 0.0, packed)
    return jnp.concatenate([low, high], axis=0).astype(BF16)


def target(r, apart, kind):
    if not apart:
        return r.keep, kind
    if hasattr(r, "send"):
        return r.send, kind
    return listed(r, "send")[kind], 0


def store_columns(r, apart, x, kind, value):
    rows = value.shape[0] // 8
    out, kind = target(r, apart, kind)
    value = value.astype(BF16)
    for y in range(2):
        for z in range(4):
            first = (y * 4 + z) * rows
            at = (flip(r.place[3], y), flip(r.place[1], x), kind, flip(r.place[2], z))
            out[at] = value[first : first + rows]


def store_rows(r, apart, y, kind, value):
    rows = value.shape[0] // 8
    out, kind = target(r, apart, kind)
    value = value.astype(BF16)
    for x in range(2):
        for z in range(4):
            first = (x * 4 + z) * rows
            at = (flip(r.place[3], y), flip(r.place[1], x), kind, flip(r.place[2], z))
            out[at] = value[first : first + rows]


def grid_refs(r, which):
    if not hasattr(r, "rows_in"):
        return [r.own]
    return [r.own if which == 0 else r.own_two] + [
        edge.at[which] for edge in (r.rows_in, r.cols_in, r.corner_in)
    ]


def attend_forward_kernel(layer, mode, r):
    width_c = r.flat.shape[1]
    heads = width_c // HEAD
    copies = fetch_attend(
        r.place, layer, (r.qkv, r.proj), listed(r, "a_part"), r.qkv_w, r.proj_w, r.a_sems
    )
    if hasattr(r, "up"):
        parts = listed(r, "a_part")
        copies += fetch_mlp(r.place, layer, (r.up, r.down), parts, r.up_w, r.down_w, r.m_sems)
    fill_windows(mode, grid_refs(r, 0), r.flat)
    r.x[...] = r.flat[...].astype(BF16)
    normed, _ = normalize(r.flat[...])
    hidden = (normed * r.gains[layer, 0:1, :]).astype(BF16)
    wait_all(copies[0])
    query = (mm(hidden, r.qkv_w[:, :width_c]) * HEAD ** (-0.5)).astype(BF16)
    r.query[...] = query
    r.query_t[...] = query.T
    r.keys[...] = mm(hidden, r.qkv_w[:, width_c : 2 * width_c]).astype(BF16)
    r.keys_t[...] = r.keys[...].T
    r.values[...] = mm(hidden, r.qkv_w[:, 2 * width_c :]).astype(BF16)
    r.values_t[...] = r.values[...].T
    if mode == "plain":
        meet = is_token((SLOT, PAIR), 0)
    else:
        same_label(r)
    for head in range(heads):
        group = slice(head // 4 * 128, head // 4 * 128 + 128)
        rows = slice(head * HEAD, head * HEAD + HEAD)
        for pair in range(r.flat.shape[0] // PAIR):
            span = slice(pair * PAIR, pair * PAIR + PAIR)
            raw = mm(r.keys[span, group], only_head(r.query_t[group, span], head % 4))
            if mode != "plain":
                meet = r.same[:, span] > 0.5
            scores = jnp.where(meet, diagonal(raw) + r.bias[layer, head], MASKED_SCORE)
            weighted = jnp.exp(scores - jnp.max(scores, 0, keepdims=True))
            attention = weighted / jnp.sum(weighted, 0, keepdims=True)
            r.probs[head, :, span] = attention
            r.mixed_t[rows, span] = mm(r.values_t[rows, span], spread_diagonal(attention)).astype(
                BF16
            )
    wait_all(copies[1])
    r.middle[...] = r.flat[...] + mm(r.mixed_t[...].T, r.proj_w[...])
    for copy in copies[2:]:
        wait_all(copy)


def attend_backward_kernel(layer, parts, kind, r):
    width_c = r.x.shape[1]
    heads = width_c // HEAD
    normed, factor = normalize(r.x[...].astype(F32))
    gain = r.gains[layer, 0:1, :]
    attended = r.grad_m[...].astype(BF16)
    if "s" in parts:
        r.out_t[...] = mm_nt(r.proj_w[...], attended).astype(BF16)
        out = r.out_t[...].T
        for first in range(0, heads, 4):
            group = slice(first * HEAD, (first + 4) * HEAD)
            totals = [jnp.zeros((SLOT, PAIR), F32)] * 4
            for pair in range(r.x.shape[0] // PAIR):
                span = slice(pair * PAIR, pair * PAIR + PAIR)
                raw = mm(r.values[span, group], by_head(r.out_t[group, span], 0))
                spread_p, spread_s = [], []
                for head in range(4):
                    attention = r.probs[first + head, :, span]
                    grad_p = diagonal(raw[:, head * PAIR : (head + 1) * PAIR])
                    grad_s = attention * (
                        grad_p - jnp.sum(grad_p * attention, 0, keepdims=True)
                    )
                    totals[head] = totals[head] + grad_s
                    spread_p.append(spread_diagonal(attention))
                    spread_s.append(spread_diagonal(grad_s))
                grad_q = mm(by_head(r.keys_t[group, span], 0), jnp.concatenate(spread_s, axis=0))
                r.grad_t[group, span] = (grad_q * HEAD ** (-0.5)).astype(BF16)
                query = r.query[span, group]
                grad_k = mm(jnp.concatenate(spread_s, axis=1), by_head(query, 1))
                r.grad_k[span, group] = grad_k.astype(BF16)
                grad_v = mm(jnp.concatenate(spread_p, axis=1), by_head(out[span, group], 1))
                r.grad_v[span, group] = grad_v.astype(BF16)
            for head in range(4):
                r.bias_grad[first + head] = totals[head]
        r.grad_t[width_c : 2 * width_c, :] = r.grad_k[...].T
        r.grad_t[2 * width_c :, :] = r.grad_v[...].T
    if "w" in parts:
        r.left[0] = (normed * gain).astype(BF16).T
        r.left[1] = r.mixed_t[...]
        r.right[0] = r.grad_t[:width_c, :].T
        r.right[1] = r.grad_k[...]
        r.right[2] = r.grad_v[...]
        r.right[3] = attended
        for apart in (1, 0):
            for x in range(2):
                chunk = 2 * flip(r.place[0], apart) + x
                left = r.left[(chunk == 3).astype(jnp.int32)]
                store_columns(r, apart, x, kind, mm(left, r.right[chunk]))
    if "i" in parts:
        grad_hidden = mm(r.qkv_w[...], r.grad_t[...]).T
        r.flat[...] = r.grad_m[...] + normalize_back(grad_hidden * gain, normed, factor)
        width = r.grid.shape[1]
        fill_grid(r.flat, r.buffer, width)
        r.grid[...] = r.buffer[:, :width, :].astype(BF16)
        if hasattr(r, "rows"):
            r.rows[0] = r.buffer[WIN - SHIFT :, :width, :].astype(BF16)
            r.cols[0] = r.buffer[:, width - SHIFT : width, :].astype(BF16)
            r.corner[0] = r.buffer[WIN - SHIFT :, width - SHIFT : width, :].astype(BF16)


GELU_A = 0.7978845608028654
GELU_B = 0.044715


def gelu_parts(inner):
    square = inner * inner
    tanh = jnp.tanh(GELU_A * (inner * (1.0 + GELU_B * square)))
    return square, tanh


def mlp_forward_kernel(layer, r):
    width_c = r.flat.shape[1]
    copies = fetch_mlp(
        r.place, layer, (r.up, r.down), listed(r, "m_part"), r.up_w, r.down_w, r.m_sems
    )
    normed, _ = normalize(r.middle[...])
    hidden = (normed * r.gains[layer, 1:2, :]).astype(BF16)
    output = r.middle[...]
    wait_all(copies[0])
    wait_all(copies[1])
    for chunk in range(r.up_w.shape[1] // width_c):
        cols = slice(chunk * width_c, (chunk + 1) * width_c)
        inner = mm(hidden, r.up_w[:, cols])
        _, tanh = gelu_parts(inner)
        output = output + mm((0.5 * inner * (1.0 + tanh)).astype(BF16), r.down_w[cols, :])
    r.flat[...] = output
    width = r.grid.shape[1]
    fill_grid(r.flat, r.buffer, width)
    r.grid[...] = r.buffer[:, :width, :].astype(BF16)
    r.rows[0] = r.buffer[:SHIFT, :width, :].astype(BF16)
    r.cols[0] = r.buffer[:, :SHIFT, :].astype(BF16)
    r.corner[0] = r.buffer[:SHIFT, :SHIFT, :].astype(BF16)
    r.rows[1] = r.top[:SHIFT]
    r.cols[1] = r.top[:, :SHIFT, :]
    r.corner[1] = r.top[:SHIFT, :SHIFT, :]


def activate(hidden, up):
    inner = mm(hidden, up)
    square, tanh = gelu_parts(inner)
    slope = 0.5 * (1.0 + tanh) + (0.5 * GELU_A) * inner * (1.0 - tanh * tanh) * (
        1.0 + 3.0 * GELU_B * square
    )
    return (0.5 * inner * (1.0 + tanh)).astype(BF16), slope


def prepare_kernel(layer, r):
    normed, _ = normalize(r.middle[...])
    hidden = (normed * r.gains[layer, 1:2, :]).astype(BF16)
    r.hidden_t[...] = hidden.T
    width_c = hidden.shape[1]
    for chunk in range(r.up_w.shape[1] // width_c):
        cols = slice(chunk * width_c, (chunk + 1) * width_c)
        activated, slope = activate(hidden, r.up_w[:, cols])
        r.activated_t[cols, :] = activated.T
        r.slope[:, cols] = slope.astype(BF16)


def mlp_backward_kernel(layer, mode, which, r):
    width_c = r.flat.shape[1]
    normed, factor = normalize(r.middle[...])
    gain = r.gains[layer, 1:2, :]
    prepared = hasattr(r, "slope")
    hidden = (normed * gain).astype(BF16)
    hidden_t = r.hidden_t[...] if prepared else hidden.T
    fill_windows(mode, grid_refs(r, which), r.flat)
    grad_low = r.flat[...].astype(BF16)
    forward = hasattr(r, "out")
    output = r.middle[...]
    grad_hidden = jnp.zeros(r.flat.shape, F32)
    for up_apart, down_apart in ((1, 1), (1, 0), (0, 1), (0, 0)):
        high, low = flip(r.place[0], up_apart), flip(r.place[0], down_apart)
        cols = pl.ds(pl.multiple_of((2 * high + low) * width_c, 128), width_c)
        if prepared:
            activated_t, slope = r.activated_t[cols, :], r.slope[:, cols].astype(F32)
        else:
            activated, slope = activate(hidden, r.up_w[:, cols])
            activated_t = activated.T
        if forward:
            output = output + mm(activated, r.down_w[cols, :])
        store_rows(r, down_apart, high, 1, mm(activated_t, grad_low))
        grad_inner = (mm_nt(grad_low, r.down_w[cols, :]) * slope).astype(BF16)
        store_columns(r, up_apart, low, 0, mm(hidden_t, grad_inner))
        grad_hidden = grad_hidden + mm_nt(grad_inner, r.up_w[:, cols])
    r.grad_m[...] = r.flat[...] + normalize_back(grad_hidden * gain, normed, factor)
    if forward:
        r.flat[...] = output
        width = r.out.shape[1]
        fill_grid(r.flat, r.buffer, width)
        r.out[...] = r.buffer[:, :width, :].astype(BF16)
        r.rows[1] = r.buffer[WIN - SHIFT :, :width, :].astype(BF16)
        r.cols[1] = r.buffer[:, width - SHIFT : width, :].astype(BF16)
        r.corner[1] = r.buffer[WIN - SHIFT :, width - SHIFT : width, :].astype(BF16)


def roll_out_kernel(r):
    refs = grid_refs(r, 1)
    width = r.mixed.shape[1]
    for row in range(WIN):
        for first, source, start, count in row_segments("out", refs, row, width):
            r.buffer[row, first : first + count, :] = source.astype(F32)[start : start + count, :]
    r.mixed[...] = r.buffer[:, :width, :].astype(BF16)


def collect_kernel(r):
    rows, cols = r.one0.shape[1] // 3, r.one0.shape[2]
    half = r.attend_f.shape[1]
    loads = start_copies([(r.w_qkv, r.qkv_w), (r.w_up, r.up_w)], r.load_sems)
    stores = []

    def store(value, out):
        copy = pltpu.make_async_copy(value, out, r.out_sems.at[len(stores)])
        copy.start()
        stores.append(copy)

    for layer, name in ((0, "one"), (1, "two")):
        places = []
        for index, ref in enumerate(listed(r, name)):
            core, x, z = flip(r.place[0], index >> 2), flip(r.place[1], index >> 1 & 1), index & 1
            for high in range(2):
                places.append((ref, high, 2 * core + x, flip(r.place[2], 2 * high + z)))
        for ref, high, chunk, z in places:
            first = pl.multiple_of((chunk * 4 + z) * rows, 16)
            r.down_f[layer, pl.ds(first, rows), :] = ref[high, rows : 2 * rows].astype(F32)
        store(r.down_f.at[layer], r.down.at[layer])
        for kind, full in ((0, r.up_f), (2, r.attend_f)):
            for ref, high, chunk, z in places:
                band = pl.ds(pl.multiple_of(z * rows, 16), rows)
                span = pl.ds(pl.multiple_of(chunk * cols, 128), cols)
                piece = ref[high, kind * rows : (kind + 1) * rows]
                full[layer, band, span] = piece.astype(F32)
        store(r.up_f.at[layer], r.up.at[layer])
        store(r.attend_f.at[layer, :, : 3 * cols], r.qkv.at[layer])
        store(r.attend_f.at[layer, :, 3 * cols :], r.proj.at[layer])
    heads = r.tables_grad.shape[1]
    small = r.total[3 * rows :].astype(F32)
    small = jnp.where(r.place[3] == 1, small[heads : 2 * heads], small[:heads])
    r.tables_grad[0] = small[:, :TABLE]
    r.tables_grad[1] = small[:, cols // 2 : cols // 2 + TABLE]
    wait_all(loads)
    r.wide[...] = jnp.zeros_like(r.wide)
    for layer in range(2):
        for which, weight, grad in ((0, r.qkv_w, r.attend_f), (1, r.up_w, r.up_f)):
            total = jnp.zeros((half, 128), F32)
            for first in range(0, weight.shape[2], 128):
                span = slice(first, first + 128)
                total = total + weight[layer, :, span].astype(F32) * grad[layer, :, span]
            r.wide[:half, :] = total
            line = jnp.sum(r.wide[...].T, 0, keepdims=True)[:, :half]
            gain = r.gains[layer, which : which + 1, :].astype(F32)
            r.gains_grad[layer, which : which + 1, :] = line / gain
    wait_all(stores)


VMEM = pl.BlockSpec(memory_space=pltpu.VMEM)
ANY = pl.BlockSpec(memory_space=pl.ANY)
HBM = pl.BlockSpec(memory_space=pltpu.HBM)


def listed(r, name):
    found = []
    while name + str(len(found)) in vars(r):
        found.append(getattr(r, name + str(len(found))))
    return found


def numbered(name, space, arrays):
    return {name + str(index): (space, array) for index, array in enumerate(arrays)}


def place_here():
    seq = lax.axis_index("seq")
    return (
        jnp.bitwise_and(seq, 1),
        jnp.bitwise_and(lax.shift_right_logical(seq, 1), 1),
        jnp.bitwise_and(lax.shift_right_logical(seq, 2), 3),
        lax.axis_index("fsdp"),
    )


def shape_of(*dims, dtype=BF16):
    return jax.ShapeDtypeStruct(dims, dtype)


def call(kernel, name, ins, outs, scratch, after=(), us=1, vmem=VMEM_LIMIT, spaces=None):
    names = list(ins) + [None] * len(after) + list(outs) + list(scratch)

    def body(*refs):
        named = {n: ref for n, ref in zip(names, refs) if n}
        kernel(types.SimpleNamespace(place=place_here(), **named))

    results = pl.pallas_call(
        body,
        name=name,
        out_shape=list(outs.values()),
        in_specs=[space for space, _ in ins.values()] + [ANY] * len(after),
        out_specs=spaces or [VMEM] * len(outs),
        scratch_shapes=list(scratch.values()),
        cost_estimate=pl.CostEstimate(
            flops=1000, bytes_accessed=us * BYTES_PER_US, transcendentals=0
        ),
        compiler_params=pltpu.CompilerParams(vmem_limit_bytes=vmem),
    )(*[array for _, array in ins.values()], *after)
    return types.SimpleNamespace(**dict(zip(outs, results)))


def attend_weights(weights, parts):
    ins = dict(qkv=(HBM, weights[0]), proj=(HBM, weights[1])) | numbered("a_part", HBM, parts)
    width_c = weights[1].shape[2]
    outs = dict(qkv_w=shape_of(width_c, 3 * width_c), proj_w=shape_of(width_c, width_c))
    return ins, outs, dict(a_sems=pltpu.SemaphoreType.DMA((2, 17)))


def mlp_weights(weights, parts):
    ins = dict(up=(HBM, weights[2]), down=(HBM, weights[3])) | numbered("m_part", HBM, parts)
    width_c, inner = weights[1].shape[2], weights[2].shape[2]
    outs = dict(up_w=shape_of(width_c, inner), down_w=shape_of(inner, width_c))
    return ins, outs, dict(m_sems=pltpu.SemaphoreType.DMA((2, 17)))


def whole(kept, *names):
    return {name: (VMEM, getattr(kept, name)) for name in names}


def tie(array, after):
    return pl.pallas_call(
        lambda *refs: None,
        name="tie",
        out_shape=jax.ShapeDtypeStruct(array.shape, array.dtype),
        in_specs=[ANY] * (1 + len(after)),
        out_specs=ANY,
        input_output_aliases={0: 0},
        compiler_params=pltpu.CompilerParams(vmem_limit_bytes=1024 * 1024),
    )(array, *after)


def grid_buffer(width, width_c):
    return pltpu.VMEM((WIN, -(-width // 8) * 8, width_c), F32)


def extra_rows(heads):
    return heads + -heads % 16


def pack(kernel, rows, weights, small=(), after=(), vmem=VMEM_LIMIT):
    wide = 4 * weights["proj"].shape[2] if "proj" in weights else weights["up"].shape[2]
    ins = {name: (HBM, w) for name, w in weights.items()}
    scratch = dict(sems=pltpu.SemaphoreType.DMA((7,)))
    if small:
        gains, tables = small
        extra = extra_rows(2 * tables.shape[1])
        rows += extra
        ins |= dict(gains=(HBM, gains), tables=(HBM, tables))
        scratch |= dict(
            small=pltpu.VMEM((extra, wide), F32),
            gains_v=pltpu.VMEM(gains.shape, BF16),
            tables_v=pltpu.VMEM(tables.shape, BF16),
            small_sems=pltpu.SemaphoreType.DMA((2,)),
        )
    outs = dict(out=shape_of(rows, wide))
    return call(kernel, "pack", ins, outs, scratch, after, vmem=vmem).out


def table_sums(grads, index, width_c, after=()):
    heads = grads[0].shape[0]
    rows = heads + -heads % 16
    ins = numbered("grad", VMEM, grads) | dict(index=(VMEM, index))
    scratch = dict(wide=pltpu.VMEM((rows, width_c), F32))
    outs = dict(out=shape_of(rows, width_c))
    return call(table_sums_kernel, "table_sums", ins, outs, scratch, after).out


def params(own, other, rel, heads):
    width_c = own.shape[1] // 4
    ins = dict(own=(VMEM, own), other=(VMEM, other), rel=(VMEM, rel))
    outs = dict(
        index=shape_of(SLOT, PAIR, dtype=jnp.int32),
        gains=shape_of(2, 2, width_c, dtype=F32),
        bias=shape_of(2, heads, SLOT, PAIR, dtype=F32),
    )
    scratch = dict(
        table=pltpu.VMEM((2 * heads, TABLE), F32),
        extra=pltpu.VMEM((extra_rows(heads), own.shape[1]), F32),
    )
    return call(params_kernel, "params", ins, outs, scratch)


def grid_ins(grid, edges=()):
    ins = dict(own=(VMEM, grid))
    if edges:
        ins |= {n: (VMEM, e) for n, e in zip(("rows_in", "cols_in", "corner_in"), edges)}
    return ins


def edge_outs(width, width_c):
    return dict(
        rows=shape_of(2, SHIFT, width, width_c),
        cols=shape_of(2, WIN, SHIFT, width_c),
        corner=shape_of(2, SHIFT, SHIFT, width_c),
    )


def attend_forward(layer, mode, grid, edges, gains, bias, region, weights, parts, after=()):
    width, width_c = grid.shape[1:]
    tokens = width // WIN * SLOT
    heads = width_c // HEAD
    more, made, scratch = attend_weights(weights, parts)
    ins = dict(gains=(VMEM, gains), bias=(VMEM, bias))
    ins |= grid_ins(grid, edges) | more
    if mode != "plain":
        more, also, sems = mlp_weights(weights, ())
        ins |= dict(region=(VMEM, region)) | more
        made |= also
        scratch |= sems
        scratch |= dict(
            labels=pltpu.VMEM((SIDE, 128), F32),
            same=pltpu.VMEM((SLOT, tokens), F32),
        )
    outs = dict(
        x=shape_of(tokens, width_c),
        middle=shape_of(tokens, width_c, dtype=F32),
        query=shape_of(tokens, width_c),
        keys_t=shape_of(width_c, tokens),
        values=shape_of(tokens, width_c),
        mixed_t=shape_of(width_c, tokens),
        probs=shape_of(heads, SLOT, tokens, dtype=F32),
    )
    outs |= made
    scratch |= dict(
        flat=pltpu.VMEM((tokens, width_c), F32),
        values_t=pltpu.VMEM((width_c, tokens), BF16),
        query_t=pltpu.VMEM((width_c, tokens), BF16),
        keys=pltpu.VMEM((tokens, width_c), BF16),
    )
    kernel = functools.partial(attend_forward_kernel, layer, mode)
    return call(kernel, "attend_forward", ins, outs, scratch, after, 4)


def mlp_forward(layer, middle, gains, weights, parts, top, after=()):
    tokens, width_c = middle.shape
    width = top.shape[1]
    more, made, scratch = mlp_weights(weights, parts)
    ins = dict(middle=(VMEM, middle), gains=(VMEM, gains)) | more
    ins |= dict(top=(VMEM, top))
    outs = dict(grid=shape_of(WIN, width, width_c)) | edge_outs(width, width_c) | made
    scratch |= dict(
        flat=pltpu.VMEM((tokens, width_c), F32),
        buffer=grid_buffer(width, width_c),
    )
    return call(functools.partial(mlp_forward_kernel, layer), "mlp_forward", ins, outs, scratch, after, 4)


def backward(layer, kept, mlp, grid, edges, gains, ready=None, after=()):
    tokens, width_c = kept.middle.shape
    width = grid.shape[1]
    heads = width_c // HEAD
    second = layer == 1
    ins = dict(gains=(VMEM, gains)) | grid_ins(grid, edges)
    if second:
        ins["own_two"] = ins.pop("own")
    ins |= whole(kept, "middle", "x", "query", "keys_t", "values", "probs", "qkv_w", "proj_w")
    ins |= whole(mlp, "up_w", "down_w")
    pieces = [shape_of(2, 2, kinds, 4, width_c // 8, width_c) for kinds in (1, 2, 3)]
    if second:
        outs = dict(keep=pieces[1], send=pieces[1])
    else:
        outs = dict(keep=pieces[2]) | {"send" + str(i): pieces[0] for i in range(3)}
    outs |= dict(
        grad_m=shape_of(tokens, width_c, dtype=F32),
        grad_t=shape_of(3 * width_c, tokens),
        grad_k=shape_of(tokens, width_c),
        grad_v=shape_of(tokens, width_c),
        bias_grad=shape_of(heads, SLOT, PAIR, dtype=F32),
    )
    scratch = dict(
        out_t=pltpu.VMEM((width_c, tokens), BF16),
        flat=pltpu.VMEM((tokens, width_c), F32),
    )
    if second:
        outs |= dict(out=shape_of(WIN, width, width_c), grid=shape_of(WIN, width, width_c))
        outs |= edge_outs(width, width_c)
        scratch |= dict(buffer=grid_buffer(width, width_c))
    else:
        ins |= dict(mixed_t=(VMEM, kept.mixed_t))
        ins |= {name: (VMEM, value) for name, value in vars(ready).items()}
        scratch |= sides(width_c, tokens)

    def kernel(r):
        mlp_backward_kernel(layer, "in" if second else "out", layer, r)
        attend_backward_kernel(layer, "si" if second else "sw", 2, r)

    return call(kernel, "backward", ins, outs, scratch, after, 15)


def prepare(layer, kept, mlp, gains, after=()):
    tokens, width_c = kept.middle.shape
    inner = mlp.up_w.shape[1]
    ins = dict(middle=(VMEM, kept.middle), gains=(VMEM, gains)) | whole(mlp, "up_w")
    outs = dict(
        hidden_t=shape_of(width_c, tokens),
        activated_t=shape_of(inner, tokens),
        slope=shape_of(tokens, inner),
    )
    kernel = functools.partial(prepare_kernel, layer)
    return call(kernel, "prepare", ins, outs, {}, after, 3)


def sides(width_c, tokens):
    return dict(
        left=pltpu.VMEM((2, width_c, tokens), BF16),
        right=pltpu.VMEM((4, tokens, width_c), BF16),
    )


def attend_weight_grads(layer, kept, back, gains, after=()):
    tokens, width_c = back.grad_m.shape
    ins = dict(gains=(VMEM, gains), grad_m=(VMEM, back.grad_m))
    ins |= dict(x=(VMEM, kept.x), mixed_t=(VMEM, kept.mixed_t), grad_t=(VMEM, back.grad_t))
    ins |= dict(grad_k=(VMEM, back.grad_k), grad_v=(VMEM, back.grad_v))
    pieces = shape_of(2, 2, 1, 4, width_c // 8, width_c)
    kernel = functools.partial(attend_backward_kernel, layer, "w", 0)
    outs = dict(keep=pieces, send=pieces)
    return call(kernel, "attend_weight_grads", ins, outs, sides(width_c, tokens), after, 2)


def input_grad(layer, kept, back, gains, own_two, edges, after=()):
    tokens, width_c = back.grad_m.shape
    width = own_two.shape[1]
    ins = dict(gains=(VMEM, gains), grad_m=(VMEM, back.grad_m))
    ins |= dict(grad_t=(VMEM, back.grad_t)) | whole(kept, "x", "qkv_w")
    ins |= grid_ins(own_two, edges)
    ins["own_two"] = ins.pop("own")
    outs = dict(grid_out=shape_of(WIN, width, width_c), mixed_out=shape_of(WIN, width, width_c))
    scratch = dict(
        flat=pltpu.VMEM((tokens, width_c), F32),
        buffer=grid_buffer(width, width_c),
        grid=pltpu.VMEM((WIN, width, width_c), BF16),
        mixed=pltpu.VMEM((WIN, width, width_c), BF16),
        sems=pltpu.SemaphoreType.DMA((2,)),
    )

    def kernel(r):
        roll_out_kernel(r)
        attend_backward_kernel(layer, "i", 0, r)
        wait_all(start_copies([(r.mixed, r.mixed_out), (r.grid, r.grid_out)], r.sems))

    return call(kernel, "input_grad", ins, outs, scratch, after, 3, spaces=[HBM] * 2)


def collect(one, two, total, weights, gains, tables):
    names = ("qkv", "proj", "up", "down", "gains_grad", "tables_grad")
    grads = [shape_of(*w.shape, dtype=F32) for w in (*weights, gains, tables)]
    ins = numbered("one", VMEM, one) | numbered("two", VMEM, two)
    ins |= dict(w_qkv=(HBM, weights[0]), w_up=(HBM, weights[2]), gains=(VMEM, gains))
    ins |= dict(total=(VMEM, total))
    scratch = dict(
        attend_f=pltpu.VMEM(grads[2].shape, F32),
        up_f=pltpu.VMEM(grads[2].shape, F32),
        down_f=pltpu.VMEM(grads[3].shape, F32),
        qkv_w=pltpu.VMEM(weights[0].shape, BF16),
        up_w=pltpu.VMEM(weights[2].shape, BF16),
        load_sems=pltpu.SemaphoreType.DMA((2,)),
        out_sems=pltpu.SemaphoreType.DMA((8,)),
        wide=pltpu.VMEM((256, 128), F32),
    )
    outs = dict(zip(names, grads))
    spaces = [HBM] * 4 + [VMEM] * 2
    return call(collect_kernel, "collect", ins, outs, scratch, spaces=spaces)


def per_device(
    tokens, norm_gains, w_qkv, w_proj, w_up, w_down, tables, region_ids, rel_index, cotangent
):
    width, width_c = tokens.shape[1:]
    weights = (w_qkv, w_proj, w_up, w_down)

    heads = 2 * tables.shape[1]

    rows = w_qkv.shape[1] // 2
    attend_w, mlp_w = dict(qkv=w_qkv, proj=w_proj), dict(up=w_up, down=w_down)
    mlp_piece = pack(pack_mlp_kernel, rows, mlp_w, (norm_gains, tables), (), PACK_VMEM_LIMIT)
    attend_piece = pack(
        pack_attend_kernel, rows, attend_w, after=(mlp_piece,), vmem=PACK_VMEM_LIMIT
    )
    mlp_first = exchange(mlp_piece, 0, 1)
    mlp_second = exchange(mlp_first, 2, 0)
    attend_one = share_halves(attend_piece, after=(mlp_first,))
    settings = params(mlp_piece, mlp_first, rel_index, heads)
    gains, bias, index = settings.gains, settings.bias, settings.index
    both_piece = pack(pack_both_kernel, 3 * rows, attend_w | mlp_w, after=(attend_piece,))

    one = attend_forward(
        0, "plain", tokens, (), gains, bias, None, weights, attend_one, after=(both_piece,)
    )
    mlp_one = share(mlp_first, mlp_second, after=(one.middle,))
    done = mlp_forward(0, one.middle, gains, weights, mlp_one, cotangent)
    edges = halo(done.rows, done.cols, done.corner, 1)
    parts_two = share_halves(both_piece, after=edges)
    two = attend_forward(
        1, "in", done.grid, edges, gains, bias, region_ids, weights, parts_two
    )
    back2 = backward(1, two, two, cotangent, edges, gains)
    got_m2 = exchange(back2.send, 1, 0)
    edges = halo(back2.rows, back2.cols, back2.corner, -1)
    att2 = attend_weight_grads(1, two, back2, gains)
    ready = prepare(0, one, done, gains, after=(att2.send,))
    side_two = start_side(
        (back2.keep, att2.keep),
        (got_m2, exchange(att2.send, 1, 0)),
        after=(*edges, ready.slope),
    )
    back1 = backward(
        0, one, done, back2.grid, edges, gains, ready, after=(side_two[0],)
    )
    rows = width_c // 8
    gots = [exchange(send, 1, 0) for send in (back1.send0, back1.send1, back1.send2)]
    small = table_sums((back1.bias_grad, back2.bias_grad), index, width_c)
    small = add_pair(small, exchange(small, 1, 0))
    side_one = start_sides((back1.keep,), gots, after=(small,))
    small = (small, exchange(small, 0, 1))
    face_two = start_face(side_two, after=side_one[:1])
    last = input_grad(
        0, one, back1, gains, back2.out, edges, after=side_one[:1]
    )
    total_two, _ = finish_sum(face_two, 3 * rows, halve_kernel)
    face_one = start_faces(side_one, small=small, after=(last.mixed_out,))
    pair_two = gather_pair(total_two, 3 * rows)
    total_one, _ = finish_sum(face_one, face_one[0].shape[0], halve_faces_kernel)
    pair_one = gather_pair(total_one, 3 * rows)
    sums = collect(gather(pair_one), gather(pair_two), total_one, weights, norm_gains, tables)
    return (
        last.mixed_out,
        last.grid_out,
        sums.gains_grad,
        sums.qkv,
        sums.proj,
        sums.up,
        sums.down,
        sums.tables_grad,
    )


def solution(mesh):
    return jax.shard_map(
        per_device,
        mesh=mesh,
        in_specs=(
            P("seq", "fsdp", None),
            P(None, None, "fsdp"),
            P(None, "fsdp", None),
            P(None, "fsdp", None),
            P(None, "fsdp", None),
            P(None, "fsdp", None),
            P(None, "fsdp", None),
            P("seq", "fsdp"),
            P(),
            P("seq", "fsdp", None),
        ),
        out_specs=(
            P("seq", "fsdp", None),
            P("seq", "fsdp", None),
            P(None, None, "fsdp"),
            P(None, "fsdp", None),
            P(None, "fsdp", None),
            P(None, "fsdp", None),
            P(None, "fsdp", None),
            P(None, "fsdp", None),
        ),
        check_vma=False,
    )
```

```python
import functools
import types

import jax
import jax.numpy as jnp
from jax import lax
from jax.experimental import pallas as pl
from jax.experimental.pallas import tpu as pltpu
from jax.sharding import PartitionSpec as P

WIN = 7
SHIFT = 3
TABLE = 169
SIDE = 8
SLOT = SIDE * SIDE
HEAD = 32
PAIR = 2 * SLOT
EPSILON = 1e-05
MASKED_SCORE = -1000000000.0
F32 = jnp.float32
BF16 = jnp.bfloat16
VMEM_LIMIT = 24 * 1024 * 1024
PACK_VMEM_LIMIT = 60 * 1024 * 1024
BYTES_PER_US = 3500000


def exchange(array, ds, dy):
    n, m = lax.axis_size("seq"), lax.axis_size("fsdp")
    pairs = [(s * m + y, (s ^ ds) * m + (y ^ dy)) for s in range(n) for y in range(m)]
    return lax.ppermute(array, ("seq", "fsdp"), pairs)


def take_from(array, ds, dy):
    n, m = lax.axis_size("seq"), lax.axis_size("fsdp")
    pairs = [((s + ds) % n * m + (y + dy) % m, s * m + y) for s in range(n) for y in range(m)]
    return lax.ppermute(array, ("seq", "fsdp"), pairs)


def halo(near_rows, near_cols, corner, step):
    return (
        take_from(near_rows, step, 0),
        take_from(near_cols, 0, step),
        take_from(corner, step, step),
    )


def share_halves(piece, after=()):
    first = exchange(piece, 0, 1)
    if after:
        first = tie(first, after)
    return (first, exchange(first, 1, 0))


def share(first, second, after):
    second = tie(second, after)
    return (first, second, exchange(first, 1, 0), exchange(second, 1, 0))


def add(*terms):
    total = terms[0].astype(F32)
    for term in terms[1:]:
        total = total + term.astype(F32)
    return total


def sum_higher(value):
    step = 16
    while step < lax.axis_size("seq"):
        value = add(value, exchange(value, step, 0)).astype(value.dtype)
        step *= 2
    return value


def start_side(keeps, gots, after=()):
    kinds = sum(keep.shape[2] for keep in keeps)
    out = shape_of(2, kinds, *keeps[0].shape[3:])
    ins = numbered("keep", VMEM, keeps) | numbered("got", VMEM, gots)
    r = call(add_side_kernel, "add_side", ins, dict(own=out, other=out), {}, after)
    return r.own, exchange(r.other, 0, 1)


def start_sides(keeps, gots, after=()):
    kinds = sum(keep.shape[2] for keep in keeps)
    out = shape_of(2, kinds, 2, *keeps[0].shape[4:])
    ins = numbered("keep", VMEM, keeps) | numbered("got", VMEM, gots)
    outs = dict(own0=out, own1=out, other0=out, other1=out)
    r = call(add_sides_kernel, "add_sides", ins, outs, {}, after)
    return r.own0, exchange(r.other0, 0, 1), r.own1, exchange(r.other1, 2, 0)


def add_pair(value, other):
    ins = numbered("part", VMEM, (value, other))
    return call(add_all_kernel, "add_all", ins, dict(out=shape_of(*value.shape)), {}).out


def start_face(parts, after=()):
    _, kinds, _, rows, cols = parts[0].shape
    out = shape_of(kinds * 2 * rows, cols)
    outs = {"out" + str(i): out for i in range(4)}
    r = call(add_face_kernel, "add_face", numbered("part", VMEM, parts), outs, {}, after)
    return r.out0, exchange(r.out3, 6, 0), exchange(r.out2, 2, 0), exchange(r.out1, 4, 0)


def start_faces(parts, after=(), small=()):
    _, kinds, _, rows, cols = parts[0].shape
    extra = small[0].shape[0] if small else 0
    first, second = shape_of(kinds * rows + extra, cols), shape_of(kinds * rows, cols)
    ins = numbered("part", VMEM, parts) | numbered("small", VMEM, small)
    outs = dict(out0=first, out1=second, side0=first, side1=second, corner0=first, corner1=second)
    outs |= dict(low=shape_of(2 * kinds * rows + extra, cols))
    r = call(add_faces_kernel, "add_faces", ins, outs, {}, after)
    corners = (exchange(r.corner0, 6, 0), exchange(r.corner1, 4, 1))
    low = exchange(r.low, 4, 0)
    return r.out0, r.out1, exchange(r.side0, 2, 0), exchange(r.side1, 0, 1), *corners, low


def finish_sum(terms, rows, kernel, after=()):
    out = shape_of(rows, terms[0].shape[1])
    r = call(kernel, "halve", numbered("term", VMEM, terms), dict(own=out, other=out), {}, after)
    got = exchange(r.other, 8, 0)
    return sum_higher(add_pair(r.own, got)), got


def gather_pair(total, rows, after=()):
    ins = dict(own=(VMEM, total), other=(VMEM, exchange(total, 8, 0)))
    out = shape_of(2, rows, total.shape[1])
    return call(stack_kernel, "stack", ins, dict(out=out), {}, after).out


def gather(pair, after=()):
    here = [pair, exchange(pair, 4, 0), exchange(pair, 2, 0), exchange(pair, 6, 0)]
    if after:
        here = [tie(part, after) for part in here]
    return here + [exchange(part, 1, 0) for part in here]


def flip(index, bits):
    return jnp.bitwise_xor(index, bits)


def mlp_pairs(layer, spot, up, down, out):
    count, width_c = out.shape[0] // 2, down.shape[2]
    start = pl.multiple_of(spot * count, 16)
    pairs = [(up.at[layer, pl.ds(start, count), :], out.at[:count])]
    for index in range(4):
        first = pl.multiple_of((spot * 4 + index) * count, 16)
        cols = slice(index * width_c, (index + 1) * width_c)
        pairs.append((down.at[layer, pl.ds(first, count), :], out.at[count:, cols]))
    return pairs


def attend_pairs(layer, spot, qkv, proj, out):
    rows, width_c = out.shape[0], proj.shape[2]
    start = pl.multiple_of(spot * rows, 16)
    return [
        (qkv.at[layer, pl.ds(start, rows), :], out.at[:, : 3 * width_c]),
        (proj.at[layer, pl.ds(start, rows), :], out.at[:, 3 * width_c :]),
    ]


def pack_mlp_kernel(r):
    rows = r.up.shape[1] // 2
    spot = 2 * r.place[0] + r.place[1]
    copies = start_copies(mlp_pairs(0, spot, r.up, r.down, r.out.at[:rows]), r.sems)
    r.small[...] = jnp.zeros_like(r.small)
    heads = r.tables.shape[1]
    half = r.gains.shape[2]
    for index in range(2):
        r.small[index * heads : (index + 1) * heads, :TABLE] = r.tables[index].astype(F32)
        r.small[2 * index : 2 * index + 2, 256 : 256 + half] = r.gains[index].astype(F32)
    r.out[rows:] = r.small[...].astype(BF16)
    wait_all(copies)


def pack_attend_kernel(r):
    wait_all(start_copies(attend_pairs(0, r.place[0], r.qkv, r.proj, r.out), r.sems))


def pack_both_kernel(r):
    rows = r.qkv.shape[1] // 2
    pairs = attend_pairs(1, r.place[0], r.qkv, r.proj, r.out.at[:rows])
    pairs += mlp_pairs(1, r.place[0], r.up, r.down, r.out.at[rows:])
    wait_all(start_copies(pairs, r.sems))


def chosen(index, key):
    line = jnp.broadcast_to(index[key : key + 1, :], (TABLE, index.shape[1]))
    entries = lax.broadcasted_iota(jnp.int32, line.shape, 0)
    return jnp.where(line == entries, 1.0, 0.0).astype(BF16)


def table_sums_kernel(r):
    heads = r.grad0.shape[0]
    total = jnp.zeros((2 * heads, TABLE), F32)
    for key in range(SLOT):
        pair = jnp.concatenate([r.grad0[:, key, :], r.grad1[:, key, :]], axis=0)
        total = total + mm_nt(pair.astype(BF16), chosen(r.index, key))
    r.wide[...] = jnp.zeros_like(r.wide)
    half = r.out.shape[1] // 2
    r.wide[:heads, :TABLE] = total[:heads]
    r.wide[:heads, half : half + TABLE] = total[heads:]
    r.out[...] = r.wide[...].astype(BF16)


def slots(rows, count):
    row = jnp.bitwise_and(lax.broadcasted_iota(jnp.int32, (rows, count), 0), SLOT - 1)
    token = lax.broadcasted_iota(jnp.int32, (rows, count), 1)
    at = token
    for side in range(1, WIN):
        at = at + jnp.where(token >= side * WIN, 1, 0)
    return jnp.where(row == at, 1.0, 0.0).astype(BF16)


def is_token(shape, axis):
    place = jnp.bitwise_and(lax.broadcasted_iota(jnp.int32, shape, axis), SLOT - 1)
    return (place < WIN * SIDE) & (jnp.bitwise_and(place, SIDE - 1) < WIN)


def spread_index(rel):
    count = rel.shape[0]
    keys = mm_nt(slots(SLOT, count), rel.astype(F32).astype(BF16))
    pairs = mm_nt(keys.astype(BF16), slots(PAIR, count))
    real = is_token(pairs.shape, 0) & is_token(pairs.shape, 1)
    return jnp.where(real, (pairs + 0.5).astype(jnp.int32), -1)


def same_label(r):
    r.labels[...] = jnp.full_like(r.labels, -1.0)
    for window in range(r.region.shape[1] // WIN):
        r.labels[:WIN, :WIN] = r.region[:, window * WIN : window * WIN + WIN].astype(F32)
        block = r.labels[:, :SIDE].astype(BF16)
        lane = lax.broadcasted_iota(jnp.int32, (SIDE, SLOT), 1)
        row = lax.broadcasted_iota(jnp.int32, (SIDE, SLOT), 0)
        repeat = jnp.where(jnp.bitwise_and(lane, SIDE - 1) == row, 1.0, 0.0).astype(BF16)
        own = (lane >= row * SIDE) & (lane < row * SIDE + SIDE)
        line = jnp.sum(jnp.where(own, mm(block, repeat), 0.0), 0, keepdims=True)
        wide = jnp.broadcast_to(line, (SLOT, SLOT))
        diagonal_only = lax.broadcasted_iota(jnp.int32, wide.shape, 0) == (
            lax.broadcasted_iota(jnp.int32, wide.shape, 1)
        )
        column = jnp.sum(jnp.where(diagonal_only, wide, 0.0), 1, keepdims=True)
        r.same[:, window * SLOT : window * SLOT + SLOT] = jnp.where(wide == column, 1.0, 0.0)


def params_kernel(r):
    half = r.gains.shape[2] // 2
    heads = r.bias.shape[1] // 2
    rows = r.own.shape[0] - r.extra.shape[0]
    flipped = r.place[3] == 1
    r.extra[...] = jnp.where(flipped, r.other[rows:].astype(F32), r.own[rows:].astype(F32))
    for part in range(2):
        for index in range(2):
            r.gains[index, :, part * half : (part + 1) * half] = r.extra[
                2 * index : 2 * index + 2, 256 : 256 + half
            ]
            start = (2 * index + part) * heads
            r.table[start : start + heads, :] = r.extra[index * heads : (index + 1) * heads, :TABLE]
        if part == 0:
            r.extra[...] = jnp.where(
                flipped, r.own[rows:].astype(F32), r.other[rows:].astype(F32)
            )
    r.index[...] = spread_index(r.rel[...])
    table = r.table[...].astype(BF16)
    for key in range(SLOT):
        line = mm(table, chosen(r.index, key))
        r.bias[0, :, key, :] = line[: 2 * heads]
        r.bias[1, :, key, :] = line[2 * heads :]


def start_copies(pairs, sems):
    copies = [
        pltpu.make_async_copy(source, target, sems.at[index])
        for index, (source, target) in enumerate(pairs)
    ]
    for copy in copies:
        copy.start()
    return copies


def fetch(place, layer, own, parts, pick, full, sems):
    half = full.shape[0] // 2
    rows = half // len(parts)
    y = place[3]
    pairs = [(own.at[layer], full.at[pl.ds(pl.multiple_of(y * half, 16), half)])]
    core, x = place[0], place[1]
    spots = [core, flip(core, 1)]
    if len(parts) == 4:
        spots = [2 * flip(core, index // 2) + flip(x, index % 2) for index in range(4)]
    for spot, part in zip(spots, parts):
        pieces = pick(part)
        count = rows // len(pieces)
        for index, piece in enumerate(pieces):
            start = pl.multiple_of((1 - y) * half + spot * rows + index * count, 16)
            pairs.append((piece, full.at[pl.ds(start, count)]))
    return start_copies(pairs, sems)


def fetch_attend(place, layer, own, parts, qkv_w, proj_w, sems):
    rows = own[0].shape[1] // 2
    wide = qkv_w.shape[1]

    def qkv(part):
        return [part.at[:rows, :wide]]

    def proj(part):
        return [part.at[:rows, wide:]]

    return [
        fetch(place, layer, own[0], parts, qkv, qkv_w, sems.at[0]),
        fetch(place, layer, own[1], parts, proj, proj_w, sems.at[1]),
    ]


def fetch_mlp(place, layer, own, parts, up_w, down_w, sems):
    rows = own[0].shape[1] // len(parts)
    first = parts[0].shape[0] - 2 * rows if len(parts) == 2 else 0
    width_c = up_w.shape[0]

    def up(part):
        return [part.at[first : first + rows]]

    def down(part):
        band = slice(first + rows, first + 2 * rows)
        return [part.at[band, i * width_c : (i + 1) * width_c] for i in range(4)]

    return [
        fetch(place, layer, own[0], parts, up, up_w, sems.at[0]),
        fetch(place, layer, own[1], parts, down, down_w, sems.at[1]),
    ]


def add_refs(refs):
    total = refs[0][...].astype(F32)
    for ref in refs[1:]:
        total = total + ref[...].astype(F32)
    return total


def add_small(r):
    return add_refs(listed(r, "small")).astype(BF16)


def kinds_of(refs):
    return [(ref, kind) for ref in refs for kind in range(ref.shape[2])]


def add_side_kernel(r):
    pairs = zip(kinds_of(listed(r, "keep")), kinds_of(listed(r, "got")))
    for index, ((keep, first), (got, second)) in enumerate(pairs):
        for y, out in enumerate((r.own, r.other)):
            for x in range(2):
                value = keep[y, x, first].astype(F32) + got[y, x, second].astype(F32)
                out[x, index] = value.astype(BF16)


def add_sides_kernel(r):
    pairs = zip(kinds_of(listed(r, "keep")), kinds_of(listed(r, "got")))
    for index, ((keep, first), (got, second)) in enumerate(pairs):
        for apart, outs in enumerate(((r.own0, r.own1), (r.other0, r.other1))):
            for along in range(2):
                for low in range(2):
                    for high, (y, x) in enumerate(((apart, along), (along, apart))):
                        z = 2 * high + low
                        value = keep[y, x, first, z].astype(F32) + got[y, x, second, z].astype(F32)
                        outs[high][along, index, low] = value.astype(BF16)


def add_face_kernel(r):
    _, kinds, _, rows, _ = r.part0.shape
    for index, out in enumerate(listed(r, "out")):
        x, z = index >> 1, index & 1
        for kind in range(kinds):
            for high in range(2):
                at = (x, kind, 2 * high + z)
                first = (kind * 2 + high) * rows
                value = r.part0[at].astype(F32) + r.part1[at].astype(F32)
                out[first : first + rows, :] = value.astype(BF16)


def add_faces_kernel(r):
    _, kinds, _, rows, _ = r.part0.shape
    size = kinds * rows
    for kind in range(kinds):
        band = slice(kind * rows, (kind + 1) * rows)
        later = slice(r.low.shape[0] - size + kind * rows, r.low.shape[0] - size + (kind + 1) * rows)
        for order, (own, got) in enumerate(((r.part0, r.part1), (r.part2, r.part3))):
            sums = [
                [add_refs((own.at[a, kind, z], got.at[a, kind, z])).astype(BF16) for z in range(2)]
                for a in range(2)
            ]
            outs = ((r.out0, r.side0, r.corner0), (r.out1, r.side1, r.corner1))[order]
            outs[0][band, :] = sums[0][0]
            outs[1][band, :] = sums[1][0]
            outs[2][band, :] = sums[1][1]
            r.low[later if order else band, :] = sums[0][1]
    if hasattr(r, "small0"):
        small = add_small(r)
        extra = slice(size, size + small.shape[0])
        for out in (r.out0, r.side0, r.corner0, r.low):
            out[extra, :] = small


def halve_kernel(r):
    terms = listed(r, "term")
    kinds = 3
    rows = r.own.shape[0] // kinds
    for high, out in enumerate((r.own, r.other)):
        for kind in range(kinds):
            first = (kind * 2 + high) * rows
            value = add_refs([term.at[first : first + rows, :] for term in terms])
            out[kind * rows : (kind + 1) * rows, :] = value.astype(BF16)


def halve_faces_kernel(r):
    own0, own1, side0, side1, corner0, corner1, low = listed(r, "term")
    size, first = own1.shape[0], own0.shape[0]
    r.own[...] = add_refs((own0, side0, corner0, low.at[:first])).astype(BF16)
    r.other[:size, :] = add_refs((own1, side1, corner1, low.at[first:])).astype(BF16)
    if first > size:
        r.other[size:, :] = r.own[size:, :]


def add_all_kernel(r):
    r.out[...] = add_refs(listed(r, "part")).astype(BF16)


def stack_kernel(r):
    rows = r.out.shape[1]
    r.out[0] = r.own[:rows, :]
    r.out[1] = r.other[:rows, :]


def wait_all(copies):
    for copy in copies:
        copy.wait()


def row_segments(mode, refs, row, width):
    if mode == "plain":
        return [(0, refs[0][row], 0, width)]
    own, rows, cols, corner = refs
    rest = width - SHIFT
    if mode == "in":
        if row < WIN - SHIFT:
            return [
                (0, own[row + SHIFT], SHIFT, rest),
                (rest, cols[row + SHIFT], 0, SHIFT),
            ]
        at = row - (WIN - SHIFT)
        return [(0, rows[at], SHIFT, rest), (rest, corner[at], 0, SHIFT)]
    if row >= SHIFT:
        return [(0, cols[row - SHIFT], 0, SHIFT), (SHIFT, own[row - SHIFT], 0, rest)]
    return [(0, corner[row], 0, SHIFT), (SHIFT, rows[row], 0, rest)]


def fill_windows(mode, refs, out):
    width = refs[0].shape[1]
    out[...] = jnp.zeros_like(out)
    for row in range(WIN):
        for first, source, start, count in row_segments(mode, refs, row, width):
            source = source.astype(F32)
            for window in range(width // WIN):
                low = max(first, window * WIN)
                high = min(first + count, window * WIN + WIN)
                if low < high:
                    spot = window * SLOT + row * SIDE + low - window * WIN
                    begin = start + low - first
                    out[spot : spot + high - low, :] = source[begin : begin + high - low, :]


def fill_grid(source, buffer, width):
    for row in range(WIN):
        for window in range(width // WIN):
            spot = window * SLOT + row * SIDE
            buffer[row, window * WIN : window * WIN + WIN, :] = source[spot : spot + WIN, :]


def normalize(values):
    centred = values - jnp.mean(values, -1, keepdims=True)
    factor = lax.rsqrt(jnp.mean(centred * centred, -1, keepdims=True) + EPSILON)
    return centred * factor, factor


def normalize_back(grad_norm, normed, factor):
    spread = jnp.mean(grad_norm * normed, -1, keepdims=True)
    return factor * (grad_norm - jnp.mean(grad_norm, -1, keepdims=True) - normed * spread)


def mm(left, right):
    return lax.dot_general(left, right, (((1,), (0,)), ((), ())), preferred_element_type=F32)


def mm_nt(left, right):
    return lax.dot_general(left, right, (((1,), (1,)), ((), ())), preferred_element_type=F32)


def only_head(group, which):
    rows = lax.broadcasted_iota(jnp.int32, group.shape, 0)
    inside = (rows >= which * HEAD) & (rows < (which + 1) * HEAD)
    return jnp.where(inside, group, jnp.zeros_like(group))


def by_head(group, axis):
    place = lax.broadcasted_iota(jnp.int32, group.shape, axis)
    copies = []
    for head in range(4):
        inside = (place >= head * HEAD) & (place < (head + 1) * HEAD)
        copies.append(jnp.where(inside, group, jnp.zeros_like(group)))
    return jnp.concatenate(copies, axis=1 - axis)


def diagonal(block):
    lanes = lax.broadcasted_iota(jnp.int32, (SLOT, PAIR), 1)
    return jnp.where(lanes < SLOT, block[:SLOT], block[SLOT:])


def spread_diagonal(packed):
    lanes = lax.broadcasted_iota(jnp.int32, (SLOT, PAIR), 1)
    low = jnp.where(lanes < SLOT, packed, 0.0)
    high = jnp.where(lanes < SLOT, 0.0, packed)
    return jnp.concatenate([low, high], axis=0).astype(BF16)


def target(r, apart, kind):
    if not apart:
        return r.keep, kind
    if hasattr(r, "send"):
        return r.send, kind
    return listed(r, "send")[kind], 0


def store_columns(r, apart, x, kind, value):
    rows = value.shape[0] // 8
    out, kind = target(r, apart, kind)
    value = value.astype(BF16)
    for y in range(2):
        for z in range(4):
            first = (y * 4 + z) * rows
            at = (flip(r.place[3], y), flip(r.place[1], x), kind, flip(r.place[2], z))
            out[at] = value[first : first + rows]


def store_rows(r, apart, y, kind, value):
    rows = value.shape[0] // 8
    out, kind = target(r, apart, kind)
    value = value.astype(BF16)
    for x in range(2):
        for z in range(4):
            first = (x * 4 + z) * rows
            at = (flip(r.place[3], y), flip(r.place[1], x), kind, flip(r.place[2], z))
            out[at] = value[first : first + rows]


def grid_refs(r, which):
    if not hasattr(r, "rows_in"):
        return [r.own]
    return [r.own if which == 0 else r.own_two] + [
        edge.at[which] for edge in (r.rows_in, r.cols_in, r.corner_in)
    ]


def attend_forward_kernel(layer, mode, r):
    width_c = r.flat.shape[1]
    heads = width_c // HEAD
    copies = fetch_attend(
        r.place, layer, (r.qkv, r.proj), listed(r, "a_part"), r.qkv_w, r.proj_w, r.a_sems
    )
    if hasattr(r, "up"):
        parts = listed(r, "a_part")
        copies += fetch_mlp(r.place, layer, (r.up, r.down), parts, r.up_w, r.down_w, r.m_sems)
    fill_windows(mode, grid_refs(r, 0), r.flat)
    r.x[...] = r.flat[...].astype(BF16)
    normed, _ = normalize(r.flat[...])
    hidden = (normed * r.gains[layer, 0:1, :]).astype(BF16)
    wait_all(copies[0])
    query = (mm(hidden, r.qkv_w[:, :width_c]) * HEAD ** (-0.5)).astype(BF16)
    r.query[...] = query
    r.query_t[...] = query.T
    r.keys[...] = mm(hidden, r.qkv_w[:, width_c : 2 * width_c]).astype(BF16)
    r.keys_t[...] = r.keys[...].T
    r.values[...] = mm(hidden, r.qkv_w[:, 2 * width_c :]).astype(BF16)
    r.values_t[...] = r.values[...].T
    if mode == "plain":
        meet = is_token((SLOT, PAIR), 0)
    else:
        same_label(r)
    for head in range(heads):
        group = slice(head // 4 * 128, head // 4 * 128 + 128)
        rows = slice(head * HEAD, head * HEAD + HEAD)
        for pair in range(r.flat.shape[0] // PAIR):
            span = slice(pair * PAIR, pair * PAIR + PAIR)
            raw = mm(r.keys[span, group], only_head(r.query_t[group, span], head % 4))
            if mode != "plain":
                meet = r.same[:, span] > 0.5
            scores = jnp.where(meet, diagonal(raw) + r.bias[layer, head], MASKED_SCORE)
            weighted = jnp.exp(scores - jnp.max(scores, 0, keepdims=True))
            attention = weighted / jnp.sum(weighted, 0, keepdims=True)
            r.probs[head, :, span] = attention
            r.mixed_t[rows, span] = mm(r.values_t[rows, span], spread_diagonal(attention)).astype(
                BF16
            )
    wait_all(copies[1])
    r.middle[...] = r.flat[...] + mm(r.mixed_t[...].T, r.proj_w[...])
    for copy in copies[2:]:
        wait_all(copy)


def attend_backward_kernel(layer, parts, kind, r):
    width_c = r.x.shape[1]
    heads = width_c // HEAD
    normed, factor = normalize(r.x[...].astype(F32))
    gain = r.gains[layer, 0:1, :]
    attended = r.grad_m[...].astype(BF16)
    if "s" in parts:
        r.out_t[...] = mm_nt(r.proj_w[...], attended).astype(BF16)
        out = r.out_t[...].T
        for first in range(0, heads, 4):
            group = slice(first * HEAD, (first + 4) * HEAD)
            totals = [jnp.zeros((SLOT, PAIR), F32)] * 4
            for pair in range(r.x.shape[0] // PAIR):
                span = slice(pair * PAIR, pair * PAIR + PAIR)
                raw = mm(r.values[span, group], by_head(r.out_t[group, span], 0))
                spread_p, spread_s = [], []
                for head in range(4):
                    attention = r.probs[first + head, :, span]
                    grad_p = diagonal(raw[:, head * PAIR : (head + 1) * PAIR])
                    grad_s = attention * (
                        grad_p - jnp.sum(grad_p * attention, 0, keepdims=True)
                    )
                    totals[head] = totals[head] + grad_s
                    spread_p.append(spread_diagonal(attention))
                    spread_s.append(spread_diagonal(grad_s))
                grad_q = mm(by_head(r.keys_t[group, span], 0), jnp.concatenate(spread_s, axis=0))
                r.grad_t[group, span] = (grad_q * HEAD ** (-0.5)).astype(BF16)
                query = r.query[span, group]
                grad_k = mm(jnp.concatenate(spread_s, axis=1), by_head(query, 1))
                r.grad_k[span, group] = grad_k.astype(BF16)
                grad_v = mm(jnp.concatenate(spread_p, axis=1), by_head(out[span, group], 1))
                r.grad_v[span, group] = grad_v.astype(BF16)
            for head in range(4):
                r.bias_grad[first + head] = totals[head]
        r.grad_t[width_c : 2 * width_c, :] = r.grad_k[...].T
        r.grad_t[2 * width_c :, :] = r.grad_v[...].T
    if "w" in parts:
        r.left[0] = (normed * gain).astype(BF16).T
        r.left[1] = r.mixed_t[...]
        r.right[0] = r.grad_t[:width_c, :].T
        r.right[1] = r.grad_k[...]
        r.right[2] = r.grad_v[...]
        r.right[3] = attended
        for apart in (1, 0):
            for x in range(2):
                chunk = 2 * flip(r.place[0], apart) + x
                left = r.left[(chunk == 3).astype(jnp.int32)]
                store_columns(r, apart, x, kind, mm(left, r.right[chunk]))
    if "i" in parts:
        grad_hidden = mm(r.qkv_w[...], r.grad_t[...]).T
        r.flat[...] = r.grad_m[...] + normalize_back(grad_hidden * gain, normed, factor)
        width = r.grid.shape[1]
        fill_grid(r.flat, r.buffer, width)
        r.grid[...] = r.buffer[:, :width, :].astype(BF16)
        if hasattr(r, "rows"):
            r.rows[0] = r.buffer[WIN - SHIFT :, :width, :].astype(BF16)
            r.cols[0] = r.buffer[:, width - SHIFT : width, :].astype(BF16)
            r.corner[0] = r.buffer[WIN - SHIFT :, width - SHIFT : width, :].astype(BF16)


GELU_A = 0.7978845608028654
GELU_B = 0.044715


def gelu_parts(inner):
    square = inner * inner
    tanh = jnp.tanh(GELU_A * (inner * (1.0 + GELU_B * square)))
    return square, tanh


def mlp_forward_kernel(layer, r):
    width_c = r.flat.shape[1]
    copies = fetch_mlp(
        r.place, layer, (r.up, r.down), listed(r, "m_part"), r.up_w, r.down_w, r.m_sems
    )
    normed, _ = normalize(r.middle[...])
    hidden = (normed * r.gains[layer, 1:2, :]).astype(BF16)
    output = r.middle[...]
    wait_all(copies[0])
    wait_all(copies[1])
    for chunk in range(r.up_w.shape[1] // width_c):
        cols = slice(chunk * width_c, (chunk + 1) * width_c)
        inner = mm(hidden, r.up_w[:, cols])
        _, tanh = gelu_parts(inner)
        output = output + mm((0.5 * inner * (1.0 + tanh)).astype(BF16), r.down_w[cols, :])
    r.flat[...] = output
    width = r.grid.shape[1]
    fill_grid(r.flat, r.buffer, width)
    r.grid[...] = r.buffer[:, :width, :].astype(BF16)
    r.rows[0] = r.buffer[:SHIFT, :width, :].astype(BF16)
    r.cols[0] = r.buffer[:, :SHIFT, :].astype(BF16)
    r.corner[0] = r.buffer[:SHIFT, :SHIFT, :].astype(BF16)
    top = r.top[...].astype(F32)
    r.rows[1] = top[:SHIFT].astype(BF16)
    r.cols[1] = top[:, :SHIFT, :].astype(BF16)
    r.corner[1] = top[:SHIFT, :SHIFT, :].astype(BF16)


def activate(hidden, up):
    inner = mm(hidden, up)
    square, tanh = gelu_parts(inner)
    slope = 0.5 * (1.0 + tanh) + (0.5 * GELU_A) * inner * (1.0 - tanh * tanh) * (
        1.0 + 3.0 * GELU_B * square
    )
    return (0.5 * inner * (1.0 + tanh)).astype(BF16), slope


def prepare_kernel(layer, r):
    normed, _ = normalize(r.middle[...])
    hidden = (normed * r.gains[layer, 1:2, :]).astype(BF16)
    r.hidden_t[...] = hidden.T
    width_c = hidden.shape[1]
    for chunk in range(r.up_w.shape[1] // width_c):
        cols = slice(chunk * width_c, (chunk + 1) * width_c)
        activated, slope = activate(hidden, r.up_w[:, cols])
        r.activated_t[cols, :] = activated.T
        r.slope[:, cols] = slope.astype(BF16)


def mlp_backward_kernel(layer, mode, which, r):
    width_c = r.flat.shape[1]
    normed, factor = normalize(r.middle[...])
    gain = r.gains[layer, 1:2, :]
    prepared = hasattr(r, "slope")
    hidden = (normed * gain).astype(BF16)
    hidden_t = r.hidden_t[...] if prepared else hidden.T
    fill_windows(mode, grid_refs(r, which), r.flat)
    grad_low = r.flat[...].astype(BF16)
    forward = hasattr(r, "out")
    output = r.middle[...]
    grad_hidden = jnp.zeros(r.flat.shape, F32)
    for up_apart, down_apart in ((1, 1), (1, 0), (0, 1), (0, 0)):
        high, low = flip(r.place[0], up_apart), flip(r.place[0], down_apart)
        cols = pl.ds(pl.multiple_of((2 * high + low) * width_c, 128), width_c)
        if prepared:
            activated_t, slope = r.activated_t[cols, :], r.slope[:, cols].astype(F32)
        else:
            activated, slope = activate(hidden, r.up_w[:, cols])
            activated_t = activated.T
        if forward:
            output = output + mm(activated, r.down_w[cols, :])
        store_rows(r, down_apart, high, 1, mm(activated_t, grad_low))
        grad_inner = (mm_nt(grad_low, r.down_w[cols, :]) * slope).astype(BF16)
        store_columns(r, up_apart, low, 0, mm(hidden_t, grad_inner))
        grad_hidden = grad_hidden + mm_nt(grad_inner, r.up_w[:, cols])
    r.grad_m[...] = r.flat[...] + normalize_back(grad_hidden * gain, normed, factor)
    if forward:
        r.flat[...] = output
        width = r.out.shape[1]
        fill_grid(r.flat, r.buffer, width)
        r.out[...] = r.buffer[:, :width, :].astype(BF16)
        r.rows[1] = r.buffer[WIN - SHIFT :, :width, :].astype(BF16)
        r.cols[1] = r.buffer[:, width - SHIFT : width, :].astype(BF16)
        r.corner[1] = r.buffer[WIN - SHIFT :, width - SHIFT : width, :].astype(BF16)


def roll_out_kernel(r):
    refs = grid_refs(r, 1)
    width = r.mixed.shape[1]
    for row in range(WIN):
        for first, source, start, count in row_segments("out", refs, row, width):
            r.buffer[row, first : first + count, :] = source.astype(F32)[start : start + count, :]
    r.mixed[...] = r.buffer[:, :width, :].astype(BF16)


def collect_kernel(r):
    rows, cols = r.one0.shape[1] // 3, r.one0.shape[2]
    half = r.attend_f.shape[1]
    loads = start_copies([(r.w_qkv, r.qkv_w), (r.w_up, r.up_w)], r.load_sems)
    stores = []

    def store(value, out):
        copy = pltpu.make_async_copy(value, out, r.out_sems.at[len(stores)])
        copy.start()
        stores.append(copy)

    for layer, name in ((0, "one"), (1, "two")):
        places = []
        for index, ref in enumerate(listed(r, name)):
            core, x, z = flip(r.place[0], index >> 2), flip(r.place[1], index >> 1 & 1), index & 1
            for high in range(2):
                places.append((ref, high, 2 * core + x, flip(r.place[2], 2 * high + z)))
        for ref, high, chunk, z in places:
            first = pl.multiple_of((chunk * 4 + z) * rows, 16)
            r.down_f[layer, pl.ds(first, rows), :] = ref[high, rows : 2 * rows].astype(F32)
        store(r.down_f.at[layer], r.down.at[layer])
        for kind, full in ((0, r.up_f), (2, r.attend_f)):
            for ref, high, chunk, z in places:
                band = pl.ds(pl.multiple_of(z * rows, 16), rows)
                span = pl.ds(pl.multiple_of(chunk * cols, 128), cols)
                piece = ref[high, kind * rows : (kind + 1) * rows]
                full[layer, band, span] = piece.astype(F32)
        store(r.up_f.at[layer], r.up.at[layer])
        store(r.attend_f.at[layer, :, : 3 * cols], r.qkv.at[layer])
        store(r.attend_f.at[layer, :, 3 * cols :], r.proj.at[layer])
    heads = r.tables_grad.shape[1]
    small = r.total[3 * rows :].astype(F32)
    small = jnp.where(r.place[3] == 1, small[heads : 2 * heads], small[:heads])
    r.tables_grad[0] = small[:, :TABLE]
    r.tables_grad[1] = small[:, cols // 2 : cols // 2 + TABLE]
    wait_all(loads)
    r.wide[...] = jnp.zeros_like(r.wide)
    for layer in range(2):
        for which, weight, grad in ((0, r.qkv_w, r.attend_f), (1, r.up_w, r.up_f)):
            total = jnp.zeros((half, 128), F32)
            for first in range(0, weight.shape[2], 128):
                span = slice(first, first + 128)
                total = total + weight[layer, :, span].astype(F32) * grad[layer, :, span]
            r.wide[:half, :] = total
            line = jnp.sum(r.wide[...].T, 0, keepdims=True)[:, :half]
            gain = r.gains[layer, which : which + 1, :].astype(F32)
            r.gains_grad[layer, which : which + 1, :] = line / gain
    wait_all(stores)


VMEM = pl.BlockSpec(memory_space=pltpu.VMEM)
ANY = pl.BlockSpec(memory_space=pl.ANY)
HBM = pl.BlockSpec(memory_space=pltpu.HBM)


def listed(r, name):
    found = []
    while name + str(len(found)) in vars(r):
        found.append(getattr(r, name + str(len(found))))
    return found


def numbered(name, space, arrays):
    return {name + str(index): (space, array) for index, array in enumerate(arrays)}


def place_here():
    seq = lax.axis_index("seq")
    return (
        jnp.bitwise_and(seq, 1),
        jnp.bitwise_and(lax.shift_right_logical(seq, 1), 1),
        jnp.bitwise_and(lax.shift_right_logical(seq, 2), 3),
        lax.axis_index("fsdp"),
    )


def shape_of(*dims, dtype=BF16):
    return jax.ShapeDtypeStruct(dims, dtype)


def call(kernel, name, ins, outs, scratch, after=(), us=1, vmem=VMEM_LIMIT, spaces=None):
    names = list(ins) + [None] * len(after) + list(outs) + list(scratch)

    def body(*refs):
        named = {n: ref for n, ref in zip(names, refs) if n}
        kernel(types.SimpleNamespace(place=place_here(), **named))

    results = pl.pallas_call(
        body,
        name=name,
        out_shape=list(outs.values()),
        in_specs=[space for space, _ in ins.values()] + [ANY] * len(after),
        out_specs=spaces or [VMEM] * len(outs),
        scratch_shapes=list(scratch.values()),
        cost_estimate=pl.CostEstimate(
            flops=1000, bytes_accessed=us * BYTES_PER_US, transcendentals=0
        ),
        compiler_params=pltpu.CompilerParams(vmem_limit_bytes=vmem),
    )(*[array for _, array in ins.values()], *after)
    return types.SimpleNamespace(**dict(zip(outs, results)))


def attend_weights(weights, parts):
    ins = dict(qkv=(HBM, weights[0]), proj=(HBM, weights[1])) | numbered("a_part", HBM, parts)
    width_c = weights[1].shape[2]
    outs = dict(qkv_w=shape_of(width_c, 3 * width_c), proj_w=shape_of(width_c, width_c))
    return ins, outs, dict(a_sems=pltpu.SemaphoreType.DMA((2, 17)))


def mlp_weights(weights, parts):
    ins = dict(up=(HBM, weights[2]), down=(HBM, weights[3])) | numbered("m_part", HBM, parts)
    width_c, inner = weights[1].shape[2], weights[2].shape[2]
    outs = dict(up_w=shape_of(width_c, inner), down_w=shape_of(inner, width_c))
    return ins, outs, dict(m_sems=pltpu.SemaphoreType.DMA((2, 17)))


def whole(kept, *names):
    return {name: (VMEM, getattr(kept, name)) for name in names}


def tie(array, after):
    return pl.pallas_call(
        lambda *refs: None,
        name="tie",
        out_shape=jax.ShapeDtypeStruct(array.shape, array.dtype),
        in_specs=[ANY] * (1 + len(after)),
        out_specs=ANY,
        input_output_aliases={0: 0},
        compiler_params=pltpu.CompilerParams(vmem_limit_bytes=1024 * 1024),
    )(array, *after)


def grid_buffer(width, width_c):
    return pltpu.VMEM((WIN, -(-width // 8) * 8, width_c), F32)


def extra_rows(heads):
    return heads + -heads % 16


def pack(kernel, rows, weights, small=(), after=(), vmem=VMEM_LIMIT):
    wide = 4 * weights["proj"].shape[2] if "proj" in weights else weights["up"].shape[2]
    ins = {name: (HBM, w) for name, w in weights.items()}
    scratch = dict(sems=pltpu.SemaphoreType.DMA((7,)))
    if small:
        gains, tables = small
        extra = extra_rows(2 * tables.shape[1])
        rows += extra
        ins |= dict(gains=(VMEM, gains), tables=(VMEM, tables))
        scratch |= dict(small=pltpu.VMEM((extra, wide), F32))
    outs = dict(out=shape_of(rows, wide))
    return call(kernel, "pack", ins, outs, scratch, after, vmem=vmem).out


def table_sums(grads, index, width_c, after=()):
    heads = grads[0].shape[0]
    rows = heads + -heads % 16
    ins = numbered("grad", VMEM, grads) | dict(index=(VMEM, index))
    scratch = dict(wide=pltpu.VMEM((rows, width_c), F32))
    outs = dict(out=shape_of(rows, width_c))
    return call(table_sums_kernel, "table_sums", ins, outs, scratch, after).out


def params(own, other, rel, heads):
    width_c = own.shape[1] // 4
    ins = dict(own=(VMEM, own), other=(VMEM, other), rel=(VMEM, rel))
    outs = dict(
        index=shape_of(SLOT, PAIR, dtype=jnp.int32),
        gains=shape_of(2, 2, width_c, dtype=F32),
        bias=shape_of(2, heads, SLOT, PAIR, dtype=F32),
    )
    scratch = dict(
        table=pltpu.VMEM((2 * heads, TABLE), F32),
        extra=pltpu.VMEM((extra_rows(heads), own.shape[1]), F32),
    )
    return call(params_kernel, "params", ins, outs, scratch)


def grid_ins(grid, edges=()):
    ins = dict(own=(VMEM, grid))
    if edges:
        ins |= {n: (VMEM, e) for n, e in zip(("rows_in", "cols_in", "corner_in"), edges)}
    return ins


def edge_outs(width, width_c):
    return dict(
        rows=shape_of(2, SHIFT, width, width_c),
        cols=shape_of(2, WIN, SHIFT, width_c),
        corner=shape_of(2, SHIFT, SHIFT, width_c),
    )


def attend_forward(layer, mode, grid, edges, gains, bias, region, weights, parts, after=()):
    width, width_c = grid.shape[1:]
    tokens = width // WIN * SLOT
    heads = width_c // HEAD
    more, made, scratch = attend_weights(weights, parts)
    ins = dict(gains=(VMEM, gains), bias=(VMEM, bias))
    ins |= grid_ins(grid, edges) | more
    if mode != "plain":
        more, also, sems = mlp_weights(weights, ())
        ins |= dict(region=(VMEM, region)) | more
        made |= also
        scratch |= sems
        scratch |= dict(
            labels=pltpu.VMEM((SIDE, 128), F32),
            same=pltpu.VMEM((SLOT, tokens), F32),
        )
    outs = dict(
        x=shape_of(tokens, width_c),
        middle=shape_of(tokens, width_c, dtype=F32),
        query=shape_of(tokens, width_c),
        keys_t=shape_of(width_c, tokens),
        values=shape_of(tokens, width_c),
        mixed_t=shape_of(width_c, tokens),
        probs=shape_of(heads, SLOT, tokens, dtype=F32),
    )
    outs |= made
    scratch |= dict(
        flat=pltpu.VMEM((tokens, width_c), F32),
        values_t=pltpu.VMEM((width_c, tokens), BF16),
        query_t=pltpu.VMEM((width_c, tokens), BF16),
        keys=pltpu.VMEM((tokens, width_c), BF16),
    )
    kernel = functools.partial(attend_forward_kernel, layer, mode)
    return call(kernel, "attend_forward", ins, outs, scratch, after, 4)


def mlp_forward(layer, middle, gains, weights, parts, top, after=()):
    tokens, width_c = middle.shape
    width = top.shape[1]
    more, made, scratch = mlp_weights(weights, parts)
    ins = dict(middle=(VMEM, middle), gains=(VMEM, gains)) | more
    ins |= dict(top=(VMEM, top))
    outs = dict(grid=shape_of(WIN, width, width_c)) | edge_outs(width, width_c) | made
    scratch |= dict(
        flat=pltpu.VMEM((tokens, width_c), F32),
        buffer=grid_buffer(width, width_c),
    )
    return call(functools.partial(mlp_forward_kernel, layer), "mlp_forward", ins, outs, scratch, after, 4)


def backward(layer, kept, mlp, grid, edges, gains, ready=None, after=()):
    tokens, width_c = kept.middle.shape
    width = grid.shape[1]
    heads = width_c // HEAD
    second = layer == 1
    ins = dict(gains=(VMEM, gains)) | grid_ins(grid, edges)
    if second:
        ins["own_two"] = ins.pop("own")
    ins |= whole(kept, "middle", "x", "query", "keys_t", "values", "probs", "qkv_w", "proj_w")
    ins |= whole(mlp, "up_w", "down_w")
    pieces = [shape_of(2, 2, kinds, 4, width_c // 8, width_c) for kinds in (1, 2, 3)]
    if second:
        outs = dict(keep=pieces[1], send=pieces[1])
    else:
        outs = dict(keep=pieces[2]) | {"send" + str(i): pieces[0] for i in range(3)}
    outs |= dict(
        grad_m=shape_of(tokens, width_c, dtype=F32),
        grad_t=shape_of(3 * width_c, tokens),
        grad_k=shape_of(tokens, width_c),
        grad_v=shape_of(tokens, width_c),
        bias_grad=shape_of(heads, SLOT, PAIR, dtype=F32),
    )
    scratch = dict(
        out_t=pltpu.VMEM((width_c, tokens), BF16),
        flat=pltpu.VMEM((tokens, width_c), F32),
    )
    if second:
        outs |= dict(out=shape_of(WIN, width, width_c), grid=shape_of(WIN, width, width_c))
        outs |= edge_outs(width, width_c)
        scratch |= dict(buffer=grid_buffer(width, width_c))
    else:
        ins |= dict(mixed_t=(VMEM, kept.mixed_t))
        ins |= {name: (VMEM, value) for name, value in vars(ready).items()}
        scratch |= sides(width_c, tokens)

    def kernel(r):
        mlp_backward_kernel(layer, "in" if second else "out", layer, r)
        attend_backward_kernel(layer, "si" if second else "sw", 2, r)

    return call(kernel, "backward", ins, outs, scratch, after, 15)


def prepare(layer, kept, mlp, gains, after=()):
    tokens, width_c = kept.middle.shape
    inner = mlp.up_w.shape[1]
    ins = dict(middle=(VMEM, kept.middle), gains=(VMEM, gains)) | whole(mlp, "up_w")
    outs = dict(
        hidden_t=shape_of(width_c, tokens),
        activated_t=shape_of(inner, tokens),
        slope=shape_of(tokens, inner),
    )
    kernel = functools.partial(prepare_kernel, layer)
    return call(kernel, "prepare", ins, outs, {}, after, 3)


def sides(width_c, tokens):
    return dict(
        left=pltpu.VMEM((2, width_c, tokens), BF16),
        right=pltpu.VMEM((4, tokens, width_c), BF16),
    )


def attend_weight_grads(layer, kept, back, gains, after=()):
    tokens, width_c = back.grad_m.shape
    ins = dict(gains=(VMEM, gains), grad_m=(VMEM, back.grad_m))
    ins |= dict(x=(VMEM, kept.x), mixed_t=(VMEM, kept.mixed_t), grad_t=(VMEM, back.grad_t))
    ins |= dict(grad_k=(VMEM, back.grad_k), grad_v=(VMEM, back.grad_v))
    pieces = shape_of(2, 2, 1, 4, width_c // 8, width_c)
    kernel = functools.partial(attend_backward_kernel, layer, "w", 0)
    outs = dict(keep=pieces, send=pieces)
    return call(kernel, "attend_weight_grads", ins, outs, sides(width_c, tokens), after, 2)


def input_grad(layer, kept, back, gains, own_two, edges, after=()):
    tokens, width_c = back.grad_m.shape
    width = own_two.shape[1]
    ins = dict(gains=(VMEM, gains), grad_m=(VMEM, back.grad_m))
    ins |= dict(grad_t=(VMEM, back.grad_t)) | whole(kept, "x", "qkv_w")
    ins |= grid_ins(own_two, edges)
    ins["own_two"] = ins.pop("own")
    outs = dict(grid=shape_of(WIN, width, width_c), mixed=shape_of(WIN, width, width_c))
    scratch = dict(
        flat=pltpu.VMEM((tokens, width_c), F32),
        buffer=grid_buffer(width, width_c),
    )

    def kernel(r):
        roll_out_kernel(r)
        attend_backward_kernel(layer, "i", 0, r)

    return call(kernel, "input_grad", ins, outs, scratch, after, 3)


def collect(one, two, total, weights, gains, tables):
    names = ("qkv", "proj", "up", "down", "gains_grad", "tables_grad")
    grads = [shape_of(*w.shape, dtype=F32) for w in (*weights, gains, tables)]
    ins = numbered("one", VMEM, one) | numbered("two", VMEM, two)
    ins |= dict(w_qkv=(HBM, weights[0]), w_up=(HBM, weights[2]), gains=(VMEM, gains))
    ins |= dict(total=(VMEM, total))
    scratch = dict(
        attend_f=pltpu.VMEM(grads[2].shape, F32),
        up_f=pltpu.VMEM(grads[2].shape, F32),
        down_f=pltpu.VMEM(grads[3].shape, F32),
        qkv_w=pltpu.VMEM(weights[0].shape, BF16),
        up_w=pltpu.VMEM(weights[2].shape, BF16),
        load_sems=pltpu.SemaphoreType.DMA((2,)),
        out_sems=pltpu.SemaphoreType.DMA((8,)),
        wide=pltpu.VMEM((256, 128), F32),
    )
    outs = dict(zip(names, grads))
    spaces = [HBM] * 4 + [VMEM] * 2
    return call(collect_kernel, "collect", ins, outs, scratch, spaces=spaces)


def per_device(
    tokens, norm_gains, w_qkv, w_proj, w_up, w_down, tables, region_ids, rel_index, cotangent
):
    width, width_c = tokens.shape[1:]
    weights = (w_qkv, w_proj, w_up, w_down)

    heads = 2 * tables.shape[1]

    rows = w_qkv.shape[1] // 2
    attend_w, mlp_w = dict(qkv=w_qkv, proj=w_proj), dict(up=w_up, down=w_down)
    mlp_piece = pack(pack_mlp_kernel, rows, mlp_w, (norm_gains, tables), (), PACK_VMEM_LIMIT)
    attend_piece = pack(
        pack_attend_kernel, rows, attend_w, after=(mlp_piece,), vmem=PACK_VMEM_LIMIT
    )
    mlp_first = exchange(mlp_piece, 0, 1)
    mlp_second = exchange(mlp_first, 2, 0)
    attend_one = share_halves(attend_piece, after=(mlp_first,))
    settings = params(mlp_piece, mlp_first, rel_index, heads)
    gains, bias, index = settings.gains, settings.bias, settings.index
    both_piece = pack(pack_both_kernel, 3 * rows, attend_w | mlp_w, after=(attend_piece,))

    one = attend_forward(
        0, "plain", tokens, (), gains, bias, None, weights, attend_one, after=(both_piece,)
    )
    mlp_one = share(mlp_first, mlp_second, after=(one.middle,))
    done = mlp_forward(0, one.middle, gains, weights, mlp_one, cotangent)
    edges = halo(done.rows, done.cols, done.corner, 1)
    parts_two = share_halves(both_piece, after=edges)
    two = attend_forward(
        1, "in", done.grid, edges, gains, bias, region_ids, weights, parts_two
    )
    back2 = backward(1, two, two, cotangent, edges, gains)
    got_m2 = exchange(back2.send, 1, 0)
    edges = halo(back2.rows, back2.cols, back2.corner, -1)
    att2 = attend_weight_grads(1, two, back2, gains)
    ready = prepare(0, one, done, gains, after=(att2.send,))
    side_two = start_side(
        (back2.keep, att2.keep),
        (got_m2, exchange(att2.send, 1, 0)),
        after=(*edges, ready.slope),
    )
    back1 = backward(
        0, one, done, back2.grid, edges, gains, ready, after=(side_two[0],)
    )
    rows = width_c // 8
    gots = [exchange(send, 1, 0) for send in (back1.send0, back1.send1, back1.send2)]
    small = table_sums((back1.bias_grad, back2.bias_grad), index, width_c)
    small = add_pair(small, exchange(small, 1, 0))
    side_one = start_sides((back1.keep,), gots, after=(small,))
    small = (small, exchange(small, 0, 1))
    face_two = start_face(side_two, after=side_one[:1])
    last = input_grad(
        0, one, back1, gains, back2.out, edges, after=side_one[:1]
    )
    total_two, _ = finish_sum(face_two, 3 * rows, halve_kernel)
    face_one = start_faces(side_one, small=small, after=(last.mixed,))
    pair_two = gather_pair(total_two, 3 * rows)
    total_one, _ = finish_sum(face_one, face_one[0].shape[0], halve_faces_kernel)
    pair_one = gather_pair(total_one, 3 * rows)
    sums = collect(gather(pair_one), gather(pair_two), total_one, weights, norm_gains, tables)
    return (
        last.mixed,
        last.grid,
        sums.gains_grad,
        sums.qkv,
        sums.proj,
        sums.up,
        sums.down,
        sums.tables_grad,
    )


def solution(mesh):
    return jax.shard_map(
        per_device,
        mesh=mesh,
        in_specs=(
            P("seq", "fsdp", None),
            P(None, None, "fsdp"),
            P(None, "fsdp", None),
            P(None, "fsdp", None),
            P(None, "fsdp", None),
            P(None, "fsdp", None),
            P(None, "fsdp", None),
            P("seq", "fsdp"),
            P(),
            P("seq", "fsdp", None),
        ),
        out_specs=(
            P("seq", "fsdp", None),
            P("seq", "fsdp", None),
            P(None, None, "fsdp"),
            P(None, "fsdp", None),
            P(None, "fsdp", None),
            P(None, "fsdp", None),
            P(None, "fsdp", None),
            P(None, "fsdp", None),
        ),
        check_vma=False,
    )
```
